128 devices in a mesh: lat: 4 (over y_hi, core), lon: 32 (over x, z, y_lo).
Axes of the slice: x: 4, y: 4 (y_hi: 2, y_lo: 2; y = y_hi * 2 + y_lo), z: 4, core: 2. Of those that a mesh axis runs over, the one named last changes fastest.
Arguments:
- tokens: bfloat16 [256, 2048, 256], P('lat', 'lon'), may hold values from -6 to 6
- gain_conv: float32 [256], replicated, may hold values from 0.25 to 1.75
- w_expand: bfloat16 [256, 1024], replicated, may hold values from -0.375 to 0.375
- dw_kernel: float32 [3, 3, 1024], replicated, may hold values from -2 to 2
- w_project: bfloat16 [1024, 256], replicated, may hold values from -0.1875 to 0.1875
- gain_block: float32 [256], replicated, may hold values from 0.25 to 1.75
- qkv_block: bfloat16 [256, 768], replicated, may hold values from -0.375 to 0.375
- bias_block: float32 [8, 64, 64], replicated, may hold values from -8 to 310
- out_block: bfloat16 [256, 256], replicated, may hold values from -0.375 to 0.375
- gain_grid: float32 [256], replicated, may hold values from 0.25 to 1.75
- qkv_grid: bfloat16 [256, 768], replicated, may hold values from -0.375 to 0.375
- bias_grid: float32 [8, 64, 64], replicated, may hold values from -8 to 310
- out_grid: bfloat16 [256, 256], replicated, may hold values from -0.375 to 0.375
Outputs:
- layer_out: bfloat16 [256, 2048, 256], P('lat', 'lon')
The draws below stay inside these ranges and needn't reach their ends.
All inputs are finite; a program needn't handle non-finite values.
Results may differ from the reference program's by a relative error of at most 0.011.
Values may be sent and summed in bfloat16 or wider, within the bound.
A program may use at most 128 MiB of HBM per device.

```python
import jax
import jax.numpy as jnp
from jax import lax

D = 256
HID = 1024
HEADS = 8
LAT = 256
LON = 2048


def draw_bias_block(key, part):
    key = jax.random.fold_in(key, 11)
    first_key = jax.random.fold_in(key, 0)
    return jnp.clip(jax.random.normal(first_key, (HEADS, 64, 64), jnp.float32), -8.0, 8.0)


def draw_bias_grid(key, part):
    key = jax.random.fold_in(key, 23)
    first_key = jax.random.fold_in(key, 0)
    return jnp.clip(jax.random.normal(first_key, (HEADS, 64, 64), jnp.float32), -8.0, 8.0)


def block_levels(key, shape, cuts, least, largest):
    level, own = 1.0, jax.random.fold_in(key, 6)
    for dim, blocks in cuts:
        heights = jnp.exp(jax.random.uniform(jax.random.fold_in(own, dim), (blocks,), jnp.float32, least / len(cuts), largest / len(cuts)))
        level = level * jnp.repeat(heights, shape[dim] // blocks).reshape([-1 if axis == dim else 1 for axis in range(len(shape))])
    return level


def scatter_about(rng, dims, deviation, reach, pieces=(), kind=jnp.bfloat16):
    array = jax.random.normal(rng, dims, jnp.float32) * deviation
    if len(pieces) > 0:
        array = block_levels(rng, dims, pieces, -0.22, 0.18) * array
    return jnp.clip(array, min=-reach, max=reach).astype(kind)


def setup_inputs(seed: int = 0) -> dict:
    key_of = jax.random.split(jax.random.key(seed), 14)
    tokens = scatter_about(key_of[0], (LAT, LON, D), 1.0, 6.0, ((0, 4), (1, 32)))
    gain_conv = jnp.clip(1.0 + 0.15 * jax.random.normal(key_of[1], (D,), jnp.float32), 0.25, 1.75)
    w_expand = scatter_about(key_of[2], (D, HID), D ** -0.5, 0.375)
    dw_kernel = scatter_about(key_of[3], (3, 3, HID), 9 ** -0.5, 2.0, (), jnp.float32)
    w_project = scatter_about(key_of[4], (HID, D), HID ** -0.5, 0.1875)
    gain_block = jnp.clip(1.0 + 0.15 * jax.random.normal(key_of[5], (D,), jnp.float32), 0.25, 1.75)
    qkv_block = scatter_about(key_of[6], (D, 3 * D), D ** -0.5, 0.375)
    bias_block = draw_bias_block(jax.random.fold_in(key_of[13], 71), 0)
    out_block = scatter_about(key_of[8], (D, D), D ** -0.5, 0.375)
    gain_grid = jnp.clip(1.0 + 0.15 * jax.random.normal(key_of[9], (D,), jnp.float32), 0.25, 1.75)
    qkv_grid = scatter_about(key_of[10], (D, 3 * D), D ** -0.5, 0.375)
    bias_grid = draw_bias_grid(jax.random.fold_in(key_of[13], 71), 0)
    out_grid = scatter_about(key_of[12], (D, D), D ** -0.5, 0.375)
    return dict(tokens=tokens, gain_conv=gain_conv, w_expand=w_expand, dw_kernel=dw_kernel, w_project=w_project, gain_block=gain_block, qkv_block=qkv_block, bias_block=bias_block, out_block=out_block, gain_grid=gain_grid, qkv_grid=qkv_grid, bias_grid=bias_grid, out_grid=out_grid)


def layer_norm(x, gain):
    xf = x.astype(jnp.float32)
    mean = lax.optimization_barrier(jnp.mean(xf, axis=-1, keepdims=True))
    var = lax.optimization_barrier(jnp.mean((xf - mean) ** 2, axis=-1, keepdims=True))
    return (xf - mean) / jnp.sqrt(var + 1e-05) * gain

def attend(x, gain, w_qkv, bias, w_out):
    groups = x.shape[0]
    width = x.shape[2]
    head_size = width // HEADS
    normed = layer_norm(x, gain).astype(jnp.bfloat16)
    qkv = jnp.dot(normed.reshape(-1, width), w_qkv, preferred_element_type=jnp.float32).astype(jnp.bfloat16)
    qkv = qkv.reshape(groups, 64, 3, HEADS, head_size)
    query = qkv[:, :, 0].astype(jnp.float32)
    keys = qkv[:, :, 1].astype(jnp.float32)
    values = qkv[:, :, 2].astype(jnp.float32)
    scores = jnp.einsum('gqhe,gkhe->ghqk', query, keys) * head_size ** (-0.5) + bias[None]
    scores = scores - lax.optimization_barrier(jnp.max(scores, axis=-1, keepdims=True))
    expo = jnp.exp(scores)
    weights = (expo / lax.optimization_barrier(jnp.sum(expo, axis=-1, keepdims=True))).astype(jnp.bfloat16)
    mixed = jnp.einsum('ghqk,gkhe->gqhe', weights.astype(jnp.float32), values).astype(jnp.bfloat16)
    result = jnp.dot(mixed.reshape(-1, width), w_out, preferred_element_type=jnp.float32)
    return result.reshape(groups, 64, width)

def reference(tokens, gain_conv, w_expand, dw_kernel, w_project, gain_block, qkv_block, bias_block, out_block, gain_grid, qkv_grid, bias_grid, out_grid):
    width = tokens.shape[2]
    padded = jnp.pad(tokens, ((1, 1), (0, 0), (0, 0)))

    def conv_band(start):
        band = lax.dynamic_slice_in_dim(padded, start, 10, 0)
        normed = layer_norm(band, gain_conv).astype(jnp.bfloat16)
        expanded = jax.nn.gelu(jnp.dot(normed, w_expand, preferred_element_type=jnp.float32)).astype(jnp.bfloat16)
        rows = start - 1 + jnp.arange(10, dtype=jnp.int32)
        valid = jnp.logical_and(rows >= 0, rows < LAT).astype(jnp.bfloat16)
        expanded = expanded * valid[:, None, None]
        wrapped = jnp.concatenate([expanded[:, -1:], expanded, expanded[:, :1]], axis=1)
        total = jnp.zeros((8, LON, HID), jnp.float32)
        for row_step in range(3):
            for col_step in range(3):
                total = total + wrapped[row_step:row_step + 8, col_step:col_step + LON].astype(jnp.float32) * dw_kernel[row_step, col_step]
        conv = jax.nn.gelu(total).astype(jnp.bfloat16)
        proj = jnp.dot(conv, w_project, preferred_element_type=jnp.float32)
        return (band[1:9].astype(jnp.float32) + proj).astype(jnp.bfloat16)
    starts = jnp.arange(LAT // 8, dtype=jnp.int32) * 8
    mixed = lax.map(conv_band, starts).reshape(LAT, LON, width)

    def block_band(band):
        groups = band.reshape(8, LON // 8, 8, width).transpose(1, 0, 2, 3).reshape(LON // 8, 64, width)
        out = attend(groups, gain_block, qkv_block, bias_block, out_block)
        new = (groups.astype(jnp.float32) + out).astype(jnp.bfloat16)
        return new.reshape(LON // 8, 8, 8, width).transpose(1, 0, 2, 3).reshape(8, LON, width)
    blocked = lax.map(block_band, mixed.reshape(LAT // 8, 8, LON, width)).reshape(LAT, LON, width)
    grids = blocked.reshape(8, LAT // 8, 8, LON // 8, width).transpose(1, 3, 0, 2, 4)

    def grid_row(row):
        groups = row.reshape(LON // 8, 64, width)
        out = attend(groups, gain_grid, qkv_grid, bias_grid, out_grid)
        new = (groups.astype(jnp.float32) + out).astype(jnp.bfloat16)
        return new.reshape(LON // 8, 8, 8, width)
    done = lax.map(grid_row, grids)
    return done.transpose(2, 0, 3, 1, 4).reshape(LAT, LON, width)
```

```python
import functools

import jax
import jax.numpy as jnp
import numpy as np
from jax import lax
from jax.experimental import pallas as pl
from jax.experimental.pallas import tpu as pltpu
from jax.sharding import PartitionSpec as P

MESH = pl.DeviceIdType.MESH
BF16 = jnp.bfloat16
F32 = jnp.float32
ROWS, COLS, D, HID, HEADS = 64, 64, 256, 1024, 8
PHASES = 4
LOG2E = 1.4426950408889634


def dot(a, b):
    return jnp.dot(a, b, preferred_element_type=F32)


def dot_nt(a, b):
    return lax.dot_general(a, b, (((1,), (1,)), ((), ())), preferred_element_type=F32)


def gelu(x):
    half = x * BF16(0.5)
    inner = x * (BF16(0.7978845608) + BF16(0.035677408) * (x * x))
    return half + half * jnp.tanh(inner)


def norm(x, gain, average):
    xf = x.astype(F32)
    d = xf - dot(x, average)
    var = dot((d * d).astype(BF16), average)
    return (d * lax.rsqrt(var + 1e-05) * gain).astype(BF16)


def expand(x, gain, average, w_expand, store):
    n = norm(x, gain, average)
    for c in range(0, HID, 256):
        store(c, gelu(dot(n, w_expand[:, c : c + 256]).astype(BF16)))


def attend(x_ref, gain, average, w_qkv, bias, w_out, masks, select, ones_bd, qkv, mixed):
    n = norm(x_ref[...], gain[...], average[...])
    scale = LOG2E / 32**0.5
    qkv[:, 0:256] = (dot(n, w_qkv[:, 0:256]) * scale).astype(BF16)
    qkv[:, 256:512] = dot(n, w_qkv[:, 256:512]).astype(BF16)
    qkv[:, 512:768] = dot(n, w_qkv[:, 512:768]).astype(BF16)

    def blocks(m):
        return jnp.concatenate(
            [m[16 * i : 16 * i + 16] * masks[h] for i in range(4) for h in range(HEADS)], axis=0
        )

    def group(g, carry):
        rows = pl.ds(pl.multiple_of(g * 64, 64), 64)
        s = dot_nt(qkv[rows, 0:256], blocks(qkv[rows, 256:512])) + bias[...]
        top = jnp.maximum(
            jnp.maximum(s[:, 0:128], s[:, 128:256]), jnp.maximum(s[:, 256:384], s[:, 384:512])
        )
        for shift in (8, 4, 2, 1):
            top = jnp.maximum(top, pltpu.roll(top, 128 - shift, 1))
        high = top.astype(BF16)
        low = (top - high.astype(F32)).astype(BF16)
        top = dot(jnp.concatenate([high, low], axis=1), select[...])
        p = jnp.concatenate(
            [jnp.exp2(s[:, 128 * i : 128 * i + 128] - top).astype(BF16) for i in range(4)], axis=1
        )
        value = dot(p, blocks(qkv[rows, 512:768]))
        total = dot(p, ones_bd[...])
        mixed[rows, :] = (value / total).astype(BF16)
        return carry

    lax.fori_loop(0, 8, group, 0, unroll=4)
    return dot(mixed[...], w_out[...])


def kernel(
    tokens,
    edge_left,
    edge_right,
    gain_conv,
    w_expand,
    dw16,
    dw_edge,
    w_project,
    gain_block,
    qkv_block,
    bias_block,
    out_block,
    gain_grid,
    qkv_grid,
    bias_grid,
    out_grid,
    average,
    masks,
    select,
    ones_bd,
    shifts,
    edge_shift,
    perm,
    out,
    e_mid,
    e_edge,
    halo_row,
    halo_col,
    edge_sum,
    conv,
    mixed,
    qkv,
    att,
    blocked,
    received,
    outgoing,
    halo_send,
    halo_recv,
    send_sem,
    recv_sem,
    back_send,
    back_recv,
):
    lat = lax.axis_index("lat")
    lon = lax.axis_index("lon")
    lats = lax.axis_size("lat")
    lons = lax.axis_size("lon")
    kind = lax.rem(lon, 4)
    place = lon // 4
    far = 3 - kind
    mine = lat * 8 + place
    my_row, my_col = mine // 4, lax.rem(mine, 4)
    west = lax.rem(lon + lons - 1, lons)
    east = lax.rem(lon + 1, lons)

    def partner(i):
        return {"lat": i // 8, "lon": lax.rem(i, 8) * 4 + far}

    barrier = pltpu.get_barrier_semaphore()

    def greet(i, carry):
        pl.semaphore_signal(barrier, inc=1, device_id=partner(i), device_id_type=MESH)
        return carry

    lax.fori_loop(0, 32, greet, 0)
    for side in (west, east):
        pl.semaphore_signal(
            barrier, inc=1, device_id={"lat": lat, "lon": side}, device_id_type=MESH
        )

    @pl.when(lat > 0)
    def _():
        for side in (lon, west, east):
            pl.semaphore_signal(
                barrier, inc=1, device_id={"lat": lat - 1, "lon": side}, device_id_type=MESH
            )

    @pl.when(lat < lats - 1)
    def _():
        for side in (lon, west, east):
            pl.semaphore_signal(
                barrier, inc=1, device_id={"lat": lat + 1, "lon": side}, device_id_type=MESH
            )

    inner = jnp.minimum(lat, 1) + jnp.minimum(lats - 1 - lat, 1)
    pl.semaphore_wait(barrier, 34 + 3 * inner)

    def halo(slot, src, dst, to_lat, to_lon):
        return pltpu.make_async_remote_copy(
            src_ref=src,
            dst_ref=dst,
            send_sem=halo_send.at[slot],
            recv_sem=halo_recv.at[slot],
            device_id={"lat": to_lat, "lon": to_lon},
            device_id_type=MESH,
        )

    to_west = halo(0, edge_left, halo_col.at[1, pl.ds(16, 64)], lat, west)
    to_east = halo(1, edge_right, halo_col.at[0, pl.ds(16, 64)], lat, east)
    north = [
        halo(2, tokens.at[0], halo_row.at[1], lat - 1, lon),
        halo(3, edge_left.at[pl.ds(0, 16)], halo_col.at[1, pl.ds(80, 16)], lat - 1, west),
        halo(4, edge_right.at[pl.ds(0, 16)], halo_col.at[0, pl.ds(80, 16)], lat - 1, east),
    ]
    south = [
        halo(5, tokens.at[ROWS - 1], halo_row.at[0], lat + 1, lon),
        halo(6, edge_left.at[pl.ds(48, 16)], halo_col.at[1, pl.ds(0, 16)], lat + 1, west),
        halo(7, edge_right.at[pl.ds(48, 16)], halo_col.at[0, pl.ds(0, 16)], lat + 1, east),
    ]
    to_west.start()
    to_east.start()

    @pl.when(lat > 0)
    def _():
        for c in north:
            c.start()

    @pl.when(lat < lats - 1)
    def _():
        for c in south:
            c.start()

    @pl.when(lat == 0)
    def _():
        halo_row[0] = jnp.zeros((COLS, D), BF16)
        halo_col[0, 0:16] = jnp.zeros((16, D), BF16)
        halo_col[1, 0:16] = jnp.zeros((16, D), BF16)

    @pl.when(lat == lats - 1)
    def _():
        halo_row[1] = jnp.zeros((COLS, D), BF16)
        halo_col[0, 80:96] = jnp.zeros((16, D), BF16)
        halo_col[1, 80:96] = jnp.zeros((16, D), BF16)

    def expand_rows(first, count):
        def store(c, v):
            e_mid[pl.ds(first + 1, count), :, c : c + 256] = v.reshape(count, COLS, 256)

        x = tokens[pl.ds(first, count)].reshape(count * COLS, D)
        expand(x, gain_conv[...], average[...], w_expand, store)

    expand_rows(0, 1)
    expand_rows(31, 2)

    to_west.wait()
    to_east.wait()

    @pl.when(lat > 0)
    def _():
        for c in north:
            c.wait_send()
        for c in south:
            c.wait_recv()

    @pl.when(lat < lats - 1)
    def _():
        for c in south:
            c.wait_send()
        for c in north:
            c.wait_recv()

    def store_rows(c, v):
        e_mid[0, :, c : c + 256] = v[0:64]
        e_mid[65, :, c : c + 256] = v[64:128]

    expand(halo_row[...].reshape(2 * COLS, D), gain_conv[...], average[...], w_expand, store_rows)

    def store_cols(c, v):
        e_edge[:, c : c + 256] = v

    expand(halo_col[...].reshape(192, D), gain_conv[...], average[...], w_expand, store_cols)
    for c in range(0, HID, 256):
        total = jnp.zeros((8, 16, 256), F32)
        for dy in range(3):
            moved = dot(edge_shift[dy], e_edge[:, c : c + 256]).reshape(8, 16, 256)
            total = total + moved * dw_edge[dy, :, c : c + 256][None]
        edge_sum[:, :, c : c + 256] = total.astype(BF16)

    def conv_band(band):
        first = band * 8

        def row(r, carry):
            for c in range(0, HID, 256):
                parts = []
                e = [e_mid[first + r + dy, :, c : c + 256] for dy in range(3)]
                for dx in range(3):
                    acc = None
                    for dy in range(3):
                        w = dw16[3 * dy + dx, :, c : c + 256]
                        w = jnp.concatenate([w] * 4, axis=0)
                        term = e[dy] * w
                        acc = term if acc is None else acc + term
                    parts.append(acc)
                parts.append(edge_sum[band, :, c : c + 256])
                total = dot(shifts[r], jnp.concatenate(parts, axis=0))
                conv[pl.ds(r * 64, 64), c : c + 256] = gelu(total.astype(BF16))
            return carry

        lax.fori_loop(0, 8, row, 0, unroll=2)

    def pieces(x):
        return jnp.concatenate(
            [x[64 * b + 8 * a : 64 * b + 8 * a + 8] for a in range(8) for b in range(8)], axis=0
        )

    def send(phase):
        def one(i, carry):
            pltpu.make_async_remote_copy(
                src_ref=blocked.at[
                    :, phase * 8 + i // 4, pl.ds(pl.multiple_of(lax.rem(i, 4) * 16, 16), 16), :
                ],
                dst_ref=received.at[phase, lat, :, place],
                send_sem=send_sem.at[phase],
                recv_sem=recv_sem.at[phase],
                device_id=partner(i),
                device_id_type=MESH,
            ).start()
            return carry

        lax.fori_loop(0, 32, one, 0)

    def send_back(phase):
        def one(i, carry):
            pltpu.make_async_remote_copy(
                src_ref=outgoing.at[phase, i // 8, :, lax.rem(i, 8)],
                dst_ref=out.at[
                    :, phase * 8 + my_row, pl.ds(pl.multiple_of(my_col * 16, 16), 16), :
                ],
                send_sem=back_send.at[phase],
                recv_sem=back_recv.at[phase],
                device_id=partner(i),
                device_id_type=MESH,
            ).start()
            return carry

        lax.fori_loop(0, 32, one, 0)

    def conv_and_block(phase):
        def half(i, carry):
            band = i * 4 + phase
            first = band * 8

            @pl.when(band < 7)
            def _():
                expand_rows(first + 1, 8)

            @pl.when(band == 7)
            def _():
                expand_rows(first + 1, 7)

            conv_band(band)
            x = tokens[pl.ds(first, 8)].reshape(512, D).astype(F32)
            mixed[...] = pieces(x + dot(conv[0:512], w_project[...])).astype(BF16)
            result = attend(
                mixed, gain_block, average, qkv_block, bias_block, out_block, masks, select,
                ones_bd, qkv, att,
            )
            blocked[i, pl.ds(phase * 8, 8)] = (
                pieces(result + mixed[...].astype(F32)).astype(BF16).reshape(8, 64, D)
            )
            return carry

        lax.fori_loop(0, 2, half, 0)

    def grid(phase):
        for half in range(2):
            for q in range(4):
                x = received[phase, q].reshape(256, D)
                y = dot(perm[128 * half : 128 * half + 128], x).astype(BF16)
                for p in range(8):
                    mixed[64 * p + 16 * q : 64 * p + 16 * q + 16] = y[16 * p : 16 * p + 16]
            result = attend(
                mixed, gain_grid, average, qkv_grid, bias_grid, out_grid, masks, select, ones_bd,
                qkv, att,
            )
            done = (result + mixed[...].astype(F32)).astype(BF16)
            for q in range(4):
                conv[256 * q + 128 * half : 256 * q + 128 * half + 128, 0:256] = jnp.concatenate(
                    [done[64 * p + 16 * q : 64 * p + 16 * q + 16] for p in range(8)], axis=0
                )
        for q in range(4):
            y = dot(perm[...], conv[256 * q : 256 * q + 256, 0:256]).astype(BF16)
            outgoing[phase, q] = y.reshape(2, 8, 16, D)

    def wait_all(ref, sem):
        pltpu.make_async_copy(ref, ref, sem).wait()

    def step(phase, carry):
        @pl.when(phase < PHASES)
        def _():
            conv_and_block(phase)
            send(phase)

        @pl.when(phase > 0)
        def _():
            wait_all(received.at[phase - 1], recv_sem.at[phase - 1])
            grid(phase - 1)
            send_back(phase - 1)

        return carry

    lax.fori_loop(0, PHASES + 1, step, 0)

    def finish(phase, carry):
        wait_all(received.at[phase], send_sem.at[phase])
        wait_all(received.at[phase], back_send.at[phase])
        wait_all(received.at[phase], back_recv.at[phase])
        return carry

    lax.fori_loop(0, PHASES, finish, 0)


def constants():
    average = np.full((D, D), 1.0 / D, np.float32)
    lane_head = np.arange(D) // 32
    masks = np.zeros((HEADS, 16, D), np.float32)
    for h in range(HEADS):
        masks[h, :, lane_head == h] = 1.0
    select = np.zeros((256, 128), np.float32)
    for c in range(128):
        select[c // 16 * 16, c] = 1.0
        select[128 + c // 16 * 16, c] = 1.0
    ones_bd = np.zeros((512, D), np.float32)
    row_head = np.arange(512) // 16 % 8
    ones_bd[row_head[:, None] == lane_head[None, :]] = 1.0
    shifts = np.zeros((8, 64, 208), np.float32)
    for r in range(8):
        for c in range(64):
            if c > 0:
                shifts[r, c, c - 1] = 1.0
            shifts[r, c, 64 + c] = 1.0
            if c < 63:
                shifts[r, c, 128 + c + 1] = 1.0
        shifts[r, 0, 192 + r] = 1.0
        shifts[r, 63, 200 + r] = 1.0
    edge_shift = np.zeros((3, 128, 192), np.float32)
    for dy in range(3):
        for band in range(8):
            for side in range(2):
                for r in range(8):
                    edge_shift[dy, band * 16 + side * 8 + r, side * 96 + 16 + band * 8 + r + dy - 1] = 1
    perm = np.zeros((256, 256), np.float32)
    for p in range(16):
        for s in range(16):
            perm[p * 16 + s, s * 16 + p] = 1.0
    return [
        jnp.asarray(a, BF16)
        for a in (average, masks, select, ones_bd, shifts, edge_shift, perm)
    ]


def spread_bias(bias):
    return (
        (bias * LOG2E).reshape(HEADS, 64, 4, 16).transpose(1, 2, 0, 3).reshape(64, 512)
    )


def shards(
    tokens,
    gain_conv,
    w_expand,
    dw_kernel,
    w_project,
    gain_block,
    qkv_block,
    bias_block,
    out_block,
    gain_grid,
    qkv_grid,
    bias_grid,
    out_grid,
):
    dw16 = jnp.broadcast_to(dw_kernel.astype(BF16).reshape(9, 1, HID), (9, 16, HID))
    dw_edge = jnp.repeat(dw_kernel[:, 0::2, :], 8, axis=1)
    operands = [
        tokens,
        tokens[:, 0],
        tokens[:, COLS - 1],
        gain_conv.reshape(1, D),
        w_expand,
        dw16,
        dw_edge,
        w_project,
        gain_block.reshape(1, D),
        qkv_block,
        spread_bias(bias_block),
        out_block,
        gain_grid.reshape(1, D),
        qkv_grid,
        spread_bias(bias_grid),
        out_grid,
        *constants(),
    ]
    result = pl.pallas_call(
        kernel,
        out_shape=jax.ShapeDtypeStruct((2, 32, COLS, D), BF16),
        in_specs=[pl.BlockSpec(memory_space=pltpu.VMEM)] * len(operands),
        out_specs=pl.BlockSpec(memory_space=pltpu.VMEM),
        scratch_shapes=[
            pltpu.VMEM((66, COLS, HID), BF16),
            pltpu.VMEM((192, HID), BF16),
            pltpu.VMEM((2, COLS, D), BF16),
            pltpu.VMEM((2, 96, D), BF16),
            pltpu.VMEM((8, 16, HID), BF16),
            pltpu.VMEM((1024, HID), BF16),
            pltpu.VMEM((512, D), BF16),
            pltpu.VMEM((512, 3 * D), BF16),
            pltpu.VMEM((512, D), BF16),
            pltpu.VMEM((2, 32, COLS, D), BF16),
            pltpu.VMEM((PHASES, 4, 2, 8, 16, D), BF16),
            pltpu.VMEM((PHASES, 4, 2, 8, 16, D), BF16),
            pltpu.SemaphoreType.DMA((8,)),
            pltpu.SemaphoreType.DMA((8,)),
            pltpu.SemaphoreType.DMA((PHASES,)),
            pltpu.SemaphoreType.DMA((PHASES,)),
            pltpu.SemaphoreType.DMA((PHASES,)),
            pltpu.SemaphoreType.DMA((PHASES,)),
        ],
        compiler_params=pltpu.CompilerParams(
            collective_id=0, has_side_effects=True, vmem_limit_bytes=60 * 1024 * 1024
        ),
    )(*operands)
    return result.reshape(ROWS, COLS, D)


def solution(mesh):
    placed = (P("lat", "lon", None), P(), P(), P(), P(), P(), P(), P(), P(), P(), P(), P(), P())
    return jax.shard_map(
        shards, mesh=mesh, in_specs=placed, out_specs=P("lat", "lon", None), check_vma=False
    )
```

```python
import functools

import jax
import jax.numpy as jnp
import numpy as np
from jax import lax
from jax.experimental import pallas as pl
from jax.experimental.pallas import tpu as pltpu
from jax.sharding import PartitionSpec as P

MESH = pl.DeviceIdType.MESH
BF16 = jnp.bfloat16
F32 = jnp.float32
ROWS, COLS, D, HID, HEADS = 64, 64, 256, 1024, 8
PHASES = 4
BATCH = 8
LOG2E = 1.4426950408889634


def dot(a, b):
    return jnp.dot(a, b, preferred_element_type=F32)


def dot_nt(a, b):
    return lax.dot_general(a, b, (((1,), (1,)), ((), ())), preferred_element_type=F32)


def exp2(x):
    return jnp.exp2(x)


def gelu(x):
    half = x * BF16(0.5)
    inner = x * (BF16(0.7978845608) + BF16(0.035677408) * (x * x))
    return half + half * jnp.tanh(inner)


def norm(x, gain, average):
    xf = x.astype(F32)
    d = xf - dot(x, average)
    var = dot((d * d).astype(BF16), average)
    return (d * lax.rsqrt(var + 1e-05) * gain).astype(BF16)


def expand(x, gain, average, w_expand, store):
    n = norm(x, gain, average)
    for c in range(0, HID, 256):
        store(c, gelu(dot(n, w_expand[:, c : c + 256]).astype(BF16)))


def blocks(m, masks):
    return jnp.concatenate(
        [m[16 * i : 16 * i + 16] * masks[h] for i in range(4) for h in range(HEADS)], axis=0
    )


def head_top(top, select):
    for shift in (8, 4, 2, 1):
        top = jnp.maximum(top, pltpu.roll(top, 128 - shift, 1))
    high = top.astype(BF16)
    low = (top - high.astype(F32)).astype(BF16)
    return dot(jnp.concatenate([high, low], axis=1), select[...])


def attend(x_ref, gain, average, w_qkv, bias, w_out, masks, select, ones_bd, qkv, mixed):
    n = norm(x_ref[...], gain[...], average[...])
    scale = LOG2E / 32**0.5
    qkv[:, 0:256] = (dot(n, w_qkv[:, 0:256]) * scale).astype(BF16)
    qkv[:, 256:512] = dot(n, w_qkv[:, 256:512]).astype(BF16)
    qkv[:, 512:768] = dot(n, w_qkv[:, 512:768]).astype(BF16)

    def batch(b, carry):
        rows = [pl.ds(pl.multiple_of((b * BATCH + i) * 64, 64), 64) for i in range(BATCH)]
        scores = [dot_nt(qkv[r, 0:256], blocks(qkv[r, 256:512], masks)) + bias[...] for r in rows]
        tops = [
            jnp.maximum(
                jnp.maximum(s[:, 0:128], s[:, 128:256]), jnp.maximum(s[:, 256:384], s[:, 384:512])
            )
            for s in scores
        ]
        top = head_top(jnp.concatenate(tops, axis=0), select)
        weights = [
            jnp.concatenate(
                [
                    exp2(s[:, 128 * i : 128 * i + 128] - top[64 * k : 64 * k + 64]).astype(BF16)
                    for i in range(4)
                ],
                axis=1,
            )
            for k, s in enumerate(scores)
        ]
        values = [dot(p, blocks(qkv[r, 512:768], masks)) for p, r in zip(weights, rows)]
        total = dot(jnp.concatenate(weights, axis=0), ones_bd[...])
        whole = pl.ds(pl.multiple_of(b * (BATCH * 64), 64), BATCH * 64)
        mixed[whole, :] = (jnp.concatenate(values, axis=0) / total).astype(BF16)
        return carry

    lax.fori_loop(0, 8 // BATCH, batch, 0)
    return dot(mixed[...], w_out[...])


def kernel(
    tokens,
    edge_left,
    edge_right,
    gain_conv,
    w_expand,
    dw16,
    dw_edge,
    w_project,
    gain_block,
    qkv_block,
    bias_block,
    out_block,
    gain_grid,
    qkv_grid,
    bias_grid,
    out_grid,
    average,
    masks,
    select,
    ones_bd,
    shifts,
    edge_shift,
    perm,
    out,
    e_mid,
    e_edge,
    halo_row,
    halo_col,
    edge_sum,
    conv,
    mixed,
    qkv,
    att,
    blocked,
    received,
    outgoing,
    halo_send,
    halo_recv,
    send_sem,
    recv_sem,
    back_send,
    back_recv,
):
    lat = lax.axis_index("lat")
    lon = lax.axis_index("lon")
    lats = lax.axis_size("lat")
    lons = lax.axis_size("lon")
    kind = lax.rem(lon, 4)
    place = lon // 4
    far = 3 - kind
    mine = lat * 8 + place
    my_row, my_col = mine // 4, lax.rem(mine, 4)
    west = lax.rem(lon + lons - 1, lons)
    east = lax.rem(lon + 1, lons)

    def partner(i):
        return {"lat": i // 8, "lon": lax.rem(i, 8) * 4 + far}

    barrier = pltpu.get_barrier_semaphore()

    def greet(i, carry):
        pl.semaphore_signal(barrier, inc=1, device_id=partner(i), device_id_type=MESH)
        return carry

    lax.fori_loop(0, 32, greet, 0)
    for side in (west, east):
        pl.semaphore_signal(
            barrier, inc=1, device_id={"lat": lat, "lon": side}, device_id_type=MESH
        )

    @pl.when(lat > 0)
    def _():
        for side in (lon, west, east):
            pl.semaphore_signal(
                barrier, inc=1, device_id={"lat": lat - 1, "lon": side}, device_id_type=MESH
            )

    @pl.when(lat < lats - 1)
    def _():
        for side in (lon, west, east):
            pl.semaphore_signal(
                barrier, inc=1, device_id={"lat": lat + 1, "lon": side}, device_id_type=MESH
            )

    inner = jnp.minimum(lat, 1) + jnp.minimum(lats - 1 - lat, 1)
    pl.semaphore_wait(barrier, 34 + 3 * inner)

    def halo(slot, src, dst, to_lat, to_lon):
        return pltpu.make_async_remote_copy(
            src_ref=src,
            dst_ref=dst,
            send_sem=halo_send.at[slot],
            recv_sem=halo_recv.at[slot],
            device_id={"lat": to_lat, "lon": to_lon},
            device_id_type=MESH,
        )

    to_west = halo(0, edge_left, halo_col.at[1, pl.ds(16, 64)], lat, west)
    to_east = halo(1, edge_right, halo_col.at[0, pl.ds(16, 64)], lat, east)
    north = [
        halo(2, tokens.at[0], halo_row.at[1], lat - 1, lon),
        halo(3, edge_left.at[pl.ds(0, 16)], halo_col.at[1, pl.ds(80, 16)], lat - 1, west),
        halo(4, edge_right.at[pl.ds(0, 16)], halo_col.at[0, pl.ds(80, 16)], lat - 1, east),
    ]
    south = [
        halo(5, tokens.at[ROWS - 1], halo_row.at[0], lat + 1, lon),
        halo(6, edge_left.at[pl.ds(48, 16)], halo_col.at[1, pl.ds(0, 16)], lat + 1, west),
        halo(7, edge_right.at[pl.ds(48, 16)], halo_col.at[0, pl.ds(0, 16)], lat + 1, east),
    ]
    to_west.start()
    to_east.start()

    @pl.when(lat > 0)
    def _():
        for c in north:
            c.start()

    @pl.when(lat < lats - 1)
    def _():
        for c in south:
            c.start()

    @pl.when(lat == 0)
    def _():
        halo_row[0] = jnp.zeros((COLS, D), BF16)
        halo_col[0, 0:16] = jnp.zeros((16, D), BF16)
        halo_col[1, 0:16] = jnp.zeros((16, D), BF16)

    @pl.when(lat == lats - 1)
    def _():
        halo_row[1] = jnp.zeros((COLS, D), BF16)
        halo_col[0, 80:96] = jnp.zeros((16, D), BF16)
        halo_col[1, 80:96] = jnp.zeros((16, D), BF16)

    def expand_rows(first, count):
        def store(c, v):
            e_mid[pl.ds(first + 1, count), :, c : c + 256] = v.reshape(count, COLS, 256)

        x = tokens[pl.ds(first, count)].reshape(count * COLS, D)
        expand(x, gain_conv[...], average[...], w_expand, store)

    expand_rows(0, 1)
    expand_rows(31, 2)

    to_west.wait()
    to_east.wait()

    @pl.when(lat > 0)
    def _():
        for c in north:
            c.wait_send()
        for c in south:
            c.wait_recv()

    @pl.when(lat < lats - 1)
    def _():
        for c in south:
            c.wait_send()
        for c in north:
            c.wait_recv()

    def store_rows(c, v):
        e_mid[0, :, c : c + 256] = v[0:64]
        e_mid[65, :, c : c + 256] = v[64:128]

    expand(halo_row[...].reshape(2 * COLS, D), gain_conv[...], average[...], w_expand, store_rows)

    def store_cols(c, v):
        e_edge[:, c : c + 256] = v

    expand(halo_col[...].reshape(192, D), gain_conv[...], average[...], w_expand, store_cols)
    for c in range(0, HID, 256):
        total = jnp.zeros((8, 16, 256), F32)
        for dy in range(3):
            moved = dot(edge_shift[dy], e_edge[:, c : c + 256]).reshape(8, 16, 256)
            total = total + moved * dw_edge[dy, :, c : c + 256][None]
        edge_sum[:, :, c : c + 256] = total.astype(BF16)

    def conv_band(band):
        first = band * 8

        def row(r, carry):
            for c in range(0, HID, 256):
                parts = []
                e = [e_mid[first + r + dy, :, c : c + 256] for dy in range(3)]
                for dx in range(3):
                    acc = None
                    for dy in range(3):
                        w = dw16[3 * dy + dx, :, c : c + 256]
                        w = jnp.concatenate([w] * 4, axis=0)
                        term = e[dy] * w
                        acc = term if acc is None else acc + term
                    parts.append(acc)
                parts.append(edge_sum[band, :, c : c + 256])
                total = dot(shifts[r], jnp.concatenate(parts, axis=0))
                conv[pl.ds(r * 64, 64), c : c + 256] = gelu(total.astype(BF16))
            return carry

        lax.fori_loop(0, 8, row, 0, unroll=2)

    def pieces(x):
        return jnp.concatenate(
            [x[64 * b + 8 * a : 64 * b + 8 * a + 8] for a in range(8) for b in range(8)], axis=0
        )

    def send(phase):
        def one(i, carry):
            pltpu.make_async_remote_copy(
                src_ref=blocked.at[
                    :, phase * 8 + i // 4, pl.ds(pl.multiple_of(lax.rem(i, 4) * 16, 16), 16), :
                ],
                dst_ref=received.at[phase, lat, :, place],
                send_sem=send_sem.at[phase],
                recv_sem=recv_sem.at[phase],
                device_id=partner(i),
                device_id_type=MESH,
            ).start()
            return carry

        lax.fori_loop(0, 32, one, 0)

    def send_back(phase):
        def one(i, carry):
            pltpu.make_async_remote_copy(
                src_ref=outgoing.at[phase, i // 8, :, lax.rem(i, 8)],
                dst_ref=out.at[
                    :, phase * 8 + my_row, pl.ds(pl.multiple_of(my_col * 16, 16), 16), :
                ],
                send_sem=back_send.at[phase],
                recv_sem=back_recv.at[phase],
                device_id=partner(i),
                device_id_type=MESH,
            ).start()
            return carry

        lax.fori_loop(0, 32, one, 0)

    def conv_and_block(phase):
        def half(i, carry):
            band = i * 4 + phase
            first = band * 8

            @pl.when(band < 7)
            def _():
                expand_rows(first + 1, 8)

            @pl.when(band == 7)
            def _():
                expand_rows(first + 1, 7)

            conv_band(band)
            x = tokens[pl.ds(first, 8)].reshape(512, D).astype(F32)
            mixed[...] = pieces(x + dot(conv[0:512], w_project[...])).astype(BF16)
            result = attend(
                mixed, gain_block, average, qkv_block, bias_block, out_block, masks, select,
                ones_bd, qkv, att,
            )
            blocked[i, pl.ds(phase * 8, 8)] = (
                pieces(result + mixed[...].astype(F32)).astype(BF16).reshape(8, 64, D)
            )
            return carry

        lax.fori_loop(0, 2, half, 0)

    def grid(phase):
        for half in range(2):
            for q in range(4):
                x = received[phase, q].reshape(256, D)
                y = dot(perm[128 * half : 128 * half + 128], x).astype(BF16)
                for p in range(8):
                    mixed[64 * p + 16 * q : 64 * p + 16 * q + 16] = y[16 * p : 16 * p + 16]
            result = attend(
                mixed, gain_grid, average, qkv_grid, bias_grid, out_grid, masks, select, ones_bd,
                qkv, att,
            )
            done = (result + mixed[...].astype(F32)).astype(BF16)
            for q in range(4):
                conv[256 * q + 128 * half : 256 * q + 128 * half + 128, 0:256] = jnp.concatenate(
                    [done[64 * p + 16 * q : 64 * p + 16 * q + 16] for p in range(8)], axis=0
                )
        for q in range(4):
            y = dot(perm[...], conv[256 * q : 256 * q + 256, 0:256]).astype(BF16)
            outgoing[phase, q] = y.reshape(2, 8, 16, D)

    def wait_all(ref, sem):
        pltpu.make_async_copy(ref, ref, sem).wait()

    def step(phase, carry):
        @pl.when(phase < PHASES)
        def _():
            conv_and_block(phase)
            send(phase)

        @pl.when(phase > 0)
        def _():
            wait_all(received.at[phase - 1], recv_sem.at[phase - 1])
            grid(phase - 1)
            send_back(phase - 1)

        return carry

    lax.fori_loop(0, PHASES + 1, step, 0)

    def finish(phase, carry):
        wait_all(received.at[phase], send_sem.at[phase])
        wait_all(received.at[phase], back_send.at[phase])
        wait_all(received.at[phase], back_recv.at[phase])
        return carry

    lax.fori_loop(0, PHASES, finish, 0)


def constants():
    average = np.full((D, D), 1.0 / D, np.float32)
    lane_head = np.arange(D) // 32
    masks = np.zeros((HEADS, 16, D), np.float32)
    for h in range(HEADS):
        masks[h, :, lane_head == h] = 1.0
    select = np.zeros((256, 128), np.float32)
    for c in range(128):
        select[c // 16 * 16, c] = 1.0
        select[128 + c // 16 * 16, c] = 1.0
    ones_bd = np.zeros((512, D), np.float32)
    row_head = np.arange(512) // 16 % 8
    ones_bd[row_head[:, None] == lane_head[None, :]] = 1.0
    shifts = np.zeros((8, 64, 208), np.float32)
    for r in range(8):
        for c in range(64):
            if c > 0:
                shifts[r, c, c - 1] = 1.0
            shifts[r, c, 64 + c] = 1.0
            if c < 63:
                shifts[r, c, 128 + c + 1] = 1.0
        shifts[r, 0, 192 + r] = 1.0
        shifts[r, 63, 200 + r] = 1.0
    edge_shift = np.zeros((3, 128, 192), np.float32)
    for dy in range(3):
        for band in range(8):
            for side in range(2):
                for r in range(8):
                    edge_shift[dy, band * 16 + side * 8 + r, side * 96 + 16 + band * 8 + r + dy - 1] = 1
    perm = np.zeros((256, 256), np.float32)
    for p in range(16):
        for s in range(16):
            perm[p * 16 + s, s * 16 + p] = 1.0
    return [
        jnp.asarray(a, BF16)
        for a in (average, masks, select, ones_bd, shifts, edge_shift, perm)
    ]


def spread_bias(bias):
    return (
        (bias * LOG2E).reshape(HEADS, 64, 4, 16).transpose(1, 2, 0, 3).reshape(64, 512)
    )


def shards(
    tokens,
    gain_conv,
    w_expand,
    dw_kernel,
    w_project,
    gain_block,
    qkv_block,
    bias_block,
    out_block,
    gain_grid,
    qkv_grid,
    bias_grid,
    out_grid,
):
    dw16 = jnp.broadcast_to(dw_kernel.astype(BF16).reshape(9, 1, HID), (9, 16, HID))
    dw_edge = jnp.repeat(dw_kernel[:, 0::2, :], 8, axis=1)
    operands = [
        tokens,
        tokens[:, 0],
        tokens[:, COLS - 1],
        gain_conv.reshape(1, D),
        w_expand,
        dw16,
        dw_edge,
        w_project,
        gain_block.reshape(1, D),
        qkv_block,
        spread_bias(bias_block),
        out_block,
        gain_grid.reshape(1, D),
        qkv_grid,
        spread_bias(bias_grid),
        out_grid,
        *constants(),
    ]
    result = pl.pallas_call(
        kernel,
        out_shape=jax.ShapeDtypeStruct((2, 32, COLS, D), BF16),
        in_specs=[pl.BlockSpec(memory_space=pltpu.VMEM)] * len(operands),
        out_specs=pl.BlockSpec(memory_space=pltpu.VMEM),
        scratch_shapes=[
            pltpu.VMEM((66, COLS, HID), BF16),
            pltpu.VMEM((192, HID), BF16),
            pltpu.VMEM((2, COLS, D), BF16),
            pltpu.VMEM((2, 96, D), BF16),
            pltpu.VMEM((8, 16, HID), BF16),
            pltpu.VMEM((1024, HID), BF16),
            pltpu.VMEM((512, D), BF16),
            pltpu.VMEM((512, 3 * D), BF16),
            pltpu.VMEM((512, D), BF16),
            pltpu.VMEM((2, 32, COLS, D), BF16),
            pltpu.VMEM((PHASES, 4, 2, 8, 16, D), BF16),
            pltpu.VMEM((PHASES, 4, 2, 8, 16, D), BF16),
            pltpu.SemaphoreType.DMA((8,)),
            pltpu.SemaphoreType.DMA((8,)),
            pltpu.SemaphoreType.DMA((PHASES,)),
            pltpu.SemaphoreType.DMA((PHASES,)),
            pltpu.SemaphoreType.DMA((PHASES,)),
            pltpu.SemaphoreType.DMA((PHASES,)),
        ],
        compiler_params=pltpu.CompilerParams(
            collective_id=0, has_side_effects=True, vmem_limit_bytes=60 * 1024 * 1024
        ),
    )(*operands)
    return result.reshape(ROWS, COLS, D)


def solution(mesh):
    placed = (P("lat", "lon", None), P(), P(), P(), P(), P(), P(), P(), P(), P(), P(), P(), P())
    return jax.shard_map(
        shards, mesh=mesh, in_specs=placed, out_specs=P("lat", "lon", None), check_vma=False
    )
```

```python
import jax
import jax.numpy as jnp
from jax import lax
from jax.experimental import pallas as pl
from jax.experimental.pallas import tpu as pltpu
from jax.sharding import PartitionSpec as P

MESH = pl.DeviceIdType.MESH
BF16 = jnp.bfloat16
F32 = jnp.float32
ROWS, COLS, D, HID, HEADS = 64, 64, 256, 1024, 8
PHASES = 4
BATCH = 16
LOG2E = 1.4426950408889634


def dot(a, b):
    return jnp.dot(a, b, preferred_element_type=F32)


def dot_nt(a, b):
    return lax.dot_general(a, b, (((1,), (1,)), ((), ())), preferred_element_type=F32)


def exp2(x):
    return jnp.exp2(x)


def gelu(x):
    half = x * BF16(0.5)
    inner = x * (BF16(0.7978845608) + BF16(0.035677408) * (x * x))
    return half + half * jnp.tanh(inner)


def norm(x, gain):
    xf = x.astype(F32)
    d = xf - jnp.mean(xf, axis=-1, keepdims=True)
    var = jnp.mean(d * d, axis=-1, keepdims=True)
    return (d * lax.rsqrt(var + 1e-05) * gain).astype(BF16)


def expand(x, gain, w_expand, store):
    n = norm(x, gain)
    for c in range(0, HID, 256):
        store(c, gelu(dot(n, w_expand[:, c : c + 256]).astype(BF16)))


def blocks(m, masks):
    return jnp.concatenate(
        [m[16 * i : 16 * i + 16] * masks[h] for i in range(4) for h in range(4)], axis=0
    )


def head_top(pairs, select):
    wide = [jnp.maximum(x, pltpu.roll(x, 64, 1)) for x in pairs]
    lane = lax.broadcasted_iota(jnp.int32, wide[0].shape, 1)
    top = jnp.where(lane < 64, wide[0], wide[1])
    for shift in (8, 4, 2, 1):
        top = jnp.maximum(top, pltpu.roll(top, 128 - shift, 1))
    high = top.astype(BF16)
    low = (top - high.astype(F32)).astype(BF16)
    return dot(jnp.concatenate([high, low], axis=1), select[...])


def attend(x_ref, gain, w_qkv, bias, w_out, masks, select, ones_bd, qkv, mixed):
    n = norm(x_ref[...], gain[...])
    scale = LOG2E / 32**0.5
    qkv[:, 0:256] = (dot(n, w_qkv[:, 0:256]) * scale).astype(BF16)
    qkv[:, 256:512] = dot(n, w_qkv[:, 256:512]).astype(BF16)
    qkv[:, 512:768] = dot(n, w_qkv[:, 512:768]).astype(BF16)
    size = BATCH * 64

    def batch(first):
        rows = [pl.ds(first + i * 64, 64) for i in range(BATCH)]
        scores = [
            jnp.concatenate(
                [
                    dot_nt(
                        qkv[r, 128 * u : 128 * u + 128],
                        blocks(qkv[r, 256 + 128 * u : 384 + 128 * u], masks),
                    )
                    + bias[:, 256 * u : 256 * u + 256]
                    for r in rows
                ],
                axis=0,
            )
            for u in range(2)
        ]
        top = head_top([jnp.maximum(s[:, 0:128], s[:, 128:256]) for s in scores], select)
        weights, sums = [], []
        for u, s in enumerate(scores):
            t = top[:, 128 * u : 128 * u + 128]
            a, b = exp2(s[:, 0:128] - t), exp2(s[:, 128:256] - t)
            sums.append((a + b).astype(BF16))
            weights.append(jnp.concatenate([a.astype(BF16), b.astype(BF16)], axis=1))
        total = dot(jnp.concatenate(sums, axis=1), ones_bd[...])
        values = jnp.concatenate(
            [
                jnp.concatenate(
                    [
                        dot(
                            w[64 * k : 64 * k + 64],
                            blocks(qkv[r, 512 + 128 * u : 640 + 128 * u], masks),
                        )
                        for k, r in enumerate(rows)
                    ],
                    axis=0,
                )
                for u, w in enumerate(weights)
            ],
            axis=1,
        )
        mixed[pl.ds(first, size), :] = (values / total).astype(BF16)

    for first in range(0, x_ref.shape[0], size):
        batch(first)
    return dot(mixed[...], w_out[...])


def spread_bias(source, target):
    lane = lax.broadcasted_iota(jnp.int32, (64, 128), 1)
    for u in range(2):
        twice = []
        for h in range(4):
            x = source[4 * u + h] * LOG2E
            twice.append(jnp.concatenate([x, x], axis=1))
        for tile in range(2):
            acc = twice[0]
            for k in range(2):
                for h in range(4):
                    at, to = (2 * tile + k) * 16, k * 64 + h * 16
                    moved = pltpu.roll(twice[h], (to - at) % 128, 1)
                    acc = jnp.where(lane // 16 == to // 16, moved, acc)
            target[:, 256 * u + 128 * tile : 256 * u + 128 * tile + 128] = acc


def pick(shape, hit):
    row = lax.broadcasted_iota(jnp.int32, shape, 0)
    col = lax.broadcasted_iota(jnp.int32, shape, 1)
    return jnp.where(hit(row, col), 1.0, 0.0).astype(BF16)


def kernel(
    tokens,
    gain_conv,
    w_expand,
    dw_kernel,
    w_project,
    gain_block,
    qkv_block,
    bias_in_block,
    out_block,
    gain_grid,
    qkv_grid,
    bias_in_grid,
    out_grid,
    out,
    e_mid,
    e_edge,
    halo_row,
    halo_col,
    edge,
    edge_sum,
    dw16,
    bias_block,
    bias_grid,
    masks,
    select,
    ones_bd,
    shifts,
    edge_shift,
    perm,
    conv,
    mixed,
    qkv,
    att,
    blocked,
    received,
    outgoing,
    halo_send,
    halo_recv,
    send_sem,
    recv_sem,
    back_send,
    back_recv,
):
    lat = lax.axis_index("lat")
    lon = lax.axis_index("lon")
    lats = lax.axis_size("lat")
    lons = lax.axis_size("lon")
    kind = lax.rem(lon, 4)
    place = lon // 4
    far = 3 - kind
    mine = lat * 8 + place
    my_row, my_col = mine // 4, lax.rem(mine, 4)
    west = lax.rem(lon + lons - 1, lons)
    east = lax.rem(lon + 1, lons)

    def partner(i):
        return {"lat": i // 8, "lon": lax.rem(i, 8) * 4 + far}

    barrier = pltpu.get_barrier_semaphore()

    def greet(i, carry):
        pl.semaphore_signal(barrier, inc=1, device_id=partner(i), device_id_type=MESH)
        return carry

    lax.fori_loop(0, 32, greet, 0)
    for side in (west, east):
        pl.semaphore_signal(
            barrier, inc=1, device_id={"lat": lat, "lon": side}, device_id_type=MESH
        )

    @pl.when(lat > 0)
    def _():
        for side in (lon, west, east):
            pl.semaphore_signal(
                barrier, inc=1, device_id={"lat": lat - 1, "lon": side}, device_id_type=MESH
            )

    @pl.when(lat < lats - 1)
    def _():
        for side in (lon, west, east):
            pl.semaphore_signal(
                barrier, inc=1, device_id={"lat": lat + 1, "lon": side}, device_id_type=MESH
            )

    for h in range(4):
        masks[h] = pick((16, 128), lambda r, c: c // 32 == h)
    select[...] = pick(
        (256, 256), lambda r, c: r % 128 == (c // 128) * 64 + ((c % 64) // 16) * 16
    )
    ones_bd[...] = pick((256, 256), lambda r, c: (r // 128) * 4 + (r % 64) // 16 == c // 32)
    for r8 in range(8):
        shifts[r8] = pick(
            (64, 208),
            lambda r, c: ((c < 64) & (c + 1 == r))
            | ((c >= 64) & (c < 128) & (c - 64 == r))
            | ((c >= 128) & (c < 192) & (c - 129 == r))
            | ((c == 192 + r8) & (r == 0))
            | ((c == 200 + r8) & (r == 63)),
        )
    for dy in range(3):
        edge_shift[dy] = pick(
            (128, 192),
            lambda r, c: c == ((r // 8) % 2) * 96 + 15 + (r // 16) * 8 + r % 8 + dy,
        )
    perm[...] = pick((256, 256), lambda r, c: (r // 16 == c % 16) & (r % 16 == c // 16))
    for side in range(2):
        first = pick((16, 256), lambda r, c: c == r * 16 + 15 * side)
        for q in range(4):
            x = tokens[16 * q : 16 * q + 16, 48 * side : 48 * side + 16].reshape(256, D)
            edge[side, 16 * q : 16 * q + 16] = dot(first, x).astype(BF16)
    for dy in range(3):
        for dx in range(3):
            dw16[3 * dy + dx] = jnp.broadcast_to(dw_kernel[dy, dx : dx + 1], (16, HID)).astype(BF16)

    def expand_rows(first, count):
        def store(c, v):
            e_mid[pl.ds(first + 1, count), :, c : c + 256] = v.reshape(count, COLS, 256)

        x = tokens[pl.ds(first, count)].reshape(count * COLS, D)
        expand(x, gain_conv[...], w_expand, store)

    def expand_band(band, carry):
        expand_rows(band * 8, 8)
        return carry

    lax.fori_loop(0, 5, expand_band, 0)

    inner = jnp.minimum(lat, 1) + jnp.minimum(lats - 1 - lat, 1)
    pl.semaphore_wait(barrier, 34 + 3 * inner)

    def halo(slot, src, dst, to_lat, to_lon):
        return pltpu.make_async_remote_copy(
            src_ref=src,
            dst_ref=dst,
            send_sem=halo_send.at[slot],
            recv_sem=halo_recv.at[slot],
            device_id={"lat": to_lat, "lon": to_lon},
            device_id_type=MESH,
        )

    to_west = halo(0, edge.at[0], halo_col.at[1, pl.ds(16, 64)], lat, west)
    to_east = halo(1, edge.at[1], halo_col.at[0, pl.ds(16, 64)], lat, east)
    north = [
        halo(2, tokens.at[0], halo_row.at[1], lat - 1, lon),
        halo(3, edge.at[0, pl.ds(0, 16)], halo_col.at[1, pl.ds(80, 16)], lat - 1, west),
        halo(4, edge.at[1, pl.ds(0, 16)], halo_col.at[0, pl.ds(80, 16)], lat - 1, east),
    ]
    south = [
        halo(5, tokens.at[ROWS - 1], halo_row.at[0], lat + 1, lon),
        halo(6, edge.at[0, pl.ds(48, 16)], halo_col.at[1, pl.ds(0, 16)], lat + 1, west),
        halo(7, edge.at[1, pl.ds(48, 16)], halo_col.at[0, pl.ds(0, 16)], lat + 1, east),
    ]
    to_west.start()
    to_east.start()

    @pl.when(lat > 0)
    def _():
        for c in north:
            c.start()

    @pl.when(lat < lats - 1)
    def _():
        for c in south:
            c.start()

    @pl.when(lat == 0)
    def _():
        halo_row[0] = jnp.zeros((COLS, D), BF16)
        halo_col[0, 0:16] = jnp.zeros((16, D), BF16)
        halo_col[1, 0:16] = jnp.zeros((16, D), BF16)

    @pl.when(lat == lats - 1)
    def _():
        halo_row[1] = jnp.zeros((COLS, D), BF16)
        halo_col[0, 80:96] = jnp.zeros((16, D), BF16)
        halo_col[1, 80:96] = jnp.zeros((16, D), BF16)

    lax.fori_loop(5, 8, expand_band, 0)
    spread_bias(bias_in_block, bias_block)
    spread_bias(bias_in_grid, bias_grid)

    to_west.wait()
    to_east.wait()

    @pl.when(lat > 0)
    def _():
        for c in north:
            c.wait_send()
        for c in south:
            c.wait_recv()

    @pl.when(lat < lats - 1)
    def _():
        for c in south:
            c.wait_send()
        for c in north:
            c.wait_recv()

    def store_rows(c, v):
        e_mid[0, :, c : c + 256] = v[0:64]
        e_mid[65, :, c : c + 256] = v[64:128]

    expand(halo_row[...].reshape(2 * COLS, D), gain_conv[...], w_expand, store_rows)

    def store_cols(c, v):
        e_edge[:, c : c + 256] = v

    expand(halo_col[...].reshape(192, D), gain_conv[...], w_expand, store_cols)
    for c in range(0, HID, 256):
        total = jnp.zeros((8, 16, 256), F32)
        for dy in range(3):
            moved = dot(edge_shift[dy], e_edge[:, c : c + 256]).reshape(8, 16, 256)
            west_east = [
                jnp.broadcast_to(dw_kernel[dy, dx : dx + 1, c : c + 256], (8, 256)) for dx in (0, 2)
            ]
            total = total + moved * jnp.concatenate(west_east, axis=0)[None]
        edge_sum[:, :, c : c + 256] = total.astype(BF16)

    def conv_band(band, half):
        first = band * 8

        def row(r, carry):
            for c in range(0, HID, 256):
                parts = []
                e = [e_mid[first + r + dy, :, c : c + 256] for dy in range(3)]
                for dx in range(3):
                    acc = None
                    for dy in range(3):
                        w = dw16[3 * dy + dx, :, c : c + 256]
                        w = jnp.concatenate([w] * 4, axis=0)
                        term = e[dy] * w
                        acc = term if acc is None else acc + term
                    parts.append(acc)
                parts.append(edge_sum[band, :, c : c + 256])
                total = dot(shifts[r], jnp.concatenate(parts, axis=0))
                conv[pl.ds(half * 512 + r * 64, 64), c : c + 256] = gelu(total.astype(BF16))
            return carry

        lax.fori_loop(0, 8, row, 0, unroll=2)

    def pieces(x):
        return jnp.concatenate(
            [x[64 * b + 8 * a : 64 * b + 8 * a + 8] for a in range(8) for b in range(8)], axis=0
        )

    def send(phase):
        def one(i, carry):
            pltpu.make_async_remote_copy(
                src_ref=blocked.at[
                    :, phase * 8 + i // 4, pl.ds(pl.multiple_of(lax.rem(i, 4) * 16, 16), 16), :
                ],
                dst_ref=received.at[phase, lat, :, place],
                send_sem=send_sem.at[phase],
                recv_sem=recv_sem.at[phase],
                device_id=partner(i),
                device_id_type=MESH,
            ).start()
            return carry

        lax.fori_loop(0, 32, one, 0)

    def send_back(phase):
        def one(i, carry):
            pltpu.make_async_remote_copy(
                src_ref=outgoing.at[phase, i // 8, :, lax.rem(i, 8)],
                dst_ref=out.at[
                    :, phase * 8 + my_row, pl.ds(pl.multiple_of(my_col * 16, 16), 16), :
                ],
                send_sem=back_send.at[phase],
                recv_sem=back_recv.at[phase],
                device_id=partner(i),
                device_id_type=MESH,
            ).start()
            return carry

        lax.fori_loop(0, 32, one, 0)

    def conv_and_block(phase):
        def half(i, carry):
            band = i * 4 + phase
            conv_band(band, i)
            x = tokens[pl.ds(band * 8, 8)].reshape(512, D).astype(F32)
            rows = pl.ds(pl.multiple_of(i * 512, 512), 512)
            mixed[rows, :] = pieces(x + dot(conv[rows, :], w_project[...])).astype(BF16)
            return carry

        lax.fori_loop(0, 2, half, 0)
        result = attend(
            mixed, gain_block, qkv_block, bias_block, out_block, masks, select, ones_bd, qkv, att
        )
        result = result + mixed[...].astype(F32)
        for i in range(2):
            blocked[i, pl.ds(phase * 8, 8)] = (
                pieces(result[512 * i : 512 * i + 512]).astype(BF16).reshape(8, 64, D)
            )

    def grid(phase):
        for q in range(4):
            x = received[phase, q].reshape(256, D)
            y = dot(perm[...], x).astype(BF16)
            for p in range(16):
                mixed[64 * p + 16 * q : 64 * p + 16 * q + 16] = y[16 * p : 16 * p + 16]
        result = attend(
            mixed, gain_grid, qkv_grid, bias_grid, out_grid, masks, select, ones_bd, qkv, att
        )
        done = (result + mixed[...].astype(F32)).astype(BF16)
        for q in range(4):
            x = jnp.concatenate(
                [done[64 * p + 16 * q : 64 * p + 16 * q + 16] for p in range(16)], axis=0
            )
            outgoing[phase, q] = dot(perm[...], x).astype(BF16).reshape(2, 8, 16, D)

    def wait_all(ref, sem):
        pltpu.make_async_copy(ref, ref, sem).wait()

    def step(phase, carry):
        @pl.when(phase < PHASES)
        def _():
            conv_and_block(phase)
            send(phase)

        @pl.when(phase > 0)
        def _():
            wait_all(received.at[phase - 1], recv_sem.at[phase - 1])
            grid(phase - 1)
            send_back(phase - 1)

        return carry

    lax.fori_loop(0, PHASES + 1, step, 0)

    def finish(phase, carry):
        wait_all(received.at[phase], send_sem.at[phase])
        wait_all(received.at[phase], back_send.at[phase])
        wait_all(received.at[phase], back_recv.at[phase])
        return carry

    lax.fori_loop(0, PHASES, finish, 0)


def shards(
    tokens,
    gain_conv,
    w_expand,
    dw_kernel,
    w_project,
    gain_block,
    qkv_block,
    bias_block,
    out_block,
    gain_grid,
    qkv_grid,
    bias_grid,
    out_grid,
):
    operands = [
        tokens,
        gain_conv.reshape(1, D),
        w_expand,
        dw_kernel,
        w_project,
        gain_block.reshape(1, D),
        qkv_block,
        bias_block,
        out_block,
        gain_grid.reshape(1, D),
        qkv_grid,
        bias_grid,
        out_grid,
    ]
    result = pl.pallas_call(
        kernel,
        out_shape=jax.ShapeDtypeStruct((2, 32, COLS, D), BF16),
        in_specs=[pl.BlockSpec(memory_space=pltpu.VMEM)] * len(operands),
        out_specs=pl.BlockSpec(memory_space=pltpu.VMEM),
        scratch_shapes=[
            pltpu.VMEM((66, COLS, HID), BF16),
            pltpu.VMEM((192, HID), BF16),
            pltpu.VMEM((2, COLS, D), BF16),
            pltpu.VMEM((2, 96, D), BF16),
            pltpu.VMEM((2, 64, D), BF16),
            pltpu.VMEM((8, 16, HID), BF16),
            pltpu.VMEM((9, 16, HID), BF16),
            pltpu.VMEM((64, 512), F32),
            pltpu.VMEM((64, 512), F32),
            pltpu.VMEM((4, 16, 128), BF16),
            pltpu.VMEM((256, 256), BF16),
            pltpu.VMEM((256, 256), BF16),
            pltpu.VMEM((8, 64, 208), BF16),
            pltpu.VMEM((3, 128, 192), BF16),
            pltpu.VMEM((256, 256), BF16),
            pltpu.VMEM((1024, HID), BF16),
            pltpu.VMEM((1024, D), BF16),
            pltpu.VMEM((1024, 3 * D), BF16),
            pltpu.VMEM((1024, D), BF16),
            pltpu.VMEM((2, 32, COLS, D), BF16),
            pltpu.VMEM((PHASES, 4, 2, 8, 16, D), BF16),
            pltpu.VMEM((PHASES, 4, 2, 8, 16, D), BF16),
            pltpu.SemaphoreType.DMA((8,)),
            pltpu.SemaphoreType.DMA((8,)),
            pltpu.SemaphoreType.DMA((PHASES,)),
            pltpu.SemaphoreType.DMA((PHASES,)),
            pltpu.SemaphoreType.DMA((PHASES,)),
            pltpu.SemaphoreType.DMA((PHASES,)),
        ],
        compiler_params=pltpu.CompilerParams(
            collective_id=0, has_side_effects=True, vmem_limit_bytes=60 * 1024 * 1024
        ),
    )(*operands)
    return result.reshape(ROWS, COLS, D)


def solution(mesh):
    placed = (P("lat", "lon", None), P(), P(), P(), P(), P(), P(), P(), P(), P(), P(), P(), P())
    return jax.shard_map(
        shards, mesh=mesh, in_specs=placed, out_specs=P("lat", "lon", None), check_vma=False
    )
```

```python
import jax
import jax.numpy as jnp
from jax import lax
from jax.experimental import pallas as pl
from jax.experimental.pallas import tpu as pltpu
from jax.sharding import PartitionSpec as P

MESH = pl.DeviceIdType.MESH
BF16 = jnp.bfloat16
F32 = jnp.float32
ROWS, COLS, D, HID, HEADS = 64, 64, 256, 1024, 8
PHASES = 4
BATCH = 16
LOG2E = 1.4426950408889634


def dot(a, b):
    return jnp.dot(a, b, preferred_element_type=F32)


def dot_nt(a, b):
    return lax.dot_general(a, b, (((1,), (1,)), ((), ())), preferred_element_type=F32)


def exp2(x):
    return jnp.exp2(x)


def gelu(x):
    half = x * BF16(0.5)
    inner = x * (BF16(0.7978845608) + BF16(0.035677408) * (x * x))
    return half + half * jnp.tanh(inner)


def norm(x, gain):
    xf = x.astype(F32)
    d = xf - jnp.mean(xf, axis=-1, keepdims=True)
    var = jnp.mean(d * d, axis=-1, keepdims=True)
    return (d * lax.rsqrt(var + 1e-05) * gain).astype(BF16)


def expand(x, gain, w_expand, store):
    n = norm(x, gain)
    for c in range(0, HID, 256):
        store(c, gelu(dot(n, w_expand[:, c : c + 256]).astype(BF16)))


def blocks(m, masks):
    return jnp.concatenate(
        [m[16 * i : 16 * i + 16] * masks[h] for i in range(4) for h in range(4)], axis=0
    )


def head_top(pairs, select):
    wide = [jnp.maximum(x, pltpu.roll(x, 64, 1)) for x in pairs]
    lane = lax.broadcasted_iota(jnp.int32, wide[0].shape, 1)
    top = jnp.where(lane < 64, wide[0], wide[1])
    for shift in (8, 4, 2, 1):
        top = jnp.maximum(top, pltpu.roll(top, 128 - shift, 1))
    high = top.astype(BF16)
    low = (top - high.astype(F32)).astype(BF16)
    return dot(jnp.concatenate([high, low], axis=1), select[...])


def attend(x_ref, gain, w_qkv, bias, w_out, masks, select, ones_bd, qkv, mixed):
    n = norm(x_ref[...], gain[...])
    scale = LOG2E / 32**0.5
    qkv[:, 0:256] = (dot(n, w_qkv[:, 0:256]) * scale).astype(BF16)
    qkv[:, 256:512] = dot(n, w_qkv[:, 256:512]).astype(BF16)
    qkv[:, 512:768] = dot(n, w_qkv[:, 512:768]).astype(BF16)
    size = min(BATCH * 64, x_ref.shape[0])

    def batch(first):
        rows = [pl.ds(first + i * 64, 64) for i in range(size // 64)]
        scores = [
            jnp.concatenate(
                [
                    dot_nt(
                        qkv[r, 128 * u : 128 * u + 128],
                        blocks(qkv[r, 256 + 128 * u : 384 + 128 * u], masks),
                    )
                    + bias[:, 256 * u : 256 * u + 256]
                    for r in rows
                ],
                axis=0,
            )
            for u in range(2)
        ]
        top = head_top([jnp.maximum(s[:, 0:128], s[:, 128:256]) for s in scores], select)
        weights, sums = [], []
        for u, s in enumerate(scores):
            t = top[:, 128 * u : 128 * u + 128]
            a, b = exp2(s[:, 0:128] - t), exp2(s[:, 128:256] - t)
            sums.append((a + b).astype(BF16))
            weights.append(jnp.concatenate([a.astype(BF16), b.astype(BF16)], axis=1))
        total = dot(jnp.concatenate(sums, axis=1), ones_bd[...])
        values = jnp.concatenate(
            [
                jnp.concatenate(
                    [
                        dot(
                            w[64 * k : 64 * k + 64],
                            blocks(qkv[r, 512 + 128 * u : 640 + 128 * u], masks),
                        )
                        for k, r in enumerate(rows)
                    ],
                    axis=0,
                )
                for u, w in enumerate(weights)
            ],
            axis=1,
        )
        mixed[pl.ds(first, size), :] = (values / total).astype(BF16)

    for first in range(0, x_ref.shape[0], size):
        batch(first)
    return dot(mixed[...], w_out[...])


def spread_bias(source, target):
    lane = lax.broadcasted_iota(jnp.int32, (64, 128), 1)
    for u in range(2):
        twice = []
        for h in range(4):
            x = source[4 * u + h] * LOG2E
            twice.append(jnp.concatenate([x, x], axis=1))
        for tile in range(2):
            acc = twice[0]
            for k in range(2):
                for h in range(4):
                    at, to = (2 * tile + k) * 16, k * 64 + h * 16
                    moved = pltpu.roll(twice[h], (to - at) % 128, 1)
                    acc = jnp.where(lane // 16 == to // 16, moved, acc)
            target[:, 256 * u + 128 * tile : 256 * u + 128 * tile + 128] = acc


def pick(shape, hit):
    row = lax.broadcasted_iota(jnp.int32, shape, 0)
    col = lax.broadcasted_iota(jnp.int32, shape, 1)
    return jnp.where(hit(row, col), 1.0, 0.0).astype(BF16)


def kernel(
    tokens_hbm,
    gain_conv_hbm,
    w_expand_hbm,
    dw_kernel_hbm,
    w_project_hbm,
    gain_block_hbm,
    qkv_block_hbm,
    bias_in_block_hbm,
    out_block_hbm,
    gain_grid_hbm,
    qkv_grid_hbm,
    bias_in_grid_hbm,
    out_grid_hbm,
    out,
    e_mid,
    e_edge,
    halo_row,
    halo_col,
    edge,
    edge_sum,
    dw16,
    bias_block,
    bias_grid,
    masks,
    select,
    ones_bd,
    shifts,
    edge_shift,
    perm,
    conv,
    mixed,
    qkv,
    att,
    blocked,
    received,
    outgoing,
    halo_send,
    halo_recv,
    send_sem,
    recv_sem,
    back_send,
    back_recv,
    tokens,
    gain_conv,
    w_expand,
    dw_kernel,
    w_project,
    gain_block,
    qkv_block,
    bias_in_block,
    out_block,
    gain_grid,
    qkv_grid,
    bias_in_grid,
    out_grid,
    fetch_sem,
):
    lat = lax.axis_index("lat")
    lon = lax.axis_index("lon")
    lats = lax.axis_size("lat")
    lons = lax.axis_size("lon")
    kind = lax.rem(lon, 4)
    place = lon // 4
    far = 3 - kind
    mine = lat * 8 + place
    my_row, my_col = mine // 4, lax.rem(mine, 4)
    west = lax.rem(lon + lons - 1, lons)
    east = lax.rem(lon + 1, lons)

    def partner(i):
        return {"lat": i // 8, "lon": lax.rem(i, 8) * 4 + far}

    fetched = [
        pltpu.make_async_copy(src, dst, fetch_sem.at[i])
        for i, (src, dst) in enumerate(
            [
                (tokens_hbm, tokens),
                (w_expand_hbm, w_expand),
                (gain_conv_hbm, gain_conv),
                (dw_kernel_hbm, dw_kernel),
                (bias_in_block_hbm, bias_in_block),
                (bias_in_grid_hbm, bias_in_grid),
                (w_project_hbm, w_project),
                (gain_block_hbm, gain_block),
                (qkv_block_hbm, qkv_block),
                (out_block_hbm, out_block),
                (gain_grid_hbm, gain_grid),
                (qkv_grid_hbm, qkv_grid),
                (out_grid_hbm, out_grid),
            ]
        )
    ]
    for copy in fetched:
        copy.start()

    barrier = pltpu.get_barrier_semaphore()

    def greet(i, carry):
        pl.semaphore_signal(barrier, inc=1, device_id=partner(i), device_id_type=MESH)
        return carry

    lax.fori_loop(0, 32, greet, 0)
    for side in (west, east):
        pl.semaphore_signal(
            barrier, inc=1, device_id={"lat": lat, "lon": side}, device_id_type=MESH
        )

    @pl.when(lat > 0)
    def _():
        for side in (lon, west, east):
            pl.semaphore_signal(
                barrier, inc=1, device_id={"lat": lat - 1, "lon": side}, device_id_type=MESH
            )

    @pl.when(lat < lats - 1)
    def _():
        for side in (lon, west, east):
            pl.semaphore_signal(
                barrier, inc=1, device_id={"lat": lat + 1, "lon": side}, device_id_type=MESH
            )

    for copy in fetched[:3]:
        copy.wait()
    for side in range(2):
        first = pick((16, 256), lambda r, c: c == r * 16 + 15 * side)
        for q in range(4):
            x = tokens[16 * q : 16 * q + 16, 48 * side : 48 * side + 16].reshape(256, D)
            edge[side, 16 * q : 16 * q + 16] = dot(first, x).astype(BF16)

    def expand_rows(first, count):
        def store(c, v):
            e_mid[pl.ds(first + 1, count), :, c : c + 256] = v.reshape(count, COLS, 256)

        x = tokens[pl.ds(first, count)].reshape(count * COLS, D)
        expand(x, gain_conv[...], w_expand, store)

    expand_rows(0, 9)

    inner = jnp.minimum(lat, 1) + jnp.minimum(lats - 1 - lat, 1)
    pl.semaphore_wait(barrier, 34 + 3 * inner)

    def halo(slot, src, dst, to_lat, to_lon):
        return pltpu.make_async_remote_copy(
            src_ref=src,
            dst_ref=dst,
            send_sem=halo_send.at[slot],
            recv_sem=halo_recv.at[slot],
            device_id={"lat": to_lat, "lon": to_lon},
            device_id_type=MESH,
        )

    to_west = halo(0, edge.at[0], halo_col.at[1, pl.ds(16, 64)], lat, west)
    to_east = halo(1, edge.at[1], halo_col.at[0, pl.ds(16, 64)], lat, east)
    north = [
        halo(2, tokens.at[0], halo_row.at[1], lat - 1, lon),
        halo(3, edge.at[0, pl.ds(0, 16)], halo_col.at[1, pl.ds(80, 16)], lat - 1, west),
        halo(4, edge.at[1, pl.ds(0, 16)], halo_col.at[0, pl.ds(80, 16)], lat - 1, east),
    ]
    south = [
        halo(5, tokens.at[ROWS - 1], halo_row.at[0], lat + 1, lon),
        halo(6, edge.at[0, pl.ds(48, 16)], halo_col.at[1, pl.ds(0, 16)], lat + 1, west),
        halo(7, edge.at[1, pl.ds(48, 16)], halo_col.at[0, pl.ds(0, 16)], lat + 1, east),
    ]
    to_west.start()
    to_east.start()

    @pl.when(lat > 0)
    def _():
        for c in north:
            c.start()

    @pl.when(lat < lats - 1)
    def _():
        for c in south:
            c.start()

    @pl.when(lat == 0)
    def _():
        halo_row[0] = jnp.zeros((COLS, D), BF16)
        halo_col[0, 0:16] = jnp.zeros((16, D), BF16)
        halo_col[1, 0:16] = jnp.zeros((16, D), BF16)

    @pl.when(lat == lats - 1)
    def _():
        halo_row[1] = jnp.zeros((COLS, D), BF16)
        halo_col[0, 80:96] = jnp.zeros((16, D), BF16)
        halo_col[1, 80:96] = jnp.zeros((16, D), BF16)

    expand_rows(31, 10)
    for copy in fetched[3:]:
        copy.wait()
    for h in range(4):
        masks[h] = pick((16, 128), lambda r, c: c // 32 == h)
    select[...] = pick(
        (256, 256), lambda r, c: r % 128 == (c // 128) * 64 + ((c % 64) // 16) * 16
    )
    ones_bd[...] = pick((256, 256), lambda r, c: (r // 128) * 4 + (r % 64) // 16 == c // 32)
    for r8 in range(8):
        shifts[r8] = pick(
            (64, 208),
            lambda r, c: ((c < 64) & (c + 1 == r))
            | ((c >= 64) & (c < 128) & (c - 64 == r))
            | ((c >= 128) & (c < 192) & (c - 129 == r))
            | ((c == 192 + r8) & (r == 0))
            | ((c == 200 + r8) & (r == 63)),
        )
    for dy in range(3):
        edge_shift[dy] = pick(
            (128, 192),
            lambda r, c: c == ((r // 8) % 2) * 96 + 15 + (r // 16) * 8 + r % 8 + dy,
        )
    perm[...] = pick((256, 256), lambda r, c: (r // 16 == c % 16) & (r % 16 == c // 16))
    for dy in range(3):
        for dx in range(3):
            dw16[3 * dy + dx] = jnp.broadcast_to(dw_kernel[dy, dx : dx + 1], (16, HID)).astype(BF16)

    spread_bias(bias_in_block, bias_block)
    spread_bias(bias_in_grid, bias_grid)

    to_west.wait()
    to_east.wait()

    @pl.when(lat > 0)
    def _():
        for c in north:
            c.wait_send()
        for c in south:
            c.wait_recv()

    @pl.when(lat < lats - 1)
    def _():
        for c in south:
            c.wait_send()
        for c in north:
            c.wait_recv()

    def store_rows(c, v):
        e_mid[0, :, c : c + 256] = v[0:64]
        e_mid[65, :, c : c + 256] = v[64:128]

    expand(halo_row[...].reshape(2 * COLS, D), gain_conv[...], w_expand, store_rows)

    def store_cols(c, v):
        e_edge[:, c : c + 256] = v

    expand(halo_col[...].reshape(192, D), gain_conv[...], w_expand, store_cols)
    for c in range(0, HID, 256):
        total = jnp.zeros((8, 16, 256), F32)
        for dy in range(3):
            moved = dot(edge_shift[dy], e_edge[:, c : c + 256]).reshape(8, 16, 256)
            west_east = [
                jnp.broadcast_to(dw_kernel[dy, dx : dx + 1, c : c + 256], (8, 256)) for dx in (0, 2)
            ]
            total = total + moved * jnp.concatenate(west_east, axis=0)[None]
        edge_sum[:, :, c : c + 256] = total.astype(BF16)

    def conv_band(band):
        first = band * 8

        def row(r, carry):
            for c in range(0, HID, 256):
                parts = []
                e = [e_mid[first + r + dy, :, c : c + 256] for dy in range(3)]
                for dx in range(3):
                    acc = None
                    for dy in range(3):
                        w = dw16[3 * dy + dx, :, c : c + 256]
                        w = jnp.concatenate([w] * 4, axis=0)
                        term = e[dy] * w
                        acc = term if acc is None else acc + term
                    parts.append(acc)
                parts.append(edge_sum[band, :, c : c + 256])
                total = dot(shifts[r], jnp.concatenate(parts, axis=0))
                conv[pl.ds(r * 64, 64), c : c + 256] = gelu(total.astype(BF16))
            return carry

        lax.fori_loop(0, 8, row, 0, unroll=4)

    def pieces(x):
        return jnp.concatenate(
            [x[64 * b + 8 * a : 64 * b + 8 * a + 8] for a in range(8) for b in range(8)], axis=0
        )

    def send(phase, half):
        def one(i, carry):
            pltpu.make_async_remote_copy(
                src_ref=blocked.at[
                    half, phase * 8 + i // 4, pl.ds(pl.multiple_of(lax.rem(i, 4) * 16, 16), 16), :
                ],
                dst_ref=received.at[phase, lat, half, place],
                send_sem=send_sem.at[phase],
                recv_sem=recv_sem.at[phase],
                device_id=partner(i),
                device_id_type=MESH,
            ).start()
            return carry

        lax.fori_loop(0, 32, one, 0, unroll=True)

    def send_back(phase):
        def one(i, carry):
            pltpu.make_async_remote_copy(
                src_ref=outgoing.at[phase, i // 8, :, lax.rem(i, 8)],
                dst_ref=out.at[
                    :, phase * 8 + my_row, pl.ds(pl.multiple_of(my_col * 16, 16), 16), :
                ],
                send_sem=back_send.at[phase],
                recv_sem=back_recv.at[phase],
                device_id=partner(i),
                device_id_type=MESH,
            ).start()
            return carry

        lax.fori_loop(0, 32, one, 0, unroll=True)

    def conv_and_block(phase):
        def half(i, carry):
            band = i * 4 + phase
            first = band * 8

            @pl.when((phase > 0) & (band < 7))
            def _():
                expand_rows(first + 1, 8)

            @pl.when(band == 7)
            def _():
                expand_rows(first + 1, 7)

            conv_band(band)
            x = tokens[pl.ds(first, 8)].reshape(512, D).astype(F32)
            x = pieces(x + dot(conv[0:512, :], w_project[...])).astype(BF16)
            mixed[0:512, :] = x
            result = attend(
                mixed.at[0:512], gain_block, qkv_block, bias_block, out_block, masks, select,
                ones_bd, qkv.at[0:512], att.at[0:512],
            )
            blocked[i, pl.ds(phase * 8, 8)] = (
                pieces(result + x.astype(F32)).astype(BF16).reshape(8, 64, D)
            )
            send(phase, i)
            return carry

        lax.fori_loop(0, 2, half, 0)

    def grid(phase):
        for q in range(4):
            x = received[phase, q].reshape(256, D)
            y = dot(perm[...], x).astype(BF16)
            for p in range(16):
                mixed[64 * p + 16 * q : 64 * p + 16 * q + 16] = y[16 * p : 16 * p + 16]
        result = attend(
            mixed, gain_grid, qkv_grid, bias_grid, out_grid, masks, select, ones_bd, qkv, att
        )
        done = (result + mixed[...].astype(F32)).astype(BF16)
        for q in range(4):
            x = jnp.concatenate(
                [done[64 * p + 16 * q : 64 * p + 16 * q + 16] for p in range(16)], axis=0
            )
            outgoing[phase, q] = dot(perm[...], x).astype(BF16).reshape(2, 8, 16, D)

    def wait_all(ref, sem):
        pltpu.make_async_copy(ref, ref, sem).wait()

    def step(phase, carry):
        @pl.when(phase < PHASES)
        def _():
            conv_and_block(phase)

        @pl.when(phase > 0)
        def _():
            wait_all(received.at[phase - 1], recv_sem.at[phase - 1])
            grid(phase - 1)
            send_back(phase - 1)

        return carry

    lax.fori_loop(0, PHASES + 1, step, 0)

    def finish(phase, carry):
        wait_all(received.at[phase], send_sem.at[phase])
        wait_all(received.at[phase], back_send.at[phase])
        wait_all(received.at[phase], back_recv.at[phase])
        return carry

    lax.fori_loop(0, PHASES, finish, 0)


def copy_kernel(source, target, sem):
    parts = [
        pltpu.make_async_copy(source.at[pl.ds(8 * i, 8)], target.at[pl.ds(8 * i, 8)], sem.at[i])
        for i in range(8)
    ]
    for part in parts:
        part.start()
    for part in parts:
        part.wait()


def shards(
    tokens,
    gain_conv,
    w_expand,
    dw_kernel,
    w_project,
    gain_block,
    qkv_block,
    bias_block,
    out_block,
    gain_grid,
    qkv_grid,
    bias_grid,
    out_grid,
):
    operands = [
        tokens,
        gain_conv.reshape(1, D),
        w_expand,
        dw_kernel,
        w_project,
        gain_block.reshape(1, D),
        qkv_block,
        bias_block,
        out_block,
        gain_grid.reshape(1, D),
        qkv_grid,
        bias_grid,
        out_grid,
    ]
    result = pl.pallas_call(
        kernel,
        out_shape=jax.ShapeDtypeStruct((2, 32, COLS, D), BF16),
        in_specs=[pl.BlockSpec(memory_space=pl.ANY)] * len(operands),
        out_specs=pl.BlockSpec(memory_space=pl.ANY),
        scratch_shapes=[
            pltpu.VMEM((66, COLS, HID), BF16),
            pltpu.VMEM((192, HID), BF16),
            pltpu.VMEM((2, COLS, D), BF16),
            pltpu.VMEM((2, 96, D), BF16),
            pltpu.VMEM((2, 64, D), BF16),
            pltpu.VMEM((8, 16, HID), BF16),
            pltpu.VMEM((9, 16, HID), BF16),
            pltpu.VMEM((64, 512), F32),
            pltpu.VMEM((64, 512), F32),
            pltpu.VMEM((4, 16, 128), BF16),
            pltpu.VMEM((256, 256), BF16),
            pltpu.VMEM((256, 256), BF16),
            pltpu.VMEM((8, 64, 208), BF16),
            pltpu.VMEM((3, 128, 192), BF16),
            pltpu.VMEM((256, 256), BF16),
            pltpu.VMEM((512, HID), BF16),
            pltpu.VMEM((1024, D), BF16),
            pltpu.VMEM((1024, 3 * D), BF16),
            pltpu.VMEM((1024, D), BF16),
            pltpu.VMEM((2, 32, COLS, D), BF16),
            pltpu.VMEM((PHASES, 4, 2, 8, 16, D), BF16),
            pltpu.VMEM((PHASES, 4, 2, 8, 16, D), BF16),
            pltpu.SemaphoreType.DMA((8,)),
            pltpu.SemaphoreType.DMA((8,)),
            pltpu.SemaphoreType.DMA((PHASES,)),
            pltpu.SemaphoreType.DMA((PHASES,)),
            pltpu.SemaphoreType.DMA((PHASES,)),
            pltpu.SemaphoreType.DMA((PHASES,)),
            *[pltpu.VMEM(a.shape, a.dtype) for a in operands],
            pltpu.SemaphoreType.DMA((len(operands),)),
        ],
        compiler_params=pltpu.CompilerParams(
            collective_id=0, has_side_effects=True, vmem_limit_bytes=60 * 1024 * 1024
        ),
    )(*operands)
    result = result.reshape(ROWS, COLS, D)
    return pl.pallas_call(
        copy_kernel,
        out_shape=jax.ShapeDtypeStruct(result.shape, result.dtype),
        in_specs=[pl.BlockSpec(memory_space=pl.ANY)],
        out_specs=pl.BlockSpec(memory_space=pl.ANY),
        scratch_shapes=[pltpu.SemaphoreType.DMA((8,))],
    )(result)


def solution(mesh):
    placed = (P("lat", "lon", None), P(), P(), P(), P(), P(), P(), P(), P(), P(), P(), P(), P())
    return jax.shard_map(
        shards, mesh=mesh, in_specs=placed, out_specs=P("lat", "lon", None), check_vma=False
    )
```

```python
import jax
import jax.numpy as jnp
from jax import lax
from jax.experimental import pallas as pl
from jax.experimental.pallas import tpu as pltpu
from jax.sharding import PartitionSpec as P

MESH = pl.DeviceIdType.MESH
BF16 = jnp.bfloat16
F32 = jnp.float32
ROWS, COLS, D, HID, HEADS = 64, 64, 256, 1024, 8
PHASES = 4
BATCH = 16
LOG2E = 1.4426950408889634


def dot(a, b):
    return jnp.dot(a, b, preferred_element_type=F32)


def dot_nt(a, b):
    return lax.dot_general(a, b, (((1,), (1,)), ((), ())), preferred_element_type=F32)


def exp2(x):
    return jnp.exp2(x)


def gelu(x):
    half = x * BF16(0.5)
    inner = x * (BF16(0.7978845608) + BF16(0.035677408) * (x * x))
    return half + half * jnp.tanh(inner)


def norm(x, gain, average):
    xf = x.astype(F32)
    d = xf - jnp.mean(xf, axis=-1, keepdims=True)
    var = dot((d * d).astype(BF16), average)
    return (d * lax.rsqrt(var + 1e-05) * gain).astype(BF16)


def expand(x, gain, average, w_expand, store):
    n = norm(x, gain, average)
    for c in range(0, HID, 256):
        store(c, gelu(dot(n, w_expand[:, c : c + 256]).astype(BF16)))


def blocks(m, masks):
    return jnp.concatenate(
        [m[16 * i : 16 * i + 16] * masks[h] for i in range(4) for h in range(4)], axis=0
    )


def head_top(pairs, select):
    wide = [jnp.maximum(x, pltpu.roll(x, 64, 1)) for x in pairs]
    lane = lax.broadcasted_iota(jnp.int32, wide[0].shape, 1)
    top = jnp.where(lane < 64, wide[0], wide[1])
    for shift in (8, 4, 2, 1):
        top = jnp.maximum(top, pltpu.roll(top, 128 - shift, 1))
    high = top.astype(BF16)
    low = (top - high.astype(F32)).astype(BF16)
    return dot(jnp.concatenate([high, low], axis=1), select[...])


def attend(x_ref, gain, average, w_qkv, bias, w_out, masks, select, ones_bd, qkv, mixed):
    n = norm(x_ref[...], gain[...], average[...])
    scale = LOG2E / 32**0.5
    qkv[:, 0:256] = (dot(n, w_qkv[:, 0:256]) * scale).astype(BF16)
    qkv[:, 256:512] = dot(n, w_qkv[:, 256:512]).astype(BF16)
    qkv[:, 512:768] = dot(n, w_qkv[:, 512:768]).astype(BF16)
    size = min(BATCH * 64, x_ref.shape[0])

    def batch(first):
        rows = [pl.ds(first + i * 64, 64) for i in range(size // 64)]
        scores = [
            jnp.concatenate(
                [
                    dot_nt(
                        qkv[r, 128 * u : 128 * u + 128],
                        blocks(qkv[r, 256 + 128 * u : 384 + 128 * u], masks),
                    )
                    + bias[:, 256 * u : 256 * u + 256]
                    for r in rows
                ],
                axis=0,
            )
            for u in range(2)
        ]
        top = head_top([jnp.maximum(s[:, 0:128], s[:, 128:256]) for s in scores], select)
        weights, sums = [], []
        for u, s in enumerate(scores):
            t = top[:, 128 * u : 128 * u + 128]
            a, b = exp2(s[:, 0:128] - t), exp2(s[:, 128:256] - t)
            sums.append((a + b).astype(BF16))
            weights.append(jnp.concatenate([a.astype(BF16), b.astype(BF16)], axis=1))
        total = dot(jnp.concatenate(sums, axis=1), ones_bd[...])
        values = jnp.concatenate(
            [
                jnp.concatenate(
                    [
                        dot(
                            w[64 * k : 64 * k + 64],
                            blocks(qkv[r, 512 + 128 * u : 640 + 128 * u], masks),
                        )
                        for k, r in enumerate(rows)
                    ],
                    axis=0,
                )
                for u, w in enumerate(weights)
            ],
            axis=1,
        )
        mixed[pl.ds(first, size), :] = (values / total).astype(BF16)

    for first in range(0, x_ref.shape[0], size):
        batch(first)
    return dot(mixed[...], w_out[...])


def spread_bias(source, target):
    lane = lax.broadcasted_iota(jnp.int32, (64, 128), 1)
    for u in range(2):
        twice = []
        for h in range(4):
            x = source[4 * u + h] * LOG2E
            twice.append(jnp.concatenate([x, x], axis=1))
        for tile in range(2):
            acc = twice[0]
            for k in range(2):
                for h in range(4):
                    at, to = (2 * tile + k) * 16, k * 64 + h * 16
                    moved = pltpu.roll(twice[h], (to - at) % 128, 1)
                    acc = jnp.where((lane >> 4) == to // 16, moved, acc)
            target[:, 256 * u + 128 * tile : 256 * u + 128 * tile + 128] = acc


def pick(shape, hit):
    row = lax.broadcasted_iota(jnp.int32, shape, 0)
    col = lax.broadcasted_iota(jnp.int32, shape, 1)
    return jnp.where(hit(row, col), 1.0, 0.0).astype(BF16)


def kernel(
    tokens_hbm,
    gain_conv_hbm,
    w_expand_hbm,
    dw_kernel_hbm,
    w_project_hbm,
    gain_block_hbm,
    qkv_block_hbm,
    bias_in_block_hbm,
    out_block_hbm,
    gain_grid_hbm,
    qkv_grid_hbm,
    bias_in_grid_hbm,
    out_grid_hbm,
    out,
    e_mid,
    e_edge,
    halo_row,
    halo_col,
    edge,
    edge_sum,
    dw16,
    bias_block,
    bias_grid,
    average,
    masks,
    select,
    ones_bd,
    shifts,
    edge_shift,
    perm,
    conv,
    mixed,
    qkv,
    att,
    blocked,
    received,
    outgoing,
    halo_send,
    halo_recv,
    send_sem,
    recv_sem,
    back_send,
    back_recv,
    tokens,
    gain_conv,
    w_expand,
    dw_kernel,
    w_project,
    gain_block,
    qkv_block,
    bias_in_block,
    out_block,
    gain_grid,
    qkv_grid,
    bias_in_grid,
    out_grid,
    fetch_sem,
):
    lat = lax.axis_index("lat")
    lon = lax.axis_index("lon")
    lats = lax.axis_size("lat")
    lons = lax.axis_size("lon")
    kind = lax.rem(lon, 4)
    place = lon // 4
    far = 3 - kind
    mine = lat * 8 + place
    my_row, my_col = mine // 4, lax.rem(mine, 4)
    west = lax.rem(lon + lons - 1, lons)
    east = lax.rem(lon + 1, lons)

    def partner(i):
        return {"lat": i // 8, "lon": lax.rem(i, 8) * 4 + far}

    fetched = [
        pltpu.make_async_copy(src, dst, fetch_sem.at[i])
        for i, (src, dst) in enumerate(
            [
                (tokens_hbm, tokens),
                (w_expand_hbm, w_expand),
                (gain_conv_hbm, gain_conv),
                (dw_kernel_hbm, dw_kernel),
                (bias_in_block_hbm, bias_in_block),
                (bias_in_grid_hbm, bias_in_grid),
                (w_project_hbm, w_project),
                (gain_block_hbm, gain_block),
                (qkv_block_hbm, qkv_block),
                (out_block_hbm, out_block),
                (gain_grid_hbm, gain_grid),
                (qkv_grid_hbm, qkv_grid),
                (out_grid_hbm, out_grid),
            ]
        )
    ]
    for copy in fetched:
        copy.start()

    barrier = pltpu.get_barrier_semaphore()

    def greet(i, carry):
        pl.semaphore_signal(barrier, inc=1, device_id=partner(i), device_id_type=MESH)
        return carry

    lax.fori_loop(0, 32, greet, 0)
    for side in (west, east):
        pl.semaphore_signal(
            barrier, inc=1, device_id={"lat": lat, "lon": side}, device_id_type=MESH
        )

    @pl.when(lat > 0)
    def _():
        for side in (lon, west, east):
            pl.semaphore_signal(
                barrier, inc=1, device_id={"lat": lat - 1, "lon": side}, device_id_type=MESH
            )

    @pl.when(lat < lats - 1)
    def _():
        for side in (lon, west, east):
            pl.semaphore_signal(
                barrier, inc=1, device_id={"lat": lat + 1, "lon": side}, device_id_type=MESH
            )

    average[...] = jnp.full((D, D), 1.0 / D, BF16)
    for copy in fetched[:3]:
        copy.wait()
    for side in range(2):
        first = pick((16, 256), lambda r, c: c == r * 16 + 15 * side)
        for q in range(4):
            x = tokens[16 * q : 16 * q + 16, 48 * side : 48 * side + 16].reshape(256, D)
            edge[side, 16 * q : 16 * q + 16] = dot(first, x).astype(BF16)

    def expand_rows(first, count):
        def store(c, v):
            e_mid[pl.ds(first + 1, count), :, c : c + 256] = v.reshape(count, COLS, 256)

        x = tokens[pl.ds(first, count)].reshape(count * COLS, D)
        expand(x, gain_conv[...], average[...], w_expand, store)

    expand_rows(0, 9)

    inner = jnp.minimum(lat, 1) + jnp.minimum(lats - 1 - lat, 1)
    pl.semaphore_wait(barrier, 34 + 3 * inner)

    def halo(slot, src, dst, to_lat, to_lon):
        return pltpu.make_async_remote_copy(
            src_ref=src,
            dst_ref=dst,
            send_sem=halo_send.at[slot],
            recv_sem=halo_recv.at[slot],
            device_id={"lat": to_lat, "lon": to_lon},
            device_id_type=MESH,
        )

    to_west = halo(0, edge.at[0], halo_col.at[1, pl.ds(16, 64)], lat, west)
    to_east = halo(1, edge.at[1], halo_col.at[0, pl.ds(16, 64)], lat, east)
    north = [
        halo(2, tokens.at[0], halo_row.at[1], lat - 1, lon),
        halo(3, edge.at[0, pl.ds(0, 16)], halo_col.at[1, pl.ds(80, 16)], lat - 1, west),
        halo(4, edge.at[1, pl.ds(0, 16)], halo_col.at[0, pl.ds(80, 16)], lat - 1, east),
    ]
    south = [
        halo(5, tokens.at[ROWS - 1], halo_row.at[0], lat + 1, lon),
        halo(6, edge.at[0, pl.ds(48, 16)], halo_col.at[1, pl.ds(0, 16)], lat + 1, west),
        halo(7, edge.at[1, pl.ds(48, 16)], halo_col.at[0, pl.ds(0, 16)], lat + 1, east),
    ]
    to_west.start()
    to_east.start()

    @pl.when(lat > 0)
    def _():
        for c in north:
            c.start()

    @pl.when(lat < lats - 1)
    def _():
        for c in south:
            c.start()

    @pl.when(lat == 0)
    def _():
        halo_row[0] = jnp.zeros((COLS, D), BF16)
        halo_col[0, 0:16] = jnp.zeros((16, D), BF16)
        halo_col[1, 0:16] = jnp.zeros((16, D), BF16)

    @pl.when(lat == lats - 1)
    def _():
        halo_row[1] = jnp.zeros((COLS, D), BF16)
        halo_col[0, 80:96] = jnp.zeros((16, D), BF16)
        halo_col[1, 80:96] = jnp.zeros((16, D), BF16)

    expand_rows(31, 10)
    for copy in fetched[3:]:
        copy.wait()
    for h in range(4):
        masks[h] = pick((16, 128), lambda r, c: (c >> 5) == h)
    select[...] = pick(
        (256, 256), lambda r, c: (r & 127) == (c >> 7) * 64 + (c & 48)
    )
    ones_bd[...] = pick((256, 256), lambda r, c: (r >> 7) * 64 + (r & 48) == (c >> 5) << 4)
    for r8 in range(8):
        shifts[r8] = pick(
            (64, 208),
            lambda r, c: ((c < 192) & ((c & 63) + 1 - (c >> 6) == r))
            | ((c == 192 + r8) & (r == 0))
            | ((c == 200 + r8) & (r == 63)),
        )
    for dy in range(3):
        edge_shift[dy] = pick(
            (128, 192),
            lambda r, c: c == ((r >> 3) & 1) * 96 + 15 + (r >> 4) * 8 + (r & 7) + dy,
        )
    perm[...] = pick((256, 256), lambda r, c: r == ((c & 15) << 4) + (c >> 4))
    for dy in range(3):
        for dx in range(3):
            dw16[3 * dy + dx] = jnp.broadcast_to(dw_kernel[dy, dx : dx + 1], (16, HID)).astype(BF16)

    spread_bias(bias_in_block, bias_block)
    spread_bias(bias_in_grid, bias_grid)

    to_west.wait()
    to_east.wait()

    @pl.when(lat > 0)
    def _():
        for c in north:
            c.wait_send()
        for c in south:
            c.wait_recv()

    @pl.when(lat < lats - 1)
    def _():
        for c in south:
            c.wait_send()
        for c in north:
            c.wait_recv()

    def store_rows(c, v):
        e_mid[0, :, c : c + 256] = v[0:64]
        e_mid[65, :, c : c + 256] = v[64:128]

    expand(halo_row[...].reshape(2 * COLS, D), gain_conv[...], average[...], w_expand, store_rows)

    def store_cols(c, v):
        e_edge[:, c : c + 256] = v

    expand(halo_col[...].reshape(192, D), gain_conv[...], average[...], w_expand, store_cols)
    for c in range(0, HID, 256):
        total = jnp.zeros((8, 16, 256), F32)
        for dy in range(3):
            moved = dot(edge_shift[dy], e_edge[:, c : c + 256]).reshape(8, 16, 256)
            west_east = [
                jnp.broadcast_to(dw_kernel[dy, dx : dx + 1, c : c + 256], (8, 256)) for dx in (0, 2)
            ]
            total = total + moved * jnp.concatenate(west_east, axis=0)[None]
        edge_sum[:, :, c : c + 256] = total.astype(BF16)

    def conv_band(band):
        first = band * 8

        def row(r, carry):
            for c in range(0, HID, 256):
                parts = []
                e = [e_mid[first + r + dy, :, c : c + 256] for dy in range(3)]
                for dx in range(3):
                    acc = None
                    for dy in range(3):
                        w = dw16[3 * dy + dx, :, c : c + 256]
                        w = jnp.concatenate([w] * 4, axis=0)
                        term = e[dy] * w
                        acc = term if acc is None else acc + term
                    parts.append(acc)
                parts.append(edge_sum[band, :, c : c + 256])
                total = dot(shifts[r], jnp.concatenate(parts, axis=0))
                conv[pl.ds(r * 64, 64), c : c + 256] = gelu(total.astype(BF16))
            return carry

        lax.fori_loop(0, 8, row, 0, unroll=4)

    def pieces(x):
        return jnp.concatenate(
            [x[64 * b + 8 * a : 64 * b + 8 * a + 8] for a in range(8) for b in range(8)], axis=0
        )

    def send(phase, half):
        def one(i, carry):
            pltpu.make_async_remote_copy(
                src_ref=blocked.at[
                    half, phase * 8 + i // 4, pl.ds(pl.multiple_of(lax.rem(i, 4) * 16, 16), 16), :
                ],
                dst_ref=received.at[phase, lat, half, place],
                send_sem=send_sem.at[phase],
                recv_sem=recv_sem.at[phase],
                device_id=partner(i),
                device_id_type=MESH,
            ).start()
            return carry

        lax.fori_loop(0, 32, one, 0, unroll=True)

    def send_back(phase):
        def one(i, carry):
            pltpu.make_async_remote_copy(
                src_ref=outgoing.at[phase, i // 8, :, lax.rem(i, 8)],
                dst_ref=out.at[
                    :, phase * 8 + my_row, pl.ds(pl.multiple_of(my_col * 16, 16), 16), :
                ],
                send_sem=back_send.at[phase],
                recv_sem=back_recv.at[phase],
                device_id=partner(i),
                device_id_type=MESH,
            ).start()
            return carry

        lax.fori_loop(0, 32, one, 0, unroll=True)

    def conv_and_block(phase):
        def half(i, carry):
            band = i * 4 + phase
            first = band * 8

            @pl.when((phase > 0) & (band < 7))
            def _():
                expand_rows(first + 1, 8)

            @pl.when(band == 7)
            def _():
                expand_rows(first + 1, 7)

            conv_band(band)
            x = tokens[pl.ds(first, 8)].reshape(512, D).astype(F32)
            x = pieces(x + dot(conv[0:512, :], w_project[...])).astype(BF16)
            mixed[0:512, :] = x
            result = attend(
                mixed.at[0:512], gain_block, average, qkv_block, bias_block, out_block, masks, select,
                ones_bd, qkv.at[0:512], att.at[0:512],
            )
            blocked[i, pl.ds(phase * 8, 8)] = (
                pieces(result + x.astype(F32)).astype(BF16).reshape(8, 64, D)
            )
            send(phase, i)
            return carry

        lax.fori_loop(0, 2, half, 0)

    def grid(phase):
        for q in range(4):
            x = received[phase, q].reshape(256, D)
            y = dot(perm[...], x).astype(BF16)
            for p in range(16):
                mixed[64 * p + 16 * q : 64 * p + 16 * q + 16] = y[16 * p : 16 * p + 16]
        result = attend(
            mixed, gain_grid, average, qkv_grid, bias_grid, out_grid, masks, select, ones_bd, qkv, att
        )
        done = (result + mixed[...].astype(F32)).astype(BF16)
        for q in range(4):
            x = jnp.concatenate(
                [done[64 * p + 16 * q : 64 * p + 16 * q + 16] for p in range(16)], axis=0
            )
            outgoing[phase, q] = dot(perm[...], x).astype(BF16).reshape(2, 8, 16, D)

    def wait_all(ref, sem):
        pltpu.make_async_copy(ref, ref, sem).wait()

    def step(phase, carry):
        @pl.when(phase < PHASES)
        def _():
            conv_and_block(phase)

        @pl.when(phase > 0)
        def _():
            wait_all(received.at[phase - 1], recv_sem.at[phase - 1])
            grid(phase - 1)
            send_back(phase - 1)

        return carry

    lax.fori_loop(0, PHASES + 1, step, 0)

    def finish(phase, carry):
        wait_all(received.at[phase], send_sem.at[phase])
        wait_all(received.at[phase], back_send.at[phase])
        wait_all(received.at[phase], back_recv.at[phase])
        return carry

    lax.fori_loop(0, PHASES, finish, 0)


def copy_kernel(source, target, held, sem_in, sem_out):
    parts = [pl.ds(8 * i, 8) for i in range(8)]
    loads = [
        pltpu.make_async_copy(source.at[p], held.at[p], sem_in.at[i]) for i, p in enumerate(parts)
    ]
    stores = [
        pltpu.make_async_copy(held.at[p], target.at[p], sem_out.at[i]) for i, p in enumerate(parts)
    ]
    for load in loads:
        load.start()
    for load, store in zip(loads, stores):
        load.wait()
        store.start()
    for store in stores:
        store.wait()


def shards(
    tokens,
    gain_conv,
    w_expand,
    dw_kernel,
    w_project,
    gain_block,
    qkv_block,
    bias_block,
    out_block,
    gain_grid,
    qkv_grid,
    bias_grid,
    out_grid,
):
    operands = [
        tokens,
        gain_conv.reshape(1, D),
        w_expand,
        dw_kernel,
        w_project,
        gain_block.reshape(1, D),
        qkv_block,
        bias_block,
        out_block,
        gain_grid.reshape(1, D),
        qkv_grid,
        bias_grid,
        out_grid,
    ]
    result = pl.pallas_call(
        kernel,
        out_shape=jax.ShapeDtypeStruct((2, 32, COLS, D), BF16),
        in_specs=[pl.BlockSpec(memory_space=pl.ANY)] * len(operands),
        out_specs=pl.BlockSpec(memory_space=pl.ANY),
        scratch_shapes=[
            pltpu.VMEM((66, COLS, HID), BF16),
            pltpu.VMEM((192, HID), BF16),
            pltpu.VMEM((2, COLS, D), BF16),
            pltpu.VMEM((2, 96, D), BF16),
            pltpu.VMEM((2, 64, D), BF16),
            pltpu.VMEM((8, 16, HID), BF16),
            pltpu.VMEM((9, 16, HID), BF16),
            pltpu.VMEM((64, 512), F32),
            pltpu.VMEM((64, 512), F32),
            pltpu.VMEM((D, D), BF16),
            pltpu.VMEM((4, 16, 128), BF16),
            pltpu.VMEM((256, 256), BF16),
            pltpu.VMEM((256, 256), BF16),
            pltpu.VMEM((8, 64, 208), BF16),
            pltpu.VMEM((3, 128, 192), BF16),
            pltpu.VMEM((256, 256), BF16),
            pltpu.VMEM((512, HID), BF16),
            pltpu.VMEM((1024, D), BF16),
            pltpu.VMEM((1024, 3 * D), BF16),
            pltpu.VMEM((1024, D), BF16),
            pltpu.VMEM((2, 32, COLS, D), BF16),
            pltpu.VMEM((PHASES, 4, 2, 8, 16, D), BF16),
            pltpu.VMEM((PHASES, 4, 2, 8, 16, D), BF16),
            pltpu.SemaphoreType.DMA((8,)),
            pltpu.SemaphoreType.DMA((8,)),
            pltpu.SemaphoreType.DMA((PHASES,)),
            pltpu.SemaphoreType.DMA((PHASES,)),
            pltpu.SemaphoreType.DMA((PHASES,)),
            pltpu.SemaphoreType.DMA((PHASES,)),
            *[pltpu.VMEM(a.shape, a.dtype) for a in operands],
            pltpu.SemaphoreType.DMA((len(operands),)),
        ],
        compiler_params=pltpu.CompilerParams(
            collective_id=0, has_side_effects=True, vmem_limit_bytes=60 * 1024 * 1024
        ),
    )(*operands)
    result = result.reshape(ROWS, COLS, D)
    return pl.pallas_call(
        copy_kernel,
        out_shape=jax.ShapeDtypeStruct(result.shape, result.dtype),
        in_specs=[pl.BlockSpec(memory_space=pl.ANY)],
        out_specs=pl.BlockSpec(memory_space=pl.ANY),
        scratch_shapes=[
            pltpu.VMEM(result.shape, result.dtype),
            pltpu.SemaphoreType.DMA((8,)),
            pltpu.SemaphoreType.DMA((8,)),
        ],
    )(result)


def solution(mesh):
    placed = (P("lat", "lon", None), P(), P(), P(), P(), P(), P(), P(), P(), P(), P(), P(), P())
    return jax.shard_map(
        shards, mesh=mesh, in_specs=placed, out_specs=P("lat", "lon", None), check_vma=False
    )
```

```python
import jax
import jax.numpy as jnp
from jax import lax
from jax.experimental import pallas as pl
from jax.experimental.pallas import tpu as pltpu
from jax.sharding import PartitionSpec as P

MESH = pl.DeviceIdType.MESH
BF16 = jnp.bfloat16
F32 = jnp.float32
ROWS, COLS, D, HID, HEADS = 64, 64, 256, 1024, 8
PHASES = 4
EARLY = 5
BATCH = 16
LOG2E = 1.4426950408889634


def dot(a, b):
    return jnp.dot(a, b, preferred_element_type=F32)


def dot_nt(a, b):
    return lax.dot_general(a, b, (((1,), (1,)), ((), ())), preferred_element_type=F32)


def exp2(x):
    return jnp.exp2(x)


def gelu(x):
    half = x * BF16(0.5)
    inner = x * (BF16(0.7978845608) + BF16(0.035677408) * (x * x))
    return half + half * jnp.tanh(inner)


def norm(x, gain, average):
    xf = x.astype(F32)
    d = xf - jnp.mean(xf, axis=-1, keepdims=True)
    var = dot((d * d).astype(BF16), average)
    return (d * lax.rsqrt(var + 1e-05) * gain).astype(BF16)


def expand(x, gain, average, w_expand, store):
    n = norm(x, gain, average)
    for c in range(0, HID, 256):
        store(c, gelu(dot(n, w_expand[:, c : c + 256]).astype(BF16)))


def blocks(m, masks):
    return jnp.concatenate(
        [m[16 * i : 16 * i + 16] * masks[h] for i in range(4) for h in range(4)], axis=0
    )


def head_top(pairs, select):
    wide = [jnp.maximum(x, pltpu.roll(x, 64, 1)) for x in pairs]
    lane = lax.broadcasted_iota(jnp.int32, wide[0].shape, 1)
    top = jnp.where(lane < 64, wide[0], wide[1])
    for shift in (8, 4, 2, 1):
        top = jnp.maximum(top, pltpu.roll(top, 128 - shift, 1))
    high = top.astype(BF16)
    low = (top - high.astype(F32)).astype(BF16)
    return dot(jnp.concatenate([high, low], axis=1), select[...])


def attend(x_ref, gain, average, w_qkv, bias, w_out, masks, select, ones_bd, qkv, mixed):
    n = norm(x_ref[...], gain[...], average[...])
    scale = LOG2E / 32**0.5
    qkv[:, 0:256] = (dot(n, w_qkv[:, 0:256]) * scale).astype(BF16)
    qkv[:, 256:512] = dot(n, w_qkv[:, 256:512]).astype(BF16)
    qkv[:, 512:768] = dot(n, w_qkv[:, 512:768]).astype(BF16)
    size = min(BATCH * 64, x_ref.shape[0])

    def batch(first):
        rows = [pl.ds(first + i * 64, 64) for i in range(size // 64)]
        scores = [
            jnp.concatenate(
                [
                    dot_nt(
                        qkv[r, 128 * u : 128 * u + 128],
                        blocks(qkv[r, 256 + 128 * u : 384 + 128 * u], masks),
                    )
                    + bias[:, 256 * u : 256 * u + 256]
                    for r in rows
                ],
                axis=0,
            )
            for u in range(2)
        ]
        top = head_top([jnp.maximum(s[:, 0:128], s[:, 128:256]) for s in scores], select)
        weights, sums = [], []
        for u, s in enumerate(scores):
            t = top[:, 128 * u : 128 * u + 128]
            a, b = exp2(s[:, 0:128] - t), exp2(s[:, 128:256] - t)
            sums.append((a + b).astype(BF16))
            weights.append(jnp.concatenate([a.astype(BF16), b.astype(BF16)], axis=1))
        total = dot(jnp.concatenate(sums, axis=1), ones_bd[...])
        values = jnp.concatenate(
            [
                jnp.concatenate(
                    [
                        dot(
                            w[64 * k : 64 * k + 64],
                            blocks(qkv[r, 512 + 128 * u : 640 + 128 * u], masks),
                        )
                        for k, r in enumerate(rows)
                    ],
                    axis=0,
                )
                for u, w in enumerate(weights)
            ],
            axis=1,
        )
        mixed[pl.ds(first, size), :] = (values / total).astype(BF16)

    for first in range(0, x_ref.shape[0], size):
        batch(first)
    return dot(mixed[...], w_out[...])


def spread_bias(source, target):
    lane = lax.broadcasted_iota(jnp.int32, (64, 128), 1)
    for u in range(2):
        twice = []
        for h in range(4):
            x = source[4 * u + h] * LOG2E
            twice.append(jnp.concatenate([x, x], axis=1))
        for tile in range(2):
            acc = twice[0]
            for k in range(2):
                for h in range(4):
                    at, to = (2 * tile + k) * 16, k * 64 + h * 16
                    moved = pltpu.roll(twice[h], (to - at) % 128, 1)
                    acc = jnp.where((lane >> 4) == to // 16, moved, acc)
            target[:, 256 * u + 128 * tile : 256 * u + 128 * tile + 128] = acc


def pick(shape, hit):
    row = lax.broadcasted_iota(jnp.int32, shape, 0)
    col = lax.broadcasted_iota(jnp.int32, shape, 1)
    return jnp.where(hit(row, col), 1.0, 0.0).astype(BF16)


def kernel(
    tokens_hbm,
    gain_conv_hbm,
    w_expand_hbm,
    dw_kernel_hbm,
    w_project_hbm,
    gain_block_hbm,
    qkv_block_hbm,
    bias_in_block_hbm,
    out_block_hbm,
    gain_grid_hbm,
    qkv_grid_hbm,
    bias_in_grid_hbm,
    out_grid_hbm,
    out,
    e_mid,
    e_edge,
    halo_row,
    halo_col,
    edge,
    edge_sum,
    dw16,
    bias_block,
    bias_grid,
    average,
    masks,
    select,
    ones_bd,
    shifts,
    edge_shift,
    perm,
    conv,
    mixed,
    qkv,
    att,
    blocked,
    received,
    outgoing,
    halo_send,
    halo_recv,
    send_sem,
    recv_sem,
    back_send,
    back_recv,
    tokens,
    gain_conv,
    w_expand,
    dw_kernel,
    w_project,
    gain_block,
    qkv_block,
    bias_in_block,
    out_block,
    gain_grid,
    qkv_grid,
    bias_in_grid,
    out_grid,
    fetch_sem,
):
    lat = lax.axis_index("lat")
    lon = lax.axis_index("lon")
    lats = lax.axis_size("lat")
    lons = lax.axis_size("lon")
    kind = lax.rem(lon, 4)
    place = lon // 4
    far = 3 - kind
    mine = lat * 8 + place
    my_row, my_col = mine // 4, lax.rem(mine, 4)
    west = lax.rem(lon + lons - 1, lons)
    east = lax.rem(lon + 1, lons)

    def partner(i):
        return {"lat": i // 8, "lon": lax.rem(i, 8) * 4 + far}

    fetched = [
        pltpu.make_async_copy(src, dst, fetch_sem.at[i])
        for i, (src, dst) in enumerate(
            [
                (tokens_hbm, tokens),
                (w_expand_hbm, w_expand),
                (gain_conv_hbm, gain_conv),
                (dw_kernel_hbm, dw_kernel),
                (bias_in_block_hbm, bias_in_block),
                (bias_in_grid_hbm, bias_in_grid),
                (w_project_hbm, w_project),
                (gain_block_hbm, gain_block),
                (qkv_block_hbm, qkv_block),
                (out_block_hbm, out_block),
                (gain_grid_hbm, gain_grid),
                (qkv_grid_hbm, qkv_grid),
                (out_grid_hbm, out_grid),
            ]
        )
    ]
    for copy in fetched:
        copy.start()

    barrier = pltpu.get_barrier_semaphore()

    def greet(i, carry):
        pl.semaphore_signal(barrier, inc=1, device_id=partner(i), device_id_type=MESH)
        return carry

    lax.fori_loop(0, 32, greet, 0, unroll=True)
    for side in (west, east):
        pl.semaphore_signal(
            barrier, inc=1, device_id={"lat": lat, "lon": side}, device_id_type=MESH
        )

    @pl.when(lat > 0)
    def _():
        for side in (lon, west, east):
            pl.semaphore_signal(
                barrier, inc=1, device_id={"lat": lat - 1, "lon": side}, device_id_type=MESH
            )

    @pl.when(lat < lats - 1)
    def _():
        for side in (lon, west, east):
            pl.semaphore_signal(
                barrier, inc=1, device_id={"lat": lat + 1, "lon": side}, device_id_type=MESH
            )

    average[...] = jnp.full((D, D), 1.0 / D, BF16)
    for copy in fetched[:3]:
        copy.wait()
    for side in range(2):
        first = pick((16, 256), lambda r, c: c == r * 16 + 15 * side)
        for q in range(4):
            x = tokens[16 * q : 16 * q + 16, 48 * side : 48 * side + 16].reshape(256, D)
            edge[side, 16 * q : 16 * q + 16] = dot(first, x).astype(BF16)

    def expand_rows(first, count):
        def store(c, v):
            e_mid[pl.ds(first + 1, count), :, c : c + 256] = v.reshape(count, COLS, 256)

        x = tokens[pl.ds(first, count)].reshape(count * COLS, D)
        expand(x, gain_conv[...], average[...], w_expand, store)

    def expand_band(band, carry):
        expand_rows(band * 8, 8)
        return carry

    lax.fori_loop(0, EARLY, expand_band, 0)

    inner = jnp.minimum(lat, 1) + jnp.minimum(lats - 1 - lat, 1)
    pl.semaphore_wait(barrier, 34 + 3 * inner)

    def halo(slot, src, dst, to_lat, to_lon):
        return pltpu.make_async_remote_copy(
            src_ref=src,
            dst_ref=dst,
            send_sem=halo_send.at[slot],
            recv_sem=halo_recv.at[slot],
            device_id={"lat": to_lat, "lon": to_lon},
            device_id_type=MESH,
        )

    to_west = halo(0, edge.at[0], halo_col.at[1, pl.ds(16, 64)], lat, west)
    to_east = halo(1, edge.at[1], halo_col.at[0, pl.ds(16, 64)], lat, east)
    north = [
        halo(2, tokens.at[0], halo_row.at[1], lat - 1, lon),
        halo(3, edge.at[0, pl.ds(0, 16)], halo_col.at[1, pl.ds(80, 16)], lat - 1, west),
        halo(4, edge.at[1, pl.ds(0, 16)], halo_col.at[0, pl.ds(80, 16)], lat - 1, east),
    ]
    south = [
        halo(5, tokens.at[ROWS - 1], halo_row.at[0], lat + 1, lon),
        halo(6, edge.at[0, pl.ds(48, 16)], halo_col.at[1, pl.ds(0, 16)], lat + 1, west),
        halo(7, edge.at[1, pl.ds(48, 16)], halo_col.at[0, pl.ds(0, 16)], lat + 1, east),
    ]
    to_west.start()
    to_east.start()

    @pl.when(lat > 0)
    def _():
        for c in north:
            c.start()

    @pl.when(lat < lats - 1)
    def _():
        for c in south:
            c.start()

    @pl.when(lat == 0)
    def _():
        halo_row[0] = jnp.zeros((COLS, D), BF16)
        halo_col[0, 0:16] = jnp.zeros((16, D), BF16)
        halo_col[1, 0:16] = jnp.zeros((16, D), BF16)

    @pl.when(lat == lats - 1)
    def _():
        halo_row[1] = jnp.zeros((COLS, D), BF16)
        halo_col[0, 80:96] = jnp.zeros((16, D), BF16)
        halo_col[1, 80:96] = jnp.zeros((16, D), BF16)

    lax.fori_loop(EARLY, 8, expand_band, 0)
    for copy in fetched[3:]:
        copy.wait()
    for h in range(4):
        masks[h] = pick((16, 128), lambda r, c: (c >> 5) == h)
    select[...] = pick(
        (256, 256), lambda r, c: (r & 127) == (c >> 7) * 64 + (c & 48)
    )
    ones_bd[...] = pick((256, 256), lambda r, c: (r >> 7) * 64 + (r & 48) == (c >> 5) << 4)
    for r8 in range(8):
        shifts[r8] = pick(
            (64, 208),
            lambda r, c: ((c < 192) & ((c & 63) + 1 - (c >> 6) == r))
            | ((c == 192 + r8) & (r == 0))
            | ((c == 200 + r8) & (r == 63)),
        )
    for dy in range(3):
        edge_shift[dy] = pick(
            (128, 192),
            lambda r, c: c == ((r >> 3) & 1) * 96 + 15 + (r >> 4) * 8 + (r & 7) + dy,
        )
    perm[...] = pick((256, 256), lambda r, c: r == ((c & 15) << 4) + (c >> 4))
    for dy in range(3):
        for dx in range(3):
            dw16[3 * dy + dx] = jnp.broadcast_to(dw_kernel[dy, dx : dx + 1], (16, HID)).astype(BF16)

    spread_bias(bias_in_block, bias_block)
    spread_bias(bias_in_grid, bias_grid)

    to_west.wait()
    to_east.wait()

    @pl.when(lat > 0)
    def _():
        for c in north:
            c.wait_send()
        for c in south:
            c.wait_recv()

    @pl.when(lat < lats - 1)
    def _():
        for c in south:
            c.wait_send()
        for c in north:
            c.wait_recv()

    def store_rows(c, v):
        e_mid[0, :, c : c + 256] = v[0:64]
        e_mid[65, :, c : c + 256] = v[64:128]

    expand(halo_row[...].reshape(2 * COLS, D), gain_conv[...], average[...], w_expand, store_rows)

    def store_cols(c, v):
        e_edge[:, c : c + 256] = v

    expand(halo_col[...].reshape(192, D), gain_conv[...], average[...], w_expand, store_cols)
    for c in range(0, HID, 256):
        total = jnp.zeros((8, 16, 256), F32)
        for dy in range(3):
            moved = dot(edge_shift[dy], e_edge[:, c : c + 256]).reshape(8, 16, 256)
            west_east = [
                jnp.broadcast_to(dw_kernel[dy, dx : dx + 1, c : c + 256], (8, 256)) for dx in (0, 2)
            ]
            total = total + moved * jnp.concatenate(west_east, axis=0)[None]
        edge_sum[:, :, c : c + 256] = total.astype(BF16)

    def conv_band(band):
        first = band * 8

        def row(r, carry):
            for c in range(0, HID, 256):
                parts = []
                e = [e_mid[first + r + dy, :, c : c + 256] for dy in range(3)]
                for dx in range(3):
                    acc = None
                    for dy in range(3):
                        w = dw16[3 * dy + dx, :, c : c + 256]
                        w = jnp.concatenate([w] * 4, axis=0)
                        term = e[dy] * w
                        acc = term if acc is None else acc + term
                    parts.append(acc)
                parts.append(edge_sum[band, :, c : c + 256])
                total = dot(shifts[r], jnp.concatenate(parts, axis=0))
                conv[pl.ds(r * 64, 64), c : c + 256] = gelu(total.astype(BF16))
            return carry

        lax.fori_loop(0, 8, row, 0, unroll=4)

    def pieces(x):
        return jnp.concatenate(
            [x[64 * b + 8 * a : 64 * b + 8 * a + 8] for a in range(8) for b in range(8)], axis=0
        )

    def send(phase, half):
        def one(i, carry):
            pltpu.make_async_remote_copy(
                src_ref=blocked.at[
                    half, phase * 8 + i // 4, pl.ds(pl.multiple_of(lax.rem(i, 4) * 16, 16), 16), :
                ],
                dst_ref=received.at[phase, lat, half, place],
                send_sem=send_sem.at[phase],
                recv_sem=recv_sem.at[phase],
                device_id=partner(i),
                device_id_type=MESH,
            ).start()
            return carry

        lax.fori_loop(0, 32, one, 0, unroll=True)

    def send_back(phase):
        def one(i, carry):
            pltpu.make_async_remote_copy(
                src_ref=outgoing.at[phase, i // 8, :, lax.rem(i, 8)],
                dst_ref=out.at[
                    :, phase * 8 + my_row, pl.ds(pl.multiple_of(my_col * 16, 16), 16), :
                ],
                send_sem=back_send.at[phase],
                recv_sem=back_recv.at[phase],
                device_id=partner(i),
                device_id_type=MESH,
            ).start()
            return carry

        lax.fori_loop(0, 32, one, 0, unroll=True)

    def conv_and_block(phase):
        def half(i, carry):
            band = i * 4 + phase
            first = band * 8

            conv_band(band)
            x = tokens[pl.ds(first, 8)].reshape(512, D).astype(F32)
            x = pieces(x + dot(conv[0:512, :], w_project[...])).astype(BF16)
            mixed[0:512, :] = x
            result = attend(
                mixed.at[0:512], gain_block, average, qkv_block, bias_block, out_block, masks, select,
                ones_bd, qkv.at[0:512], att.at[0:512],
            )
            blocked[i, pl.ds(phase * 8, 8)] = (
                pieces(result + x.astype(F32)).astype(BF16).reshape(8, 64, D)
            )
            send(phase, i)
            return carry

        lax.fori_loop(0, 2, half, 0)

    def grid(phase):
        for q in range(4):
            x = received[phase, q].reshape(256, D)
            y = dot(perm[...], x).astype(BF16)
            for p in range(16):
                mixed[64 * p + 16 * q : 64 * p + 16 * q + 16] = y[16 * p : 16 * p + 16]
        result = attend(
            mixed, gain_grid, average, qkv_grid, bias_grid, out_grid, masks, select, ones_bd, qkv, att
        )
        done = (result + mixed[...].astype(F32)).astype(BF16)
        for q in range(4):
            x = jnp.concatenate(
                [done[64 * p + 16 * q : 64 * p + 16 * q + 16] for p in range(16)], axis=0
            )
            outgoing[phase, q] = dot(perm[...], x).astype(BF16).reshape(2, 8, 16, D)

    def wait_all(ref, sem):
        pltpu.make_async_copy(ref, ref, sem).wait()

    def step(phase, carry):
        @pl.when(phase < PHASES)
        def _():
            conv_and_block(phase)

        @pl.when(phase > 0)
        def _():
            wait_all(received.at[phase - 1], recv_sem.at[phase - 1])
            grid(phase - 1)
            send_back(phase - 1)

        return carry

    lax.fori_loop(0, PHASES + 1, step, 0)

    def finish(phase, carry):
        wait_all(received.at[phase], send_sem.at[phase])
        wait_all(received.at[phase], back_send.at[phase])
        wait_all(received.at[phase], back_recv.at[phase])
        return carry

    lax.fori_loop(0, PHASES, finish, 0)


def copy_kernel(source, target, held, sem_in, sem_out):
    parts = [pl.ds(8 * i, 8) for i in range(8)]
    loads = [
        pltpu.make_async_copy(source.at[p], held.at[p], sem_in.at[i]) for i, p in enumerate(parts)
    ]
    stores = [
        pltpu.make_async_copy(held.at[p], target.at[p], sem_out.at[i]) for i, p in enumerate(parts)
    ]
    for load in loads:
        load.start()
    for load, store in zip(loads, stores):
        load.wait()
        store.start()
    for store in stores:
        store.wait()


def shards(
    tokens,
    gain_conv,
    w_expand,
    dw_kernel,
    w_project,
    gain_block,
    qkv_block,
    bias_block,
    out_block,
    gain_grid,
    qkv_grid,
    bias_grid,
    out_grid,
):
    operands = [
        tokens,
        gain_conv.reshape(1, D),
        w_expand,
        dw_kernel,
        w_project,
        gain_block.reshape(1, D),
        qkv_block,
        bias_block,
        out_block,
        gain_grid.reshape(1, D),
        qkv_grid,
        bias_grid,
        out_grid,
    ]
    result = pl.pallas_call(
        kernel,
        out_shape=jax.ShapeDtypeStruct((2, 32, COLS, D), BF16),
        in_specs=[pl.BlockSpec(memory_space=pl.ANY)] * len(operands),
        out_specs=pl.BlockSpec(memory_space=pl.ANY),
        scratch_shapes=[
            pltpu.VMEM((66, COLS, HID), BF16),
            pltpu.VMEM((192, HID), BF16),
            pltpu.VMEM((2, COLS, D), BF16),
            pltpu.VMEM((2, 96, D), BF16),
            pltpu.VMEM((2, 64, D), BF16),
            pltpu.VMEM((8, 16, HID), BF16),
            pltpu.VMEM((9, 16, HID), BF16),
            pltpu.VMEM((64, 512), F32),
            pltpu.VMEM((64, 512), F32),
            pltpu.VMEM((D, D), BF16),
            pltpu.VMEM((4, 16, 128), BF16),
            pltpu.VMEM((256, 256), BF16),
            pltpu.VMEM((256, 256), BF16),
            pltpu.VMEM((8, 64, 208), BF16),
            pltpu.VMEM((3, 128, 192), BF16),
            pltpu.VMEM((256, 256), BF16),
            pltpu.VMEM((512, HID), BF16),
            pltpu.VMEM((1024, D), BF16),
            pltpu.VMEM((1024, 3 * D), BF16),
            pltpu.VMEM((1024, D), BF16),
            pltpu.VMEM((2, 32, COLS, D), BF16),
            pltpu.VMEM((PHASES, 4, 2, 8, 16, D), BF16),
            pltpu.VMEM((PHASES, 4, 2, 8, 16, D), BF16),
            pltpu.SemaphoreType.DMA((8,)),
            pltpu.SemaphoreType.DMA((8,)),
            pltpu.SemaphoreType.DMA((PHASES,)),
            pltpu.SemaphoreType.DMA((PHASES,)),
            pltpu.SemaphoreType.DMA((PHASES,)),
            pltpu.SemaphoreType.DMA((PHASES,)),
            *[pltpu.VMEM(a.shape, a.dtype) for a in operands],
            pltpu.SemaphoreType.DMA((len(operands),)),
        ],
        compiler_params=pltpu.CompilerParams(
            collective_id=0, has_side_effects=True, vmem_limit_bytes=60 * 1024 * 1024
        ),
    )(*operands)
    result = result.reshape(ROWS, COLS, D)
    return pl.pallas_call(
        copy_kernel,
        out_shape=jax.ShapeDtypeStruct(result.shape, result.dtype),
        in_specs=[pl.BlockSpec(memory_space=pl.ANY)],
        out_specs=pl.BlockSpec(memory_space=pl.ANY),
        scratch_shapes=[
            pltpu.VMEM(result.shape, result.dtype),
            pltpu.SemaphoreType.DMA((8,)),
            pltpu.SemaphoreType.DMA((8,)),
        ],
    )(result)


def solution(mesh):
    placed = (P("lat", "lon", None), P(), P(), P(), P(), P(), P(), P(), P(), P(), P(), P(), P())
    return jax.shard_map(
        shards, mesh=mesh, in_specs=placed, out_specs=P("lat", "lon", None), check_vma=False
    )
```

```python
import jax
import jax.numpy as jnp
from jax import lax
from jax.experimental import pallas as pl
from jax.experimental.pallas import tpu as pltpu
from jax.sharding import PartitionSpec as P

MESH = pl.DeviceIdType.MESH
BF16 = jnp.bfloat16
F32 = jnp.float32
ROWS, COLS, D, HID, HEADS = 64, 64, 256, 1024, 8
PHASES = 4
BATCH = 16
LOG2E = 1.4426950408889634


def dot(a, b):
    return jnp.dot(a, b, preferred_element_type=F32)


def dot_nt(a, b):
    return lax.dot_general(a, b, (((1,), (1,)), ((), ())), preferred_element_type=F32)


def exp2(x):
    return jnp.exp2(x)


def gelu(x):
    half = x * BF16(0.5)
    inner = x * (BF16(0.7978845608) + BF16(0.035677408) * (x * x))
    return half + half * jnp.tanh(inner)


def norm(x, gain, average):
    xf = x.astype(F32)
    d = xf - jnp.mean(xf, axis=-1, keepdims=True)
    var = dot((d * d).astype(BF16), average)
    return (d * lax.rsqrt(var + 1e-05) * gain).astype(BF16)


def expand(x, gain, average, w_expand, store):
    n = norm(x, gain, average)
    for c in range(0, HID, 256):
        store(c, gelu(dot(n, w_expand[:, c : c + 256]).astype(BF16)))


def blocks(m, masks):
    return jnp.concatenate(
        [m[16 * i : 16 * i + 16] * masks[h] for i in range(4) for h in range(4)], axis=0
    )


def head_top(pairs, select):
    lane = lax.broadcasted_iota(jnp.int32, pairs[0].shape, 1)
    here = jnp.where(lane < 64, pairs[0], pairs[1])
    there = jnp.where(lane < 64, pairs[1], pairs[0])
    top = jnp.maximum(here, pltpu.roll(there, 64, 1))
    for shift in (8, 4, 2, 1):
        top = jnp.maximum(top, pltpu.roll(top, 128 - shift, 1))
    high = top.astype(BF16)
    low = (top - high.astype(F32)).astype(BF16)
    return dot(jnp.concatenate([high, low], axis=1), select[...])


def attend(x_ref, gain, average, w_qkv, bias, w_out, masks, select, ones_bd, qkv, mixed):
    n = norm(x_ref[...], gain[...], average[...])
    scale = LOG2E / 32**0.5
    qkv[:, 0:256] = (dot(n, w_qkv[:, 0:256]) * scale).astype(BF16)
    qkv[:, 256:512] = dot(n, w_qkv[:, 256:512]).astype(BF16)
    qkv[:, 512:768] = dot(n, w_qkv[:, 512:768]).astype(BF16)
    size = min(BATCH * 64, x_ref.shape[0])

    def batch(first):
        rows = [pl.ds(first + i * 64, 64) for i in range(size // 64)]
        scores = [
            jnp.concatenate(
                [
                    dot_nt(
                        qkv[r, 128 * u : 128 * u + 128],
                        blocks(qkv[r, 256 + 128 * u : 384 + 128 * u], masks),
                    )
                    + bias[:, 256 * u : 256 * u + 256]
                    for r in rows
                ],
                axis=0,
            )
            for u in range(2)
        ]
        top = head_top([jnp.maximum(s[:, 0:128], s[:, 128:256]) for s in scores], select)
        weights, sums = [], []
        for u, s in enumerate(scores):
            t = top[:, 128 * u : 128 * u + 128]
            a, b = exp2(s[:, 0:128] - t), exp2(s[:, 128:256] - t)
            sums.append((a + b).astype(BF16))
            weights.append(jnp.concatenate([a.astype(BF16), b.astype(BF16)], axis=1))
        total = dot(jnp.concatenate(sums, axis=1), ones_bd[...])
        values = jnp.concatenate(
            [
                jnp.concatenate(
                    [
                        dot(
                            w[64 * k : 64 * k + 64],
                            blocks(qkv[r, 512 + 128 * u : 640 + 128 * u], masks),
                        )
                        for k, r in enumerate(rows)
                    ],
                    axis=0,
                )
                for u, w in enumerate(weights)
            ],
            axis=1,
        )
        mixed[pl.ds(first, size), :] = (values / total).astype(BF16)

    for first in range(0, x_ref.shape[0], size):
        batch(first)
    return dot(mixed[...], w_out[...])


def spread_bias(source, target):
    lane = lax.broadcasted_iota(jnp.int32, (64, 128), 1)
    for u in range(2):
        twice = []
        for h in range(4):
            x = source[4 * u + h] * LOG2E
            twice.append(jnp.concatenate([x, x], axis=1))
        for tile in range(2):
            acc = twice[0]
            for k in range(2):
                for h in range(4):
                    at, to = (2 * tile + k) * 16, k * 64 + h * 16
                    moved = pltpu.roll(twice[h], (to - at) % 128, 1)
                    acc = jnp.where((lane >> 4) == to // 16, moved, acc)
            target[:, 256 * u + 128 * tile : 256 * u + 128 * tile + 128] = acc


def pick(shape, hit):
    row = lax.broadcasted_iota(jnp.int32, shape, 0)
    col = lax.broadcasted_iota(jnp.int32, shape, 1)
    return jnp.where(hit(row, col), 1.0, 0.0).astype(BF16)


def kernel(
    tokens_hbm,
    gain_conv_hbm,
    w_expand_hbm,
    dw_kernel_hbm,
    w_project_hbm,
    gain_block_hbm,
    qkv_block_hbm,
    bias_in_block_hbm,
    out_block_hbm,
    gain_grid_hbm,
    qkv_grid_hbm,
    bias_in_grid_hbm,
    out_grid_hbm,
    out,
    e_mid,
    e_edge,
    halo_row,
    halo_col,
    edge,
    edge_sum,
    dw16,
    bias_block,
    bias_grid,
    average,
    masks,
    select,
    ones_bd,
    shifts,
    edge_shift,
    perm,
    conv,
    mixed,
    qkv,
    att,
    blocked,
    received,
    outgoing,
    halo_send,
    halo_recv,
    send_sem,
    recv_sem,
    back_send,
    back_recv,
    tokens,
    gain_conv,
    w_expand,
    dw_kernel,
    w_project,
    gain_block,
    qkv_block,
    bias_in_block,
    out_block,
    gain_grid,
    qkv_grid,
    bias_in_grid,
    out_grid,
    fetch_sem,
):
    lat = lax.axis_index("lat")
    lon = lax.axis_index("lon")
    lats = lax.axis_size("lat")
    lons = lax.axis_size("lon")
    kind = lax.rem(lon, 4)
    place = lon // 4
    far = 3 - kind
    mine = lat * 8 + place
    my_row, my_col = mine // 4, lax.rem(mine, 4)
    west = lax.rem(lon + lons - 1, lons)
    east = lax.rem(lon + 1, lons)

    def partner(i):
        return {"lat": i // 8, "lon": lax.rem(i, 8) * 4 + far}

    fetched = [
        pltpu.make_async_copy(src, dst, fetch_sem.at[i])
        for i, (src, dst) in enumerate(
            [
                (w_expand_hbm, w_expand),
                (gain_conv_hbm, gain_conv),
                *[
                    (tokens_hbm.at[pl.ds(16 * k, 16)], tokens.at[pl.ds(16 * k, 16)])
                    for k in range(4)
                ],
                (dw_kernel_hbm, dw_kernel),
                (bias_in_block_hbm, bias_in_block),
                (bias_in_grid_hbm, bias_in_grid),
                (w_project_hbm, w_project),
                (gain_block_hbm, gain_block),
                (qkv_block_hbm, qkv_block),
                (out_block_hbm, out_block),
                (gain_grid_hbm, gain_grid),
                (qkv_grid_hbm, qkv_grid),
                (out_grid_hbm, out_grid),
            ]
        )
    ]
    for copy in fetched:
        copy.start()

    barrier = pltpu.get_barrier_semaphore()

    def greet(i, carry):
        pl.semaphore_signal(barrier, inc=1, device_id=partner(i), device_id_type=MESH)
        return carry

    lax.fori_loop(0, 32, greet, 0, unroll=True)
    for side in (west, east):
        pl.semaphore_signal(
            barrier, inc=1, device_id={"lat": lat, "lon": side}, device_id_type=MESH
        )

    @pl.when(lat > 0)
    def _():
        for side in (lon, west, east):
            pl.semaphore_signal(
                barrier, inc=1, device_id={"lat": lat - 1, "lon": side}, device_id_type=MESH
            )

    @pl.when(lat < lats - 1)
    def _():
        for side in (lon, west, east):
            pl.semaphore_signal(
                barrier, inc=1, device_id={"lat": lat + 1, "lon": side}, device_id_type=MESH
            )

    average[...] = jnp.full((D, D), 1.0 / D, BF16)
    def expand_rows(first, count):
        def store(c, v):
            e_mid[pl.ds(first + 1, count), :, c : c + 256] = v.reshape(count, COLS, 256)

        x = tokens[pl.ds(first, count)].reshape(count * COLS, D)
        expand(x, gain_conv[...], average[...], w_expand, store)

    for copy in fetched[:3]:
        copy.wait()
    expand_rows(0, 8)
    for copy in fetched[3:6]:
        copy.wait()
    for side in range(2):
        first = pick((16, 256), lambda r, c: c == r * 16 + 15 * side)
        for q in range(4):
            x = tokens[16 * q : 16 * q + 16, 48 * side : 48 * side + 16].reshape(256, D)
            edge[side, 16 * q : 16 * q + 16] = dot(first, x).astype(BF16)

    inner = jnp.minimum(lat, 1) + jnp.minimum(lats - 1 - lat, 1)
    pl.semaphore_wait(barrier, 34 + 3 * inner)

    def halo(slot, src, dst, to_lat, to_lon):
        return pltpu.make_async_remote_copy(
            src_ref=src,
            dst_ref=dst,
            send_sem=halo_send.at[slot],
            recv_sem=halo_recv.at[slot],
            device_id={"lat": to_lat, "lon": to_lon},
            device_id_type=MESH,
        )

    to_west = halo(0, edge.at[0], halo_col.at[1, pl.ds(16, 64)], lat, west)
    to_east = halo(1, edge.at[1], halo_col.at[0, pl.ds(16, 64)], lat, east)
    north = [
        halo(2, tokens.at[0], halo_row.at[1], lat - 1, lon),
        halo(3, edge.at[0, pl.ds(0, 16)], halo_col.at[1, pl.ds(80, 16)], lat - 1, west),
        halo(4, edge.at[1, pl.ds(0, 16)], halo_col.at[0, pl.ds(80, 16)], lat - 1, east),
    ]
    south = [
        halo(5, tokens.at[ROWS - 1], halo_row.at[0], lat + 1, lon),
        halo(6, edge.at[0, pl.ds(48, 16)], halo_col.at[1, pl.ds(0, 16)], lat + 1, west),
        halo(7, edge.at[1, pl.ds(48, 16)], halo_col.at[0, pl.ds(0, 16)], lat + 1, east),
    ]
    to_west.start()
    to_east.start()

    @pl.when(lat > 0)
    def _():
        for c in north:
            c.start()

    @pl.when(lat < lats - 1)
    def _():
        for c in south:
            c.start()

    @pl.when(lat == 0)
    def _():
        halo_row[0] = jnp.zeros((COLS, D), BF16)
        halo_col[0, 0:16] = jnp.zeros((16, D), BF16)
        halo_col[1, 0:16] = jnp.zeros((16, D), BF16)

    @pl.when(lat == lats - 1)
    def _():
        halo_row[1] = jnp.zeros((COLS, D), BF16)
        halo_col[0, 80:96] = jnp.zeros((16, D), BF16)
        halo_col[1, 80:96] = jnp.zeros((16, D), BF16)

    expand_rows(8, 9)
    expand_rows(31, 9)
    expand_rows(40, 9)
    for copy in fetched[6:]:
        copy.wait()
    for h in range(4):
        masks[h] = pick((16, 128), lambda r, c: (c >> 5) == h)
    select[...] = pick(
        (256, 256), lambda r, c: (r & 127) == (c >> 7) * 64 + (c & 48)
    )
    ones_bd[...] = pick((256, 256), lambda r, c: (r >> 7) * 64 + (r & 48) == (c >> 5) << 4)
    for r8 in range(8):
        shifts[r8] = pick(
            (64, 208),
            lambda r, c: ((c < 192) & ((c & 63) + 1 - (c >> 6) == r))
            | ((c == 192 + r8) & (r == 0))
            | ((c == 200 + r8) & (r == 63)),
        )
    for dy in range(3):
        edge_shift[dy] = pick(
            (128, 192),
            lambda r, c: c == ((r >> 3) & 1) * 96 + 15 + (r >> 4) * 8 + (r & 7) + dy,
        )
    perm[...] = pick((256, 256), lambda r, c: r == ((c & 15) << 4) + (c >> 4))
    for dy in range(3):
        for dx in range(3):
            dw16[3 * dy + dx] = jnp.broadcast_to(dw_kernel[dy, dx : dx + 1], (16, HID)).astype(BF16)

    spread_bias(bias_in_block, bias_block)
    spread_bias(bias_in_grid, bias_grid)

    to_west.wait()
    to_east.wait()

    @pl.when(lat > 0)
    def _():
        for c in north:
            c.wait_send()
        for c in south:
            c.wait_recv()

    @pl.when(lat < lats - 1)
    def _():
        for c in south:
            c.wait_send()
        for c in north:
            c.wait_recv()

    def store_rows(c, v):
        e_mid[0, :, c : c + 256] = v[0:64]
        e_mid[65, :, c : c + 256] = v[64:128]

    expand(halo_row[...].reshape(2 * COLS, D), gain_conv[...], average[...], w_expand, store_rows)

    def store_cols(c, v):
        e_edge[:, c : c + 256] = v

    expand(halo_col[...].reshape(192, D), gain_conv[...], average[...], w_expand, store_cols)
    for c in range(0, HID, 256):
        total = jnp.zeros((8, 16, 256), F32)
        for dy in range(3):
            moved = dot(edge_shift[dy], e_edge[:, c : c + 256]).reshape(8, 16, 256)
            west_east = [
                jnp.broadcast_to(dw_kernel[dy, dx : dx + 1, c : c + 256], (8, 256)) for dx in (0, 2)
            ]
            total = total + moved * jnp.concatenate(west_east, axis=0)[None]
        edge_sum[:, :, c : c + 256] = total.astype(BF16)

    def conv_band(band):
        first = band * 8

        def row(r, carry):
            for c in range(0, HID, 256):
                parts = []
                e = [e_mid[first + r + dy, :, c : c + 256] for dy in range(3)]
                for dx in range(3):
                    acc = None
                    for dy in range(3):
                        w = dw16[3 * dy + dx, :, c : c + 256]
                        w = jnp.concatenate([w] * 4, axis=0)
                        term = e[dy] * w
                        acc = term if acc is None else acc + term
                    parts.append(acc)
                parts.append(edge_sum[band, :, c : c + 256])
                total = dot(shifts[r], jnp.concatenate(parts, axis=0))
                conv[pl.ds(r * 64, 64), c : c + 256] = gelu(total.astype(BF16))
            return carry

        lax.fori_loop(0, 8, row, 0, unroll=4)

    def pieces(x):
        return jnp.concatenate(
            [x[64 * b + 8 * a : 64 * b + 8 * a + 8] for a in range(8) for b in range(8)], axis=0
        )

    def send(phase, half):
        def one(i, carry):
            pltpu.make_async_remote_copy(
                src_ref=blocked.at[
                    half, phase * 8 + i // 4, pl.ds(pl.multiple_of(lax.rem(i, 4) * 16, 16), 16), :
                ],
                dst_ref=received.at[phase, lat, half, place],
                send_sem=send_sem.at[phase],
                recv_sem=recv_sem.at[phase],
                device_id=partner(i),
                device_id_type=MESH,
            ).start()
            return carry

        lax.fori_loop(0, 32, one, 0, unroll=True)

    def send_back(phase, q):
        for j in range(8):
            pltpu.make_async_remote_copy(
                src_ref=outgoing.at[phase, q, :, j],
                dst_ref=out.at[
                    :, phase * 8 + my_row, pl.ds(pl.multiple_of(my_col * 16, 16), 16), :
                ],
                send_sem=back_send.at[phase],
                recv_sem=back_recv.at[phase],
                device_id={"lat": q, "lon": 4 * j + far},
                device_id_type=MESH,
            ).start()

    def conv_and_block(phase):
        def half(i, carry):
            band = i * 4 + phase
            first = band * 8

            @pl.when((phase > 1) & (band < 7))
            def _():
                expand_rows(first + 1, 8)

            @pl.when(band == 7)
            def _():
                expand_rows(first + 1, 7)

            conv_band(band)
            x = tokens[pl.ds(first, 8)].reshape(512, D).astype(F32)
            x = pieces(x + dot(conv[0:512, :], w_project[...])).astype(BF16)
            mixed[0:512, :] = x
            result = attend(
                mixed.at[0:512], gain_block, average, qkv_block, bias_block, out_block, masks, select,
                ones_bd, qkv.at[0:512], att.at[0:512],
            )
            blocked[i, pl.ds(phase * 8, 8)] = (
                pieces(result + x.astype(F32)).astype(BF16).reshape(8, 64, D)
            )
            send(phase, i)
            return carry

        lax.fori_loop(0, 2, half, 0)

    def grid(phase):
        for q in range(4):
            x = received[phase, q].reshape(256, D)
            y = dot(perm[...], x).astype(BF16)
            for p in range(16):
                mixed[64 * p + 16 * q : 64 * p + 16 * q + 16] = y[16 * p : 16 * p + 16]
        result = attend(
            mixed, gain_grid, average, qkv_grid, bias_grid, out_grid, masks, select, ones_bd, qkv, att
        )
        done = (result + mixed[...].astype(F32)).astype(BF16)
        for q in range(4):
            x = jnp.concatenate(
                [done[64 * p + 16 * q : 64 * p + 16 * q + 16] for p in range(16)], axis=0
            )
            outgoing[phase, q] = dot(perm[...], x).astype(BF16).reshape(2, 8, 16, D)
            send_back(phase, q)

    def wait_all(ref, sem):
        pltpu.make_async_copy(ref, ref, sem).wait()

    def step(phase, carry):
        @pl.when(phase < PHASES)
        def _():
            conv_and_block(phase)

        @pl.when(phase > 0)
        def _():
            wait_all(received.at[phase - 1], recv_sem.at[phase - 1])
            grid(phase - 1)

        return carry

    lax.fori_loop(0, PHASES + 1, step, 0)

    def finish(phase, carry):
        wait_all(received.at[phase], send_sem.at[phase])
        wait_all(received.at[phase], back_send.at[phase])
        wait_all(received.at[phase], back_recv.at[phase])
        return carry

    lax.fori_loop(0, PHASES, finish, 0)


def copy_kernel(source, target, held, sem_in, sem_out):
    parts = [pl.ds(8 * i, 8) for i in range(8)]
    loads = [
        pltpu.make_async_copy(source.at[p], held.at[p], sem_in.at[i]) for i, p in enumerate(parts)
    ]
    stores = [
        pltpu.make_async_copy(held.at[p], target.at[p], sem_out.at[i]) for i, p in enumerate(parts)
    ]
    for load in loads:
        load.start()
    for load, store in zip(loads, stores):
        load.wait()
        store.start()
    for store in stores:
        store.wait()


def shards(
    tokens,
    gain_conv,
    w_expand,
    dw_kernel,
    w_project,
    gain_block,
    qkv_block,
    bias_block,
    out_block,
    gain_grid,
    qkv_grid,
    bias_grid,
    out_grid,
):
    operands = [
        tokens,
        gain_conv.reshape(1, D),
        w_expand,
        dw_kernel,
        w_project,
        gain_block.reshape(1, D),
        qkv_block,
        bias_block,
        out_block,
        gain_grid.reshape(1, D),
        qkv_grid,
        bias_grid,
        out_grid,
    ]
    result = pl.pallas_call(
        kernel,
        out_shape=jax.ShapeDtypeStruct((2, 32, COLS, D), BF16),
        in_specs=[pl.BlockSpec(memory_space=pl.ANY)] * len(operands),
        out_specs=pl.BlockSpec(memory_space=pl.ANY),
        scratch_shapes=[
            pltpu.VMEM((66, COLS, HID), BF16),
            pltpu.VMEM((192, HID), BF16),
            pltpu.VMEM((2, COLS, D), BF16),
            pltpu.VMEM((2, 96, D), BF16),
            pltpu.VMEM((2, 64, D), BF16),
            pltpu.VMEM((8, 16, HID), BF16),
            pltpu.VMEM((9, 16, HID), BF16),
            pltpu.VMEM((64, 512), F32),
            pltpu.VMEM((64, 512), F32),
            pltpu.VMEM((D, D), BF16),
            pltpu.VMEM((4, 16, 128), BF16),
            pltpu.VMEM((256, 256), BF16),
            pltpu.VMEM((256, 256), BF16),
            pltpu.VMEM((8, 64, 208), BF16),
            pltpu.VMEM((3, 128, 192), BF16),
            pltpu.VMEM((256, 256), BF16),
            pltpu.VMEM((512, HID), BF16),
            pltpu.VMEM((1024, D), BF16),
            pltpu.VMEM((1024, 3 * D), BF16),
            pltpu.VMEM((1024, D), BF16),
            pltpu.VMEM((2, 32, COLS, D), BF16),
            pltpu.VMEM((PHASES, 4, 2, 8, 16, D), BF16),
            pltpu.VMEM((PHASES, 4, 2, 8, 16, D), BF16),
            pltpu.SemaphoreType.DMA((8,)),
            pltpu.SemaphoreType.DMA((8,)),
            pltpu.SemaphoreType.DMA((PHASES,)),
            pltpu.SemaphoreType.DMA((PHASES,)),
            pltpu.SemaphoreType.DMA((PHASES,)),
            pltpu.SemaphoreType.DMA((PHASES,)),
            *[pltpu.VMEM(a.shape, a.dtype) for a in operands],
            pltpu.SemaphoreType.DMA((len(operands) + 3,)),
        ],
        compiler_params=pltpu.CompilerParams(
            collective_id=0, has_side_effects=True, vmem_limit_bytes=60 * 1024 * 1024
        ),
    )(*operands)
    result = result.reshape(ROWS, COLS, D)
    return pl.pallas_call(
        copy_kernel,
        out_shape=jax.ShapeDtypeStruct(result.shape, result.dtype),
        in_specs=[pl.BlockSpec(memory_space=pl.ANY)],
        out_specs=pl.BlockSpec(memory_space=pl.ANY),
        scratch_shapes=[
            pltpu.VMEM(result.shape, result.dtype),
            pltpu.SemaphoreType.DMA((8,)),
            pltpu.SemaphoreType.DMA((8,)),
        ],
    )(result)


def solution(mesh):
    placed = (P("lat", "lon", None), P(), P(), P(), P(), P(), P(), P(), P(), P(), P(), P(), P())
    return jax.shard_map(
        shards, mesh=mesh, in_specs=placed, out_specs=P("lat", "lon", None), check_vma=False
    )
```

```python
import functools

import jax
import jax.numpy as jnp
from jax import lax
from jax.experimental import pallas as pl
from jax.experimental.pallas import tpu as pltpu
from jax.sharding import PartitionSpec as P

MESH = pl.DeviceIdType.MESH
BF16 = jnp.bfloat16
F32 = jnp.float32
ROWS, COLS, D, HID, HEADS = 64, 64, 256, 1024, 8
PHASES = 4
EARLY = 5
STEPS = 15
LOG2E = 1.4426950408889634


def dot(a, b):
    return jnp.dot(a, b, preferred_element_type=F32)


def dot_nt(a, b):
    return lax.dot_general(a, b, (((1,), (1,)), ((), ())), preferred_element_type=F32)


def exp2(x):
    return jnp.exp2(x)


def gelu(x):
    half = x * BF16(0.5)
    inner = x * (BF16(0.7978845608) + BF16(0.035677408) * (x * x))
    return half + half * jnp.tanh(inner)


def norm(x, gain, average):
    xf = x.astype(F32)
    d = xf - jnp.mean(xf, axis=-1, keepdims=True)
    var = dot((d * d).astype(BF16), average)
    return (d * lax.rsqrt(var + 1e-05) * gain).astype(BF16)


def expand(x, gain, average, w_expand, store):
    n = norm(x, gain, average)
    for c in range(0, HID, 256):
        store(c, gelu(dot(n, w_expand[:, c : c + 256]).astype(BF16)))


def blocks(m, masks):
    return jnp.concatenate(
        [m[16 * i : 16 * i + 16] * masks[h] for i in range(4) for h in range(4)], axis=0
    )


def beside(steps, others):
    marks = list(steps_count(len(others)))
    for at, _ in enumerate(steps):
        while marks and marks[0] <= at:
            marks.pop(0)
            others.pop(0)()
    for other in others:
        other()


def steps_count(count):
    return (k * STEPS // count for k in range(count))


def attend(x_ref, gain, average, w_qkv, bias, w_out, masks, select, ones_bd, qkv, mixed):
    n = norm(x_ref[...], gain[...], average[...])
    scale = LOG2E / 32**0.5
    qkv[:, 0:256] = (dot(n, w_qkv[:, 0:256]) * scale).astype(BF16)
    qkv[:, 256:512] = dot(n, w_qkv[:, 256:512]).astype(BF16)
    qkv[:, 512:768] = dot(n, w_qkv[:, 512:768]).astype(BF16)
    groups = x_ref.shape[0] // 64
    scores, weights, sums, totals = {}, {}, {}, {}

    def rows(g):
        return pl.ds(64 * g, 64)

    def score(g):
        scores[g] = [
            dot_nt(
                qkv[rows(g), 128 * u : 128 * u + 128],
                blocks(qkv[rows(g), 256 + 128 * u : 384 + 128 * u], masks),
            )
            + bias[:, 256 * u : 256 * u + 256]
            for u in range(2)
        ]

    def soften(batch):
        pairs = [
            jnp.concatenate(
                [jnp.maximum(scores[g][u][:, 0:128], scores[g][u][:, 128:256]) for g in batch],
                axis=0,
            )
            for u in range(2)
        ]
        yield
        lane = lax.broadcasted_iota(jnp.int32, pairs[0].shape, 1)
        here = jnp.where(lane < 64, pairs[0], pairs[1])
        there = jnp.where(lane < 64, pairs[1], pairs[0])
        top = jnp.maximum(here, pltpu.roll(there, 64, 1))
        yield
        for shift in (8, 4, 2, 1):
            top = jnp.maximum(top, pltpu.roll(top, 128 - shift, 1))
            yield
        high = top.astype(BF16)
        low = (top - high.astype(F32)).astype(BF16)
        top = dot(jnp.concatenate([high, low], axis=1), select[...])
        yield
        for k, g in enumerate(batch):
            parts, weights[g] = [], []
            for u, s in enumerate(scores[g]):
                t = top[64 * k : 64 * k + 64, 128 * u : 128 * u + 128]
                a, b = exp2(s[:, 0:128] - t), exp2(s[:, 128:256] - t)
                parts.append((a + b).astype(BF16))
                weights[g].append(jnp.concatenate([a.astype(BF16), b.astype(BF16)], axis=1))
            sums[g] = jnp.concatenate(parts, axis=1)
            yield

    def combine(batch):
        total = dot(jnp.concatenate([sums[g] for g in batch], axis=0), ones_bd[...])
        for k, g in enumerate(batch):
            totals[g] = total[64 * k : 64 * k + 64]

    def value(g):
        out = jnp.concatenate(
            [
                dot(w, blocks(qkv[rows(g), 512 + 128 * u : 640 + 128 * u], masks))
                for u, w in enumerate(weights[g])
            ],
            axis=1,
        )
        mixed[rows(g), :] = (out / totals[g]).astype(BF16)

    early, late = range(groups // 2), range(groups // 2, groups)
    for g in early:
        score(g)
    beside(soften(early), [functools.partial(score, g) for g in late])
    combine(early)
    beside(soften(late), [functools.partial(value, g) for g in early])
    combine(late)
    for g in late:
        value(g)
    return dot(mixed[...], w_out[...])


def spread_bias(source, target):
    lane = lax.broadcasted_iota(jnp.int32, (64, 128), 1)
    for u in range(2):
        twice = []
        for h in range(4):
            x = source[4 * u + h] * LOG2E
            twice.append(jnp.concatenate([x, x], axis=1))
        for tile in range(2):
            acc = twice[0]
            for k in range(2):
                for h in range(4):
                    at, to = (2 * tile + k) * 16, k * 64 + h * 16
                    moved = pltpu.roll(twice[h], (to - at) % 128, 1)
                    acc = jnp.where((lane >> 4) == to // 16, moved, acc)
            target[:, 256 * u + 128 * tile : 256 * u + 128 * tile + 128] = acc


def pick(shape, hit):
    row = lax.broadcasted_iota(jnp.int32, shape, 0)
    col = lax.broadcasted_iota(jnp.int32, shape, 1)
    return jnp.where(hit(row, col), 1.0, 0.0).astype(BF16)


def kernel(
    tokens_hbm,
    gain_conv_hbm,
    w_expand_hbm,
    dw_kernel_hbm,
    w_project_hbm,
    gain_block_hbm,
    qkv_block_hbm,
    bias_in_block_hbm,
    out_block_hbm,
    gain_grid_hbm,
    qkv_grid_hbm,
    bias_in_grid_hbm,
    out_grid_hbm,
    out,
    e_mid,
    e_edge,
    halo_row,
    halo_col,
    edge,
    edge_sum,
    dw16,
    bias_block,
    bias_grid,
    average,
    masks,
    select,
    ones_bd,
    shifts,
    edge_shift,
    perm,
    conv,
    mixed,
    qkv,
    att,
    blocked,
    received,
    outgoing,
    halo_send,
    halo_recv,
    send_sem,
    recv_sem,
    back_send,
    back_recv,
    tokens,
    gain_conv,
    w_expand,
    dw_kernel,
    w_project,
    gain_block,
    qkv_block,
    bias_in_block,
    out_block,
    gain_grid,
    qkv_grid,
    bias_in_grid,
    out_grid,
    fetch_sem,
):
    lat = lax.axis_index("lat")
    lon = lax.axis_index("lon")
    lats = lax.axis_size("lat")
    lons = lax.axis_size("lon")
    kind = lax.rem(lon, 4)
    place = lon // 4
    far = 3 - kind
    mine = lat * 8 + place
    my_row, my_col = mine // 4, lax.rem(mine, 4)
    west = lax.rem(lon + lons - 1, lons)
    east = lax.rem(lon + 1, lons)

    def partner(i):
        return {"lat": i // 8, "lon": lax.rem(i, 8) * 4 + far}

    fetched = [
        pltpu.make_async_copy(src, dst, fetch_sem.at[i])
        for i, (src, dst) in enumerate(
            [
                (tokens_hbm, tokens),
                (w_expand_hbm, w_expand),
                (gain_conv_hbm, gain_conv),
                (dw_kernel_hbm, dw_kernel),
                (bias_in_block_hbm, bias_in_block),
                (bias_in_grid_hbm, bias_in_grid),
                (w_project_hbm, w_project),
                (gain_block_hbm, gain_block),
                (qkv_block_hbm, qkv_block),
                (out_block_hbm, out_block),
                (gain_grid_hbm, gain_grid),
                (qkv_grid_hbm, qkv_grid),
                (out_grid_hbm, out_grid),
            ]
        )
    ]
    for copy in fetched:
        copy.start()

    barrier = pltpu.get_barrier_semaphore()

    def greet(i, carry):
        pl.semaphore_signal(barrier, inc=1, device_id=partner(i), device_id_type=MESH)
        return carry

    lax.fori_loop(0, 32, greet, 0, unroll=True)
    for side in (west, east):
        pl.semaphore_signal(
            barrier, inc=1, device_id={"lat": lat, "lon": side}, device_id_type=MESH
        )

    @pl.when(lat > 0)
    def _():
        for side in (lon, west, east):
            pl.semaphore_signal(
                barrier, inc=1, device_id={"lat": lat - 1, "lon": side}, device_id_type=MESH
            )

    @pl.when(lat < lats - 1)
    def _():
        for side in (lon, west, east):
            pl.semaphore_signal(
                barrier, inc=1, device_id={"lat": lat + 1, "lon": side}, device_id_type=MESH
            )

    average[...] = jnp.full((D, D), 1.0 / D, BF16)
    for copy in fetched[:3]:
        copy.wait()
    for side in range(2):
        first = pick((16, 256), lambda r, c: c == r * 16 + 15 * side)
        for q in range(4):
            x = tokens[16 * q : 16 * q + 16, 48 * side : 48 * side + 16].reshape(256, D)
            edge[side, 16 * q : 16 * q + 16] = dot(first, x).astype(BF16)

    def expand_rows(first, count):
        def store(c, v):
            e_mid[pl.ds(first + 1, count), :, c : c + 256] = v.reshape(count, COLS, 256)

        x = tokens[pl.ds(first, count)].reshape(count * COLS, D)
        expand(x, gain_conv[...], average[...], w_expand, store)

    def expand_band(band, carry):
        expand_rows(band * 8, 8)
        return carry

    lax.fori_loop(0, EARLY, expand_band, 0)

    inner = jnp.minimum(lat, 1) + jnp.minimum(lats - 1 - lat, 1)
    pl.semaphore_wait(barrier, 34 + 3 * inner)

    def halo(slot, src, dst, to_lat, to_lon):
        return pltpu.make_async_remote_copy(
            src_ref=src,
            dst_ref=dst,
            send_sem=halo_send.at[slot],
            recv_sem=halo_recv.at[slot],
            device_id={"lat": to_lat, "lon": to_lon},
            device_id_type=MESH,
        )

    to_west = halo(0, edge.at[0], halo_col.at[1, pl.ds(16, 64)], lat, west)
    to_east = halo(1, edge.at[1], halo_col.at[0, pl.ds(16, 64)], lat, east)
    north = [
        halo(2, tokens.at[0], halo_row.at[1], lat - 1, lon),
        halo(3, edge.at[0, pl.ds(0, 16)], halo_col.at[1, pl.ds(80, 16)], lat - 1, west),
        halo(4, edge.at[1, pl.ds(0, 16)], halo_col.at[0, pl.ds(80, 16)], lat - 1, east),
    ]
    south = [
        halo(5, tokens.at[ROWS - 1], halo_row.at[0], lat + 1, lon),
        halo(6, edge.at[0, pl.ds(48, 16)], halo_col.at[1, pl.ds(0, 16)], lat + 1, west),
        halo(7, edge.at[1, pl.ds(48, 16)], halo_col.at[0, pl.ds(0, 16)], lat + 1, east),
    ]
    to_west.start()
    to_east.start()

    @pl.when(lat > 0)
    def _():
        for c in north:
            c.start()

    @pl.when(lat < lats - 1)
    def _():
        for c in south:
            c.start()

    @pl.when(lat == 0)
    def _():
        halo_row[0] = jnp.zeros((COLS, D), BF16)
        halo_col[0, 0:16] = jnp.zeros((16, D), BF16)
        halo_col[1, 0:16] = jnp.zeros((16, D), BF16)

    @pl.when(lat == lats - 1)
    def _():
        halo_row[1] = jnp.zeros((COLS, D), BF16)
        halo_col[0, 80:96] = jnp.zeros((16, D), BF16)
        halo_col[1, 80:96] = jnp.zeros((16, D), BF16)

    lax.fori_loop(EARLY, 8, expand_band, 0)
    for copy in fetched[3:]:
        copy.wait()
    for h in range(4):
        masks[h] = pick((16, 128), lambda r, c: (c >> 5) == h)
    select[...] = pick(
        (256, 256), lambda r, c: (r & 127) == (c >> 7) * 64 + (c & 48)
    )
    ones_bd[...] = pick((256, 256), lambda r, c: (r >> 7) * 64 + (r & 48) == (c >> 5) << 4)
    for r8 in range(8):
        shifts[r8] = pick(
            (64, 208),
            lambda r, c: ((c < 192) & ((c & 63) + 1 - (c >> 6) == r))
            | ((c == 192 + r8) & (r == 0))
            | ((c == 200 + r8) & (r == 63)),
        )
    for dy in range(3):
        edge_shift[dy] = pick(
            (128, 192),
            lambda r, c: c == ((r >> 3) & 1) * 96 + 15 + (r >> 4) * 8 + (r & 7) + dy,
        )
    perm[...] = pick((256, 256), lambda r, c: r == ((c & 15) << 4) + (c >> 4))
    for dy in range(3):
        for dx in range(3):
            dw16[3 * dy + dx] = jnp.broadcast_to(dw_kernel[dy, dx : dx + 1], (16, HID)).astype(BF16)

    spread_bias(bias_in_block, bias_block)
    spread_bias(bias_in_grid, bias_grid)

    to_west.wait()
    to_east.wait()

    @pl.when(lat > 0)
    def _():
        for c in north:
            c.wait_send()
        for c in south:
            c.wait_recv()

    @pl.when(lat < lats - 1)
    def _():
        for c in south:
            c.wait_send()
        for c in north:
            c.wait_recv()

    def store_rows(c, v):
        e_mid[0, :, c : c + 256] = v[0:64]
        e_mid[65, :, c : c + 256] = v[64:128]

    expand(halo_row[...].reshape(2 * COLS, D), gain_conv[...], average[...], w_expand, store_rows)

    def store_cols(c, v):
        e_edge[:, c : c + 256] = v

    expand(halo_col[...].reshape(192, D), gain_conv[...], average[...], w_expand, store_cols)
    for c in range(0, HID, 256):
        total = jnp.zeros((8, 16, 256), F32)
        for dy in range(3):
            moved = dot(edge_shift[dy], e_edge[:, c : c + 256]).reshape(8, 16, 256)
            west_east = [
                jnp.broadcast_to(dw_kernel[dy, dx : dx + 1, c : c + 256], (8, 256)) for dx in (0, 2)
            ]
            total = total + moved * jnp.concatenate(west_east, axis=0)[None]
        edge_sum[:, :, c : c + 256] = total.astype(BF16)

    def conv_band(band):
        first = band * 8

        def row(r, carry):
            for c in range(0, HID, 256):
                parts = []
                e = [e_mid[first + r + dy, :, c : c + 256] for dy in range(3)]
                for dx in range(3):
                    acc = None
                    for dy in range(3):
                        w = dw16[3 * dy + dx, :, c : c + 256]
                        w = jnp.concatenate([w] * 4, axis=0)
                        term = e[dy] * w
                        acc = term if acc is None else acc + term
                    parts.append(acc)
                parts.append(edge_sum[band, :, c : c + 256])
                total = dot(shifts[r], jnp.concatenate(parts, axis=0))
                conv[pl.ds(r * 64, 64), c : c + 256] = gelu(total.astype(BF16))
            return carry

        lax.fori_loop(0, 8, row, 0, unroll=4)

    def pieces(x):
        return jnp.concatenate(
            [x[64 * b + 8 * a : 64 * b + 8 * a + 8] for a in range(8) for b in range(8)], axis=0
        )

    def send(phase):
        def one(i, carry):
            pltpu.make_async_remote_copy(
                src_ref=blocked.at[
                    :, phase * 8 + i // 4, pl.ds(pl.multiple_of(lax.rem(i, 4) * 16, 16), 16), :
                ],
                dst_ref=received.at[phase, lat, :, place],
                send_sem=send_sem.at[phase],
                recv_sem=recv_sem.at[phase],
                device_id=partner(i),
                device_id_type=MESH,
            ).start()
            return carry

        lax.fori_loop(0, 32, one, 0, unroll=True)

    def send_back(phase):
        def one(i, carry):
            pltpu.make_async_remote_copy(
                src_ref=outgoing.at[phase, i // 8, :, lax.rem(i, 8)],
                dst_ref=out.at[
                    :, phase * 8 + my_row, pl.ds(pl.multiple_of(my_col * 16, 16), 16), :
                ],
                send_sem=back_send.at[phase],
                recv_sem=back_recv.at[phase],
                device_id=partner(i),
                device_id_type=MESH,
            ).start()
            return carry

        lax.fori_loop(0, 32, one, 0, unroll=True)

    def conv_and_block(phase):
        def half(i, carry):
            band = i * 4 + phase
            first = band * 8

            conv_band(band)
            x = tokens[pl.ds(first, 8)].reshape(512, D).astype(F32)
            rows = pl.ds(pl.multiple_of(i * 512, 512), 512)
            mixed[rows, :] = pieces(x + dot(conv[0:512, :], w_project[...])).astype(BF16)
            return carry

        lax.fori_loop(0, 2, half, 0)
        result = attend(
            mixed, gain_block, average, qkv_block, bias_block, out_block, masks, select, ones_bd,
            qkv, att,
        )
        result = result + mixed[...].astype(F32)
        for i in range(2):
            blocked[i, pl.ds(phase * 8, 8)] = (
                pieces(result[512 * i : 512 * i + 512]).astype(BF16).reshape(8, 64, D)
            )
        send(phase)

    def grid(phase):
        for q in range(4):
            x = received[phase, q].reshape(256, D)
            y = dot(perm[...], x).astype(BF16)
            for p in range(16):
                mixed[64 * p + 16 * q : 64 * p + 16 * q + 16] = y[16 * p : 16 * p + 16]
        result = attend(
            mixed, gain_grid, average, qkv_grid, bias_grid, out_grid, masks, select, ones_bd, qkv, att
        )
        done = (result + mixed[...].astype(F32)).astype(BF16)
        for q in range(4):
            x = jnp.concatenate(
                [done[64 * p + 16 * q : 64 * p + 16 * q + 16] for p in range(16)], axis=0
            )
            outgoing[phase, q] = dot(perm[...], x).astype(BF16).reshape(2, 8, 16, D)

    def wait_all(ref, sem):
        pltpu.make_async_copy(ref, ref, sem).wait()

    def step(phase, carry):
        @pl.when(phase < PHASES)
        def _():
            conv_and_block(phase)

        @pl.when(phase > 0)
        def _():
            wait_all(received.at[phase - 1], recv_sem.at[phase - 1])
            grid(phase - 1)
            send_back(phase - 1)

        return carry

    lax.fori_loop(0, PHASES + 1, step, 0)

    def finish(phase, carry):
        wait_all(received.at[phase], send_sem.at[phase])
        wait_all(received.at[phase], back_send.at[phase])
        wait_all(received.at[phase], back_recv.at[phase])
        return carry

    lax.fori_loop(0, PHASES, finish, 0)


def copy_kernel(source, target, held, sem_in, sem_out):
    parts = [pl.ds(8 * i, 8) for i in range(8)]
    loads = [
        pltpu.make_async_copy(source.at[p], held.at[p], sem_in.at[i]) for i, p in enumerate(parts)
    ]
    stores = [
        pltpu.make_async_copy(held.at[p], target.at[p], sem_out.at[i]) for i, p in enumerate(parts)
    ]
    for load in loads:
        load.start()
    for load, store in zip(loads, stores):
        load.wait()
        store.start()
    for store in stores:
        store.wait()


def shards(
    tokens,
    gain_conv,
    w_expand,
    dw_kernel,
    w_project,
    gain_block,
    qkv_block,
    bias_block,
    out_block,
    gain_grid,
    qkv_grid,
    bias_grid,
    out_grid,
):
    operands = [
        tokens,
        gain_conv.reshape(1, D),
        w_expand,
        dw_kernel,
        w_project,
        gain_block.reshape(1, D),
        qkv_block,
        bias_block,
        out_block,
        gain_grid.reshape(1, D),
        qkv_grid,
        bias_grid,
        out_grid,
    ]
    result = pl.pallas_call(
        kernel,
        out_shape=jax.ShapeDtypeStruct((2, 32, COLS, D), BF16),
        in_specs=[pl.BlockSpec(memory_space=pl.ANY)] * len(operands),
        out_specs=pl.BlockSpec(memory_space=pl.ANY),
        scratch_shapes=[
            pltpu.VMEM((66, COLS, HID), BF16),
            pltpu.VMEM((192, HID), BF16),
            pltpu.VMEM((2, COLS, D), BF16),
            pltpu.VMEM((2, 96, D), BF16),
            pltpu.VMEM((2, 64, D), BF16),
            pltpu.VMEM((8, 16, HID), BF16),
            pltpu.VMEM((9, 16, HID), BF16),
            pltpu.VMEM((64, 512), F32),
            pltpu.VMEM((64, 512), F32),
            pltpu.VMEM((D, D), BF16),
            pltpu.VMEM((4, 16, 128), BF16),
            pltpu.VMEM((256, 256), BF16),
            pltpu.VMEM((256, 256), BF16),
            pltpu.VMEM((8, 64, 208), BF16),
            pltpu.VMEM((3, 128, 192), BF16),
            pltpu.VMEM((256, 256), BF16),
            pltpu.VMEM((512, HID), BF16),
            pltpu.VMEM((1024, D), BF16),
            pltpu.VMEM((1024, 3 * D), BF16),
            pltpu.VMEM((1024, D), BF16),
            pltpu.VMEM((2, 32, COLS, D), BF16),
            pltpu.VMEM((PHASES, 4, 2, 8, 16, D), BF16),
            pltpu.VMEM((PHASES, 4, 2, 8, 16, D), BF16),
            pltpu.SemaphoreType.DMA((8,)),
            pltpu.SemaphoreType.DMA((8,)),
            pltpu.SemaphoreType.DMA((PHASES,)),
            pltpu.SemaphoreType.DMA((PHASES,)),
            pltpu.SemaphoreType.DMA((PHASES,)),
            pltpu.SemaphoreType.DMA((PHASES,)),
            *[pltpu.VMEM(a.shape, a.dtype) for a in operands],
            pltpu.SemaphoreType.DMA((len(operands),)),
        ],
        compiler_params=pltpu.CompilerParams(
            collective_id=0, has_side_effects=True, vmem_limit_bytes=60 * 1024 * 1024
        ),
    )(*operands)
    result = result.reshape(ROWS, COLS, D)
    return pl.pallas_call(
        copy_kernel,
        out_shape=jax.ShapeDtypeStruct(result.shape, result.dtype),
        in_specs=[pl.BlockSpec(memory_space=pl.ANY)],
        out_specs=pl.BlockSpec(memory_space=pl.ANY),
        scratch_shapes=[
            pltpu.VMEM(result.shape, result.dtype),
            pltpu.SemaphoreType.DMA((8,)),
            pltpu.SemaphoreType.DMA((8,)),
        ],
    )(result)


def solution(mesh):
    placed = (P("lat", "lon", None), P(), P(), P(), P(), P(), P(), P(), P(), P(), P(), P(), P())
    return jax.shard_map(
        shards, mesh=mesh, in_specs=placed, out_specs=P("lat", "lon", None), check_vma=False
    )
```

```python
import functools

import jax
import jax.numpy as jnp
from jax import lax
from jax.experimental import pallas as pl
from jax.experimental.pallas import tpu as pltpu
from jax.sharding import PartitionSpec as P

MESH = pl.DeviceIdType.MESH
BF16 = jnp.bfloat16
F32 = jnp.float32
ROWS, COLS, D, HID, HEADS = 64, 64, 256, 1024, 8
PHASES = 4
STEPS = 15
LOG2E = 1.4426950408889634


def dot(a, b):
    return jnp.dot(a, b, preferred_element_type=F32)


def dot_nt(a, b):
    return lax.dot_general(a, b, (((1,), (1,)), ((), ())), preferred_element_type=F32)


def exp2(x):
    return jnp.exp2(x)


def gelu(x):
    half = x * BF16(0.5)
    inner = x * (BF16(0.7978845608) + BF16(0.035677408) * (x * x))
    return half + half * jnp.tanh(inner)


def norm(x, gain, average):
    xf = x.astype(F32)
    d = xf - jnp.mean(xf, axis=-1, keepdims=True)
    var = dot((d * d).astype(BF16), average)
    return (d * lax.rsqrt(var + 1e-05) * gain).astype(BF16)


def expand(x, gain, average, w_expand, store):
    n = norm(x, gain, average)
    for c in range(0, HID, 256):
        store(c, gelu(dot(n, w_expand[:, c : c + 256]).astype(BF16)))


def blocks(m, masks):
    return jnp.concatenate(
        [m[16 * i : 16 * i + 16] * masks[h] for i in range(4) for h in range(4)], axis=0
    )


def beside(steps, others):
    marks = list(steps_count(len(others)))
    for at, _ in enumerate(steps):
        while marks and marks[0] <= at:
            marks.pop(0)
            others.pop(0)()
    for other in others:
        other()


def steps_count(count):
    return (k * STEPS // count for k in range(count))


def attend(x_ref, gain, average, w_qkv, bias, w_out, masks, select, ones_bd, qkv, mixed):
    n = norm(x_ref[...], gain[...], average[...])
    scale = LOG2E / 32**0.5
    qkv[:, 0:256] = (dot(n, w_qkv[:, 0:256]) * scale).astype(BF16)
    qkv[:, 256:512] = dot(n, w_qkv[:, 256:512]).astype(BF16)
    qkv[:, 512:768] = dot(n, w_qkv[:, 512:768]).astype(BF16)
    groups = x_ref.shape[0] // 64
    scores, weights, sums, totals = {}, {}, {}, {}

    def rows(g):
        return pl.ds(64 * g, 64)

    def score(g):
        scores[g] = [
            dot_nt(
                qkv[rows(g), 128 * u : 128 * u + 128],
                blocks(qkv[rows(g), 256 + 128 * u : 384 + 128 * u], masks),
            )
            + bias[:, 256 * u : 256 * u + 256]
            for u in range(2)
        ]

    def soften(batch):
        pairs = [
            jnp.concatenate(
                [jnp.maximum(scores[g][u][:, 0:128], scores[g][u][:, 128:256]) for g in batch],
                axis=0,
            )
            for u in range(2)
        ]
        yield
        lane = lax.broadcasted_iota(jnp.int32, pairs[0].shape, 1)
        here = jnp.where(lane < 64, pairs[0], pairs[1])
        there = jnp.where(lane < 64, pairs[1], pairs[0])
        top = jnp.maximum(here, pltpu.roll(there, 64, 1))
        yield
        for shift in (8, 4, 2, 1):
            top = jnp.maximum(top, pltpu.roll(top, 128 - shift, 1))
            yield
        high = top.astype(BF16)
        low = (top - high.astype(F32)).astype(BF16)
        top = dot(jnp.concatenate([high, low], axis=1), select[...])
        yield
        for k, g in enumerate(batch):
            parts, weights[g] = [], []
            for u, s in enumerate(scores[g]):
                t = top[64 * k : 64 * k + 64, 128 * u : 128 * u + 128]
                a, b = exp2(s[:, 0:128] - t), exp2(s[:, 128:256] - t)
                parts.append((a + b).astype(BF16))
                weights[g].append(jnp.concatenate([a.astype(BF16), b.astype(BF16)], axis=1))
            sums[g] = jnp.concatenate(parts, axis=1)
            yield

    def combine(batch):
        total = dot(jnp.concatenate([sums[g] for g in batch], axis=0), ones_bd[...])
        for k, g in enumerate(batch):
            totals[g] = total[64 * k : 64 * k + 64]

    def value(g):
        out = jnp.concatenate(
            [
                dot(w, blocks(qkv[rows(g), 512 + 128 * u : 640 + 128 * u], masks))
                for u, w in enumerate(weights[g])
            ],
            axis=1,
        )
        mixed[rows(g), :] = (out / totals[g]).astype(BF16)

    early, late = range(groups // 2), range(groups // 2, groups)
    for g in early:
        score(g)
    beside(soften(early), [functools.partial(score, g) for g in late])
    combine(early)
    beside(soften(late), [functools.partial(value, g) for g in early])
    combine(late)
    for g in late:
        value(g)
    return dot(mixed[...], w_out[...])


def spread_bias(source, target):
    lane = lax.broadcasted_iota(jnp.int32, (64, 128), 1)
    for u in range(2):
        twice = []
        for h in range(4):
            x = source[4 * u + h] * LOG2E
            twice.append(jnp.concatenate([x, x], axis=1))
        for tile in range(2):
            acc = twice[0]
            for k in range(2):
                for h in range(4):
                    at, to = (2 * tile + k) * 16, k * 64 + h * 16
                    moved = pltpu.roll(twice[h], (to - at) % 128, 1)
                    acc = jnp.where((lane >> 4) == to // 16, moved, acc)
            target[:, 256 * u + 128 * tile : 256 * u + 128 * tile + 128] = acc


def pick(shape, hit):
    row = lax.broadcasted_iota(jnp.int32, shape, 0)
    col = lax.broadcasted_iota(jnp.int32, shape, 1)
    return jnp.where(hit(row, col), 1.0, 0.0).astype(BF16)


def kernel(
    tokens_hbm,
    gain_conv_hbm,
    w_expand_hbm,
    dw_kernel_hbm,
    w_project_hbm,
    gain_block_hbm,
    qkv_block_hbm,
    bias_in_block_hbm,
    out_block_hbm,
    gain_grid_hbm,
    qkv_grid_hbm,
    bias_in_grid_hbm,
    out_grid_hbm,
    out,
    e_mid,
    e_edge,
    halo_row,
    halo_col,
    edge,
    edge_sum,
    dw16,
    bias_block,
    bias_grid,
    average,
    masks,
    select,
    ones_bd,
    shifts,
    edge_shift,
    perm,
    conv,
    mixed,
    qkv,
    att,
    blocked,
    received,
    outgoing,
    halo_send,
    halo_recv,
    send_sem,
    recv_sem,
    back_send,
    back_recv,
    tokens,
    gain_conv,
    w_expand,
    dw_kernel,
    w_project,
    gain_block,
    qkv_block,
    bias_in_block,
    out_block,
    gain_grid,
    qkv_grid,
    bias_in_grid,
    out_grid,
    fetch_sem,
):
    lat = lax.axis_index("lat")
    lon = lax.axis_index("lon")
    lats = lax.axis_size("lat")
    lons = lax.axis_size("lon")
    kind = lax.rem(lon, 4)
    place = lon // 4
    far = 3 - kind
    mine = lat * 8 + place
    my_row, my_col = mine // 4, lax.rem(mine, 4)
    west = lax.rem(lon + lons - 1, lons)
    east = lax.rem(lon + 1, lons)

    def partner(i):
        return {"lat": i // 8, "lon": lax.rem(i, 8) * 4 + far}

    fetched = [
        pltpu.make_async_copy(src, dst, fetch_sem.at[i])
        for i, (src, dst) in enumerate(
            [
                (w_expand_hbm, w_expand),
                (gain_conv_hbm, gain_conv),
                *[
                    (tokens_hbm.at[pl.ds(16 * k, 16)], tokens.at[pl.ds(16 * k, 16)])
                    for k in range(4)
                ],
                (dw_kernel_hbm, dw_kernel),
                (bias_in_block_hbm, bias_in_block),
                (bias_in_grid_hbm, bias_in_grid),
                (w_project_hbm, w_project),
                (gain_block_hbm, gain_block),
                (qkv_block_hbm, qkv_block),
                (out_block_hbm, out_block),
                (gain_grid_hbm, gain_grid),
                (qkv_grid_hbm, qkv_grid),
                (out_grid_hbm, out_grid),
            ]
        )
    ]
    for copy in fetched:
        copy.start()

    barrier = pltpu.get_barrier_semaphore()

    def greet(i, carry):
        pl.semaphore_signal(barrier, inc=1, device_id=partner(i), device_id_type=MESH)
        return carry

    lax.fori_loop(0, 32, greet, 0, unroll=True)
    for side in (west, east):
        pl.semaphore_signal(
            barrier, inc=1, device_id={"lat": lat, "lon": side}, device_id_type=MESH
        )

    @pl.when(lat > 0)
    def _():
        for side in (lon, west, east):
            pl.semaphore_signal(
                barrier, inc=1, device_id={"lat": lat - 1, "lon": side}, device_id_type=MESH
            )

    @pl.when(lat < lats - 1)
    def _():
        for side in (lon, west, east):
            pl.semaphore_signal(
                barrier, inc=1, device_id={"lat": lat + 1, "lon": side}, device_id_type=MESH
            )

    average[...] = jnp.full((D, D), 1.0 / D, BF16)
    def expand_rows(first, count):
        def store(c, v):
            e_mid[pl.ds(first + 1, count), :, c : c + 256] = v.reshape(count, COLS, 256)

        x = tokens[pl.ds(first, count)].reshape(count * COLS, D)
        expand(x, gain_conv[...], average[...], w_expand, store)

    for copy in fetched[:3]:
        copy.wait()
    expand_rows(0, 8)
    for copy in fetched[3:6]:
        copy.wait()
    for side in range(2):
        first = pick((16, 256), lambda r, c: c == r * 16 + 15 * side)
        for q in range(4):
            x = tokens[16 * q : 16 * q + 16, 48 * side : 48 * side + 16].reshape(256, D)
            edge[side, 16 * q : 16 * q + 16] = dot(first, x).astype(BF16)

    inner = jnp.minimum(lat, 1) + jnp.minimum(lats - 1 - lat, 1)
    pl.semaphore_wait(barrier, 34 + 3 * inner)

    def halo(slot, src, dst, to_lat, to_lon):
        return pltpu.make_async_remote_copy(
            src_ref=src,
            dst_ref=dst,
            send_sem=halo_send.at[slot],
            recv_sem=halo_recv.at[slot],
            device_id={"lat": to_lat, "lon": to_lon},
            device_id_type=MESH,
        )

    to_west = halo(0, edge.at[0], halo_col.at[1, pl.ds(16, 64)], lat, west)
    to_east = halo(1, edge.at[1], halo_col.at[0, pl.ds(16, 64)], lat, east)
    north = [
        halo(2, tokens.at[0], halo_row.at[1], lat - 1, lon),
        halo(3, edge.at[0, pl.ds(0, 16)], halo_col.at[1, pl.ds(80, 16)], lat - 1, west),
        halo(4, edge.at[1, pl.ds(0, 16)], halo_col.at[0, pl.ds(80, 16)], lat - 1, east),
    ]
    south = [
        halo(5, tokens.at[ROWS - 1], halo_row.at[0], lat + 1, lon),
        halo(6, edge.at[0, pl.ds(48, 16)], halo_col.at[1, pl.ds(0, 16)], lat + 1, west),
        halo(7, edge.at[1, pl.ds(48, 16)], halo_col.at[0, pl.ds(0, 16)], lat + 1, east),
    ]
    to_west.start()
    to_east.start()

    @pl.when(lat > 0)
    def _():
        for c in north:
            c.start()

    @pl.when(lat < lats - 1)
    def _():
        for c in south:
            c.start()

    @pl.when(lat == 0)
    def _():
        halo_row[0] = jnp.zeros((COLS, D), BF16)
        halo_col[0, 0:16] = jnp.zeros((16, D), BF16)
        halo_col[1, 0:16] = jnp.zeros((16, D), BF16)

    @pl.when(lat == lats - 1)
    def _():
        halo_row[1] = jnp.zeros((COLS, D), BF16)
        halo_col[0, 80:96] = jnp.zeros((16, D), BF16)
        halo_col[1, 80:96] = jnp.zeros((16, D), BF16)

    expand_rows(8, 9)
    expand_rows(31, 9)
    expand_rows(40, 9)
    for copy in fetched[6:]:
        copy.wait()
    for h in range(4):
        masks[h] = pick((16, 128), lambda r, c: (c >> 5) == h)
    select[...] = pick(
        (256, 256), lambda r, c: (r & 127) == (c >> 7) * 64 + (c & 48)
    )
    ones_bd[...] = pick((256, 256), lambda r, c: (r >> 7) * 64 + (r & 48) == (c >> 5) << 4)
    for r8 in range(8):
        shifts[r8] = pick(
            (64, 208),
            lambda r, c: ((c < 192) & ((c & 63) + 1 - (c >> 6) == r))
            | ((c == 192 + r8) & (r == 0))
            | ((c == 200 + r8) & (r == 63)),
        )
    for dy in range(3):
        edge_shift[dy] = pick(
            (128, 192),
            lambda r, c: c == ((r >> 3) & 1) * 96 + 15 + (r >> 4) * 8 + (r & 7) + dy,
        )
    perm[...] = pick((256, 256), lambda r, c: r == ((c & 15) << 4) + (c >> 4))
    for dy in range(3):
        for dx in range(3):
            dw16[3 * dy + dx] = jnp.broadcast_to(dw_kernel[dy, dx : dx + 1], (16, HID)).astype(BF16)

    spread_bias(bias_in_block, bias_block)
    spread_bias(bias_in_grid, bias_grid)

    to_west.wait()
    to_east.wait()

    @pl.when(lat > 0)
    def _():
        for c in north:
            c.wait_send()
        for c in south:
            c.wait_recv()

    @pl.when(lat < lats - 1)
    def _():
        for c in south:
            c.wait_send()
        for c in north:
            c.wait_recv()

    def store_rows(c, v):
        e_mid[0, :, c : c + 256] = v[0:64]
        e_mid[65, :, c : c + 256] = v[64:128]

    expand(halo_row[...].reshape(2 * COLS, D), gain_conv[...], average[...], w_expand, store_rows)

    def store_cols(c, v):
        e_edge[:, c : c + 256] = v

    expand(halo_col[...].reshape(192, D), gain_conv[...], average[...], w_expand, store_cols)
    for c in range(0, HID, 256):
        total = jnp.zeros((8, 16, 256), F32)
        for dy in range(3):
            moved = dot(edge_shift[dy], e_edge[:, c : c + 256]).reshape(8, 16, 256)
            west_east = [
                jnp.broadcast_to(dw_kernel[dy, dx : dx + 1, c : c + 256], (8, 256)) for dx in (0, 2)
            ]
            total = total + moved * jnp.concatenate(west_east, axis=0)[None]
        edge_sum[:, :, c : c + 256] = total.astype(BF16)

    def conv_band(band):
        first = band * 8

        def row(r, carry):
            for c in range(0, HID, 256):
                parts = []
                e = [e_mid[first + r + dy, :, c : c + 256] for dy in range(3)]
                for dx in range(3):
                    acc = None
                    for dy in range(3):
                        w = dw16[3 * dy + dx, :, c : c + 256]
                        w = jnp.concatenate([w] * 4, axis=0)
                        term = e[dy] * w
                        acc = term if acc is None else acc + term
                    parts.append(acc)
                parts.append(edge_sum[band, :, c : c + 256])
                total = dot(shifts[r], jnp.concatenate(parts, axis=0))
                conv[pl.ds(r * 64, 64), c : c + 256] = gelu(total.astype(BF16))
            return carry

        lax.fori_loop(0, 8, row, 0, unroll=4)

    def pieces(x):
        return jnp.concatenate(
            [x[64 * b + 8 * a : 64 * b + 8 * a + 8] for a in range(8) for b in range(8)], axis=0
        )

    def send(phase):
        def one(i, carry):
            pltpu.make_async_remote_copy(
                src_ref=blocked.at[
                    :, phase * 8 + i // 4, pl.ds(pl.multiple_of(lax.rem(i, 4) * 16, 16), 16), :
                ],
                dst_ref=received.at[phase, lat, :, place],
                send_sem=send_sem.at[phase],
                recv_sem=recv_sem.at[phase],
                device_id=partner(i),
                device_id_type=MESH,
            ).start()
            return carry

        lax.fori_loop(0, 32, one, 0, unroll=True)

    def send_back(phase, q):
        for j in range(8):
            pltpu.make_async_remote_copy(
                src_ref=outgoing.at[phase, q, :, j],
                dst_ref=out.at[
                    :, phase * 8 + my_row, pl.ds(pl.multiple_of(my_col * 16, 16), 16), :
                ],
                send_sem=back_send.at[phase],
                recv_sem=back_recv.at[phase],
                device_id={"lat": q, "lon": 4 * j + far},
                device_id_type=MESH,
            ).start()

    def conv_and_block(phase):
        def half(i, carry):
            band = i * 4 + phase
            first = band * 8

            @pl.when((phase > 1) & (band < 7))
            def _():
                expand_rows(first + 1, 8)

            @pl.when(band == 7)
            def _():
                expand_rows(first + 1, 7)

            conv_band(band)
            x = tokens[pl.ds(first, 8)].reshape(512, D).astype(F32)
            rows = pl.ds(pl.multiple_of(i * 512, 512), 512)
            mixed[rows, :] = pieces(x + dot(conv[0:512, :], w_project[...])).astype(BF16)
            return carry

        lax.fori_loop(0, 2, half, 0)
        result = attend(
            mixed, gain_block, average, qkv_block, bias_block, out_block, masks, select, ones_bd,
            qkv, att,
        )
        result = result + mixed[...].astype(F32)
        for i in range(2):
            blocked[i, pl.ds(phase * 8, 8)] = (
                pieces(result[512 * i : 512 * i + 512]).astype(BF16).reshape(8, 64, D)
            )
        send(phase)

    def grid(phase):
        for q in range(4):
            x = received[phase, q].reshape(256, D)
            y = dot(perm[...], x).astype(BF16)
            for p in range(16):
                mixed[64 * p + 16 * q : 64 * p + 16 * q + 16] = y[16 * p : 16 * p + 16]
        result = attend(
            mixed, gain_grid, average, qkv_grid, bias_grid, out_grid, masks, select, ones_bd, qkv, att
        )
        done = (result + mixed[...].astype(F32)).astype(BF16)
        for q in range(4):
            x = jnp.concatenate(
                [done[64 * p + 16 * q : 64 * p + 16 * q + 16] for p in range(16)], axis=0
            )
            outgoing[phase, q] = dot(perm[...], x).astype(BF16).reshape(2, 8, 16, D)
            send_back(phase, q)

    def wait_all(ref, sem):
        pltpu.make_async_copy(ref, ref, sem).wait()

    def step(phase, carry):
        @pl.when(phase < PHASES)
        def _():
            conv_and_block(phase)

        @pl.when(phase > 0)
        def _():
            wait_all(received.at[phase - 1], recv_sem.at[phase - 1])
            grid(phase - 1)

        return carry

    lax.fori_loop(0, PHASES + 1, step, 0)

    def finish(phase, carry):
        wait_all(received.at[phase], send_sem.at[phase])
        wait_all(received.at[phase], back_send.at[phase])
        wait_all(received.at[phase], back_recv.at[phase])
        return carry

    lax.fori_loop(0, PHASES, finish, 0)


def copy_kernel(source, target, held, sem_in, sem_out):
    parts = [pl.ds(8 * i, 8) for i in range(8)]
    loads = [
        pltpu.make_async_copy(source.at[p], held.at[p], sem_in.at[i]) for i, p in enumerate(parts)
    ]
    stores = [
        pltpu.make_async_copy(held.at[p], target.at[p], sem_out.at[i]) for i, p in enumerate(parts)
    ]
    for load in loads:
        load.start()
    for load, store in zip(loads, stores):
        load.wait()
        store.start()
    for store in stores:
        store.wait()


def shards(
    tokens,
    gain_conv,
    w_expand,
    dw_kernel,
    w_project,
    gain_block,
    qkv_block,
    bias_block,
    out_block,
    gain_grid,
    qkv_grid,
    bias_grid,
    out_grid,
):
    operands = [
        tokens,
        gain_conv.reshape(1, D),
        w_expand,
        dw_kernel,
        w_project,
        gain_block.reshape(1, D),
        qkv_block,
        bias_block,
        out_block,
        gain_grid.reshape(1, D),
        qkv_grid,
        bias_grid,
        out_grid,
    ]
    result = pl.pallas_call(
        kernel,
        out_shape=jax.ShapeDtypeStruct((2, 32, COLS, D), BF16),
        in_specs=[pl.BlockSpec(memory_space=pl.ANY)] * len(operands),
        out_specs=pl.BlockSpec(memory_space=pl.ANY),
        scratch_shapes=[
            pltpu.VMEM((66, COLS, HID), BF16),
            pltpu.VMEM((192, HID), BF16),
            pltpu.VMEM((2, COLS, D), BF16),
            pltpu.VMEM((2, 96, D), BF16),
            pltpu.VMEM((2, 64, D), BF16),
            pltpu.VMEM((8, 16, HID), BF16),
            pltpu.VMEM((9, 16, HID), BF16),
            pltpu.VMEM((64, 512), F32),
            pltpu.VMEM((64, 512), F32),
            pltpu.VMEM((D, D), BF16),
            pltpu.VMEM((4, 16, 128), BF16),
            pltpu.VMEM((256, 256), BF16),
            pltpu.VMEM((256, 256), BF16),
            pltpu.VMEM((8, 64, 208), BF16),
            pltpu.VMEM((3, 128, 192), BF16),
            pltpu.VMEM((256, 256), BF16),
            pltpu.VMEM((512, HID), BF16),
            pltpu.VMEM((1024, D), BF16),
            pltpu.VMEM((1024, 3 * D), BF16),
            pltpu.VMEM((1024, D), BF16),
            pltpu.VMEM((2, 32, COLS, D), BF16),
            pltpu.VMEM((PHASES, 4, 2, 8, 16, D), BF16),
            pltpu.VMEM((PHASES, 4, 2, 8, 16, D), BF16),
            pltpu.SemaphoreType.DMA((8,)),
            pltpu.SemaphoreType.DMA((8,)),
            pltpu.SemaphoreType.DMA((PHASES,)),
            pltpu.SemaphoreType.DMA((PHASES,)),
            pltpu.SemaphoreType.DMA((PHASES,)),
            pltpu.SemaphoreType.DMA((PHASES,)),
            *[pltpu.VMEM(a.shape, a.dtype) for a in operands],
            pltpu.SemaphoreType.DMA((len(operands) + 3,)),
        ],
        compiler_params=pltpu.CompilerParams(
            collective_id=0, has_side_effects=True, vmem_limit_bytes=60 * 1024 * 1024
        ),
    )(*operands)
    result = result.reshape(ROWS, COLS, D)
    return pl.pallas_call(
        copy_kernel,
        out_shape=jax.ShapeDtypeStruct(result.shape, result.dtype),
        in_specs=[pl.BlockSpec(memory_space=pl.ANY)],
        out_specs=pl.BlockSpec(memory_space=pl.ANY),
        scratch_shapes=[
            pltpu.VMEM(result.shape, result.dtype),
            pltpu.SemaphoreType.DMA((8,)),
            pltpu.SemaphoreType.DMA((8,)),
        ],
    )(result)


def solution(mesh):
    placed = (P("lat", "lon", None), P(), P(), P(), P(), P(), P(), P(), P(), P(), P(), P(), P())
    return jax.shard_map(
        shards, mesh=mesh, in_specs=placed, out_specs=P("lat", "lon", None), check_vma=False
    )
```
